32 devices in a mesh: parts: 2 (over x), gx: 16 (over z, y, core).
Axes of the slice: x: 2, y: 2, z: 4, core: 2. Of those that a mesh axis runs over, the one named last changes fastest.
Arguments:
- salt: float32 [16, 128, 256], P('parts', 'gx'), parts along dimension 0, may hold values from 0 to 1
- recharge: int32 [128, 512], P('gx', 'parts'), parts along dimension 1, may hold values 0 or 1
- conductivity: float32 [16, 64, 32], P('parts', 'gx'), parts along dimension 0, may hold values from 0.1 to 10
- codes: int32 [64, 64], P('gx', 'parts'), parts along dimension 1, may hold values from 0 to 2
Outputs:
- tendency: float32 [16, 128, 256], P('parts', 'gx'), parts along dimension 0
- head: float32 [16, 64, 32], P('parts', 'gx'), parts along dimension 0
The draws below stay inside these ranges and needn't reach their ends.
There are 2 independent parts, one for each index of `parts`. The reference program is written for one: setup_inputs(seed, part) draws one part's arguments, and reference() takes and returns one part's arrays. A program takes and returns all parts, laid end to end along the dimension named above; each array names one. Nothing has to cross between parts.
Inputs may be any that keep to these rules, and one draw needn't show every extreme that they name: `codes`: 0 marks inland cells without a boundary, 1 sea cells, 2 river cells.
All inputs are finite; a program needn't handle non-finite values. Where the reference program divides by a largest or mean magnitude, that divisor is 1e-20 or more. No bound on the sum of `recharge` on one device may be relied on, other than what follows from the above.
Results may differ from the reference program's by a relative error of at most 0.0003.
Values sent between devices are 32-bit elements; how exact they have to be, the bound alone decides.
No kernel may reach another device: no remote copies, remote signals or barrier semaphores. Data moves between devices by JAX's collectives and lax.ppermute only.
A program may use at most 128 MiB of HBM per device.

```python
import math
import jax
import jax.numpy as jnp
from jax import lax

LAYERS = 8
CYCLES = 2
SMOOTH = 2
COARSE_SWEEPS = 6
FINE_X = 128
FINE_Y = 256
COARSE_X = 32
COARSE_Y = 64


def with_ends(values, stream_key, least, high):
    dims = values.shape
    place = [jax.random.randint(jax.random.fold_in(stream_key, axis), (), 0, dims[axis]) for axis in range(len(dims))]
    values = values.at[tuple(place)].set(least)
    longest = dims.index(max(dims))
    place[longest] = (place[longest] + 1) % dims[longest]
    return values.at[tuple(place)].set(high)


def steps_of(stream_key, extent, pieces, low, high):
    loudness = 1.0
    for axis_at, blocks in pieces:
        heights = jax.random.uniform(jax.random.fold_in(jax.random.fold_in(stream_key, 6), axis_at), (blocks,), jnp.float32, low / len(pieces), high / len(pieces))
        loudness = loudness * jnp.repeat(jnp.exp(heights), extent[axis_at] // blocks).reshape((-1,) + (1,) * (len(extent) - 1 - axis_at))
    return loudness


def setup_inputs(seed: int = 0, part: int = 0) -> dict:
    keys = jax.random.split(jax.random.key(seed), 5)
    part_keys = jax.random.split(jax.random.fold_in(keys[4], part), 5)
    return {
        "salt": jnp.clip(1.0 * jax.random.uniform(part_keys[0], (LAYERS, FINE_X, FINE_Y), jnp.float32) ** steps_of(part_keys[0], (LAYERS, FINE_X, FINE_Y), ((1, 16),), -0.2, 0.2), 0.0, 1.0),
        "recharge": with_ends((jax.random.randint(part_keys[1], (FINE_X, FINE_Y), 0, 3) < 1).astype(jnp.int32), jax.random.fold_in(part_keys[1], 1), 0, 1),
        "conductivity": jnp.clip(jnp.exp(math.log(10.0) - 4.6051702 * jax.random.uniform(part_keys[2], (LAYERS, COARSE_Y, COARSE_X), jnp.float32) ** steps_of(part_keys[2], (LAYERS, COARSE_Y, COARSE_X), ((1, 16),), -0.2, 0.2)), 0.1, 10.0),
        "codes": with_ends(jax.random.randint(part_keys[3], (COARSE_Y, COARSE_X), 0, 3), jax.random.fold_in(part_keys[3], 1), 0, 2).astype(jnp.int32),
    }


relax_weight = 0.8
vertical_ratio = 0.5
sea_penalty = 2.0
river_penalty = 0.5
river_head = 1.0
recharge_rate = 1.0
courant = 0.45
freshening = 1.0


def harmonic(first, second):
    total = first + second
    return 2.0 * first * second / (total + jnp.where(total > 0, 0.0, 1.0))


def coefficients(padded, penalty, vertical_scale):
    inner = padded[:, 1:-1, :]
    y_low = harmonic(inner, padded[:, :-2, :])
    y_high = harmonic(inner, padded[:, 2:, :])
    x_face = harmonic(inner[:, :, :-1], inner[:, :, 1:])
    zero_col = jnp.zeros_like(inner[:, :, :1])
    x_low = jnp.concatenate([zero_col, x_face], axis=2)
    x_high = jnp.concatenate([x_face, zero_col], axis=2)
    z_face = (vertical_scale * vertical_ratio) * harmonic(inner[:-1], inner[1:])
    zero_layer = jnp.zeros_like(inner[:1])
    z_up = jnp.concatenate([zero_layer, z_face], axis=0)
    z_down = jnp.concatenate([z_face, zero_layer], axis=0)
    top_term = jnp.concatenate([penalty[None], jnp.zeros_like(inner[1:])], axis=0)
    diagonal = x_low + x_high + y_low + y_high + z_up + z_down + top_term
    return (x_low, x_high, y_low, y_high, z_up, z_down, diagonal)


def neighbors(padded):
    center = padded[:, 1:-1, :]
    zero_col = jnp.zeros_like(center[:, :, :1])
    west = jnp.concatenate([zero_col, center[:, :, :-1]], axis=2)
    east = jnp.concatenate([center[:, :, 1:], zero_col], axis=2)
    zero_layer = jnp.zeros_like(center[:1])
    upper = jnp.concatenate([zero_layer, center[:-1]], axis=0)
    lower = jnp.concatenate([center[1:], zero_layer], axis=0)
    return center, west, east, padded[:, :-2, :], padded[:, 2:, :], upper, lower


def apply_operator(padded, coeffs):
    center, west, east, south, north, upper, lower = neighbors(padded)
    x_low, x_high, y_low, y_high, z_up, z_down, diagonal = coeffs
    return (diagonal * center - x_low * west - x_high * east - y_low * south
            - y_high * north - z_up * upper - z_down * lower)


def relax(padded, coeffs, right_side):
    return padded[:, 1:-1, :] + relax_weight * (right_side - apply_operator(padded, coeffs)) / coeffs[6]


def pad_rows(field):
    return jnp.pad(field, ((0, 0), (1, 1), (0, 0)))


def block_mean(field):
    leading = field.shape[:-2]
    count_a, count_b = field.shape[-2:]
    grouped = field.reshape(leading + (count_a // 4, 4, count_b // 4, 4))
    return jnp.sum(grouped, axis=(-3, -1)) * 0.0625


def pair_sum(field):
    leading = field.shape[:-2]
    count_a, count_b = field.shape[-2:]
    grouped = field.reshape(leading + (count_a // 2, 2, count_b // 2, 2))
    return jnp.sum(grouped, axis=(-3, -1))


def upsample(field, factor):
    return jnp.repeat(jnp.repeat(field, factor, axis=-2), factor, axis=-1)


def minmod(first, second):
    return 0.5 * (jnp.sign(first) + jnp.sign(second)) * jnp.minimum(jnp.abs(first), jnp.abs(second))


def portion(field, start, stop, axis):
    return lax.slice_in_dim(field, start, stop, axis=axis)


def divergence(cells, speed, axis):
    length = cells.shape[axis]
    widths = [(0, 0)] * cells.ndim
    widths[axis] = (1, 1)
    padded = jnp.pad(cells, widths)
    steps_diff = portion(padded, 1, length + 2, axis) - portion(padded, 0, length + 1, axis)
    slope = minmod(portion(steps_diff, 0, length, axis), portion(steps_diff, 1, length + 1, axis))
    faces = 0.5 * (portion(speed, 0, length - 1, axis) + portion(speed, 1, length, axis))
    left = portion(cells, 0, length - 1, axis) + 0.5 * portion(slope, 0, length - 1, axis)
    right = portion(cells, 1, length, axis) - 0.5 * portion(slope, 1, length, axis)
    flux = jnp.pad(faces * jnp.where(faces > 0, left, right), widths)
    return portion(flux, 1, length + 1, axis) - portion(flux, 0, length, axis)


def velocities(padded, coeffs, above, below):
    center, west, east, south, north, upper, lower = neighbors(padded)
    x_low, x_high, y_low, y_high, z_up, z_down, diagonal = coeffs
    vel_x = 0.5 * (x_low * (west - center) + x_high * (center - east))
    vel_y = 0.5 * (y_low * (south - center) + y_high * (center - north))
    vel_z = 0.5 * (z_up * (upper - center + above) + z_down * (center - lower + below))
    return vel_z, vel_x, vel_y


def buoyancy_terms(salt_coarse):
    face_salt = 0.5 * (salt_coarse[:-1] + salt_coarse[1:])
    zero_layer = jnp.zeros_like(salt_coarse[:1])
    above = jnp.concatenate([zero_layer, face_salt], axis=0)
    below = jnp.concatenate([face_salt, zero_layer], axis=0)
    return above, below


def boundary_penalty(codes):
    return jnp.where(codes == 1, sea_penalty, 0.0) + jnp.where(codes == 2, river_penalty, 0.0)


def source_terms(coeffs, above, below, recharge_frac, codes):
    top_source = recharge_rate * recharge_frac + river_head * jnp.where(codes == 2, river_penalty, 0.0)
    surface = jnp.concatenate([top_source[None], jnp.zeros_like(above[1:])], axis=0)
    return coeffs[4] * above - coeffs[5] * below + surface


def reference(salt, recharge, conductivity, codes):
    wet = recharge.astype(jnp.float32)
    salt_coarse = jnp.transpose(block_mean(salt), (0, 2, 1))
    recharge_frac = jnp.transpose(block_mean(wet))
    penalty = boundary_penalty(codes)
    coeffs = coefficients(pad_rows(conductivity), penalty, 1.0)
    above, below = buoyancy_terms(salt_coarse)
    right_side = source_terms(coeffs, above, below, recharge_frac, codes)
    coarse_coeffs = coefficients(pad_rows(0.25 * pair_sum(conductivity)), pair_sum(penalty), 4.0)
    head = jnp.zeros_like(conductivity)
    for cycle_no in range(CYCLES):
        for sweep in range(SMOOTH):
            head = relax(pad_rows(head), coeffs, right_side)
        residual = right_side - apply_operator(pad_rows(head), coeffs)
        coarse_resid = pair_sum(residual)
        correction = jnp.zeros_like(coarse_resid)
        for sweep in range(COARSE_SWEEPS):
            correction = relax(pad_rows(correction), coarse_coeffs, coarse_resid)
        head = head + upsample(correction, 2)
        for sweep in range(SMOOTH):
            head = relax(pad_rows(head), coeffs, right_side)
    vel_z, vel_x, vel_y = velocities(pad_rows(head), coeffs, above, below)
    fastest = jnp.max(jnp.abs(vel_x) + jnp.abs(vel_y) + jnp.abs(vel_z))
    step = courant / (fastest + 1e-6)
    fine_z = upsample(jnp.transpose(vel_z, (0, 2, 1)), 4)
    fine_x = upsample(jnp.transpose(vel_x, (0, 2, 1)), 4)
    fine_y = upsample(jnp.transpose(vel_y, (0, 2, 1)), 4)
    change = divergence(salt, fine_z, 0) + divergence(salt, fine_x, 1) + divergence(salt, fine_y, 2)
    dilution = jnp.concatenate([(freshening * wet * salt[0])[None], jnp.zeros_like(salt[1:])], axis=0)
    tendency = -step * change - step * dilution
    return tendency, head
```

```python
import jax
import jax.numpy as jnp
from jax import lax
from jax.experimental import pallas as pl
from jax.experimental.pallas import tpu as pltpu
from jax.sharding import PartitionSpec as P

CYCLES = 2
SMOOTH = 2
COARSE_SWEEPS = 6

relax_weight = 0.8
vertical_ratio = 0.5
sea_penalty = 2.0
river_penalty = 0.5
river_head = 1.0
recharge_rate = 1.0
courant = 0.45
freshening = 1.0

def padded_2(array, sides, width):
    for axis, dim in sides:
        count, length = (lax.axis_size(axis), array.shape[dim])
        up = [(i, (i + 1) % count) for i in range(count - 1)]
        down = [(j, i) for i, j in up]
        last = lax.slice_in_dim(array, length - width, length, axis=dim)
        first = lax.slice_in_dim(array, 0, width, axis=dim)
        before = lax.ppermute(last, axis, up)
        after = lax.ppermute(first, axis, down)
        array = jnp.concatenate([before, array, after], axis=dim)
    return array

def harmonic(first, second):
    total = first + second
    return 2.0 * first * second / (total + jnp.where(total > 0, 0.0, 1.0))

def coefficients(padded, penalty, vertical_scale):
    inner = padded[:, 1:-1, :]
    y_low = harmonic(inner, padded[:, :-2, :])
    y_high = harmonic(inner, padded[:, 2:, :])
    x_face = harmonic(inner[:, :, :-1], inner[:, :, 1:])
    zero_col = jnp.zeros_like(inner[:, :, :1])
    x_low = jnp.concatenate([zero_col, x_face], axis=2)
    x_high = jnp.concatenate([x_face, zero_col], axis=2)
    z_face = vertical_scale * vertical_ratio * harmonic(inner[:-1], inner[1:])
    zero_layer = jnp.zeros_like(inner[:1])
    z_up = jnp.concatenate([zero_layer, z_face], axis=0)
    z_down = jnp.concatenate([z_face, zero_layer], axis=0)
    top_term = jnp.concatenate([penalty[None], jnp.zeros_like(inner[1:])], axis=0)
    diagonal = x_low + x_high + y_low + y_high + z_up + z_down + top_term
    return (x_low, x_high, y_low, y_high, z_up, z_down, diagonal)

def neighbors(padded):
    center = padded[:, 1:-1, :]
    zero_col = jnp.zeros_like(center[:, :, :1])
    west = jnp.concatenate([zero_col, center[:, :, :-1]], axis=2)
    east = jnp.concatenate([center[:, :, 1:], zero_col], axis=2)
    zero_layer = jnp.zeros_like(center[:1])
    upper = jnp.concatenate([zero_layer, center[:-1]], axis=0)
    lower = jnp.concatenate([center[1:], zero_layer], axis=0)
    return (center, west, east, padded[:, :-2, :], padded[:, 2:, :], upper, lower)

def apply_operator(padded, coeffs):
    center, west, east, south, north, upper, lower = neighbors(padded)
    x_low, x_high, y_low, y_high, z_up, z_down, diagonal = coeffs
    return (
        diagonal * center
        - x_low * west
        - x_high * east
        - y_low * south
        - y_high * north
        - z_up * upper
        - z_down * lower
    )

def relax(padded, coeffs, right_side):
    return (
        padded[:, 1:-1, :]
        + relax_weight * (right_side - apply_operator(padded, coeffs)) / coeffs[6]
    )

def block_mean(field):
    leading = field.shape[:-2]
    count_a, count_b = field.shape[-2:]
    grouped = field.reshape(leading + (count_a // 4, 4, count_b // 4, 4))
    return jnp.sum(grouped, axis=(-3, -1)) * 0.0625

def pair_sum(field):
    leading = field.shape[:-2]
    count_a, count_b = field.shape[-2:]
    grouped = field.reshape(leading + (count_a // 2, 2, count_b // 2, 2))
    return jnp.sum(grouped, axis=(-3, -1))

def upsample(field, factor):
    return jnp.repeat(jnp.repeat(field, factor, axis=-2), factor, axis=-1)

def minmod(first, second):
    return 0.5 * (jnp.sign(first) + jnp.sign(second)) * jnp.minimum(jnp.abs(first), jnp.abs(second))

def portion(field, start, stop, axis):
    return lax.slice_in_dim(field, start, stop, axis=axis)

def divergence(cells, speed, axis):
    length = cells.shape[axis]
    widths = [(0, 0)] * cells.ndim
    widths[axis] = (1, 1)
    padded = jnp.pad(cells, widths)
    steps_diff = portion(padded, 1, length + 2, axis) - portion(padded, 0, length + 1, axis)
    slope = minmod(portion(steps_diff, 0, length, axis), portion(steps_diff, 1, length + 1, axis))
    faces = 0.5 * (portion(speed, 0, length - 1, axis) + portion(speed, 1, length, axis))
    left = portion(cells, 0, length - 1, axis) + 0.5 * portion(slope, 0, length - 1, axis)
    right = portion(cells, 1, length, axis) - 0.5 * portion(slope, 1, length, axis)
    flux = jnp.pad(faces * jnp.where(faces > 0, left, right), widths)
    return portion(flux, 1, length + 1, axis) - portion(flux, 0, length, axis)

def divergence_x(extended, faces):
    steps_diff = extended[:, 1:] - extended[:, :-1]
    slope = minmod(steps_diff[:, :-1], steps_diff[:, 1:])
    cells = extended[:, 1:-1]
    left = cells[:, :-1] + 0.5 * slope[:, :-1]
    right = cells[:, 1:] - 0.5 * slope[:, 1:]
    flux = faces * jnp.where(faces > 0, left, right)
    return flux[:, 1:] - flux[:, :-1]

def velocities(padded, coeffs, above, below):
    center, west, east, south, north, upper, lower = neighbors(padded)
    x_low, x_high, y_low, y_high, z_up, z_down, diagonal = coeffs
    vel_x = 0.5 * (x_low * (west - center) + x_high * (center - east))
    vel_y = 0.5 * (y_low * (south - center) + y_high * (center - north))
    vel_z = 0.5 * (z_up * (upper - center + above) + z_down * (center - lower + below))
    return (vel_z, vel_x, vel_y)

def buoyancy_terms(salt_coarse):
    face_salt = 0.5 * (salt_coarse[:-1] + salt_coarse[1:])
    zero_layer = jnp.zeros_like(salt_coarse[:1])
    above = jnp.concatenate([zero_layer, face_salt], axis=0)
    below = jnp.concatenate([face_salt, zero_layer], axis=0)
    return (above, below)

def boundary_penalty(codes):
    return jnp.where(codes == 1, sea_penalty, 0.0) + jnp.where(codes == 2, river_penalty, 0.0)

def source_terms(coeffs, above, below, recharge_frac, codes):
    top_source = recharge_rate * recharge_frac + river_head * jnp.where(
        codes == 2, river_penalty, 0.0
    )
    surface = jnp.concatenate([top_source[None], jnp.zeros_like(above[1:])], axis=0)
    return coeffs[4] * above - coeffs[5] * below + surface

def local_shared(salt, recharge, conductivity, codes):
    layers = salt.shape[0]
    tile = salt.shape[1]
    wet = recharge.astype(jnp.float32)
    blocks = jnp.concatenate([block_mean(salt), block_mean(wet)[None]], axis=0)
    owned = lax.all_to_all(
        jnp.transpose(blocks, (0, 2, 1)), "gx", split_axis=1, concat_axis=2, tiled=True
    )
    salt_coarse = owned[:layers]
    recharge_frac = owned[layers]
    penalty = boundary_penalty(codes)
    cond_padded = padded_2(conductivity, (("gx", 1),), 1)
    coeffs = coefficients(cond_padded, penalty, 1.0)
    above, below = buoyancy_terms(salt_coarse)
    right_side = source_terms(coeffs, above, below, recharge_frac, codes)
    coarse_cond = 0.25 * pair_sum(conductivity)
    coarse_pen = pair_sum(penalty)
    coarse_padded = padded_2(coarse_cond, (("gx", 1),), 1)
    coarse_coeffs = coefficients(coarse_padded, coarse_pen, 4.0)

    def smooth(current):
        padded = padded_2(current, (("gx", 1),), 1)
        return relax(padded, coeffs, right_side)

    head = jnp.zeros_like(conductivity)
    for cycle_no in range(CYCLES):
        for sweep in range(SMOOTH):
            head = smooth(head)
        head_padded = padded_2(head, (("gx", 1),), 1)
        residual = right_side - apply_operator(head_padded, coeffs)
        coarse_resid = pair_sum(residual)
        correction = jnp.zeros_like(coarse_resid)
        for sweep in range(COARSE_SWEEPS):
            corr_padded = padded_2(correction, (("gx", 1),), 1)
            correction = relax(corr_padded, coarse_coeffs, coarse_resid)
        head = head + upsample(correction, 2)
        for sweep in range(SMOOTH):
            head = smooth(head)
    final_padded = padded_2(head, (("gx", 1),), 1)
    vel_z, vel_x, vel_y = velocities(final_padded, coeffs, above, below)
    local_fastest = jnp.max(jnp.abs(vel_x) + jnp.abs(vel_y) + jnp.abs(vel_z))
    fastest = lax.pmax(local_fastest, "gx")
    step = courant / (fastest + 1e-06)
    packed = jnp.stack([vel_z, vel_x, vel_y])
    returned = jnp.transpose(
        lax.all_to_all(packed, "gx", split_axis=3, concat_axis=2, tiled=True), (0, 1, 3, 2)
    )
    fine_x = upsample(returned[1], 4)
    both = padded_2(jnp.stack([salt, fine_x]), (("gx", 2),), 2)
    extended = both[0]
    inner_x = both[1][:, 1:-1]
    faces = 0.5 * (inner_x[:, :-1] + inner_x[:, 1:])
    position = jnp.arange(tile + 1)
    device = lax.axis_index("gx")
    final_device = lax.axis_size("gx") - 1
    edge = (position == 0) & (device == 0) | (position == tile) & (device == final_device)
    faces = jnp.where(edge[None, :, None], 0.0, faces)
    fine_z = upsample(returned[0], 4)
    fine_y = upsample(returned[2], 4)
    change = (
        divergence(salt, fine_z, 0) + divergence_x(extended, faces) + divergence(salt, fine_y, 2)
    )
    dilution = jnp.concatenate(
        [(freshening * wet * salt[0])[None], jnp.zeros_like(salt[1:])], axis=0
    )
    tendency = -step * change - step * dilution
    return (tendency, head)

def split_dot(values, table):
    rows = values.shape[0]
    high = values.astype(jnp.bfloat16)
    rest = values - high.astype(jnp.float32)
    mid = rest.astype(jnp.bfloat16)
    low = (rest - mid.astype(jnp.float32)).astype(jnp.bfloat16)
    stacked = jnp.concatenate([high, mid, low], axis=0)
    out = jnp.dot(stacked, table, preferred_element_type=jnp.float32)
    return out[:rows] + out[rows : 2 * rows] + out[2 * rows :]

def table_of(shape, same):
    row = lax.broadcasted_iota(jnp.int32, shape, 0)
    col = lax.broadcasted_iota(jnp.int32, shape, 1)
    return jnp.where(same(row, col), 1.0, 0.0).astype(jnp.bfloat16)

def iotas(shape):
    return lax.broadcasted_iota(jnp.int32, shape, 0), lax.broadcasted_iota(jnp.int32, shape, 1)

BLOCK = 24
ROUNDS = (8, 4, 2, 1)

def pack_kernel(salt_ref, recharge_ref, cond_ref, codes_ref, block_ref, inner_ref, outer_ref, flat_ref):
    even = lax.rem(lax.axis_index("gx"), 2) == 0
    for j in range(2):
        first = salt_ref[:, j, :]
        last = salt_ref[:, 6 + j, :]
        inner_ref[j] = jnp.where(even, last, first)
        outer_ref[j] = jnp.where(even, first, last)
    sums = table_of((256, 128), lambda r, c: r // 4 == c // 2)
    salt_y = split_dot(salt_ref[...].reshape(64, 256), sums).reshape(8, 8, 128)
    sub, lane = iotas((8, 128))
    mine = sub // 4 == lane % 2
    block_ref[0:8, :] = jnp.sum(jnp.where(mine[None], salt_y, 0.0), axis=1) * 0.0625
    wet_y = jnp.dot(
        recharge_ref[...].astype(jnp.float32).astype(jnp.bfloat16), sums, preferred_element_type=jnp.float32
    )
    wet_row = jnp.sum(jnp.where(mine, wet_y, 0.0), axis=0, keepdims=True) * 0.0625
    for layer in range(8):
        flat_ref[4 * layer : 4 * layer + 4, :] = cond_ref[layer]
    spread = table_of((32, 256), lambda r, c: r == (c // 128) * 16 + (c % 128) // 8)
    cond_x = split_dot(flat_ref[...], spread)
    row32, lane32 = iotas((32, 256))
    cond_x = jnp.where(row32 // 4 == lane32 % 8, cond_x, 0.0)
    summed = cond_x[0:8] + cond_x[8:16] + cond_x[16:24] + cond_x[24:32]
    summed = summed + pltpu.roll(summed, 4, 0)
    block_ref[pl.ds(8, 4, stride=2), :] = summed[0:4, 0:128]
    block_ref[pl.ds(9, 4, stride=2), :] = summed[0:4, 128:256]
    spread_codes = table_of((32, 128), lambda r, c: r == 16 * ((7 - c % 8) % 2) + c // 8)
    code_x = jnp.dot(
        codes_ref[...].astype(jnp.float32).astype(jnp.bfloat16), spread_codes, preferred_element_type=jnp.float32
    )
    row4, lane4 = iotas((4, 128))
    code_row = jnp.sum(jnp.where(row4 == (7 - lane4 % 8) // 2, code_x, 0.0), axis=0, keepdims=True)
    block_ref[16:24, :] = jnp.where(sub == 0, wet_row, jnp.where(sub == 1, code_row, 0.0))

def harm(first, second):
    return 2.0 * first * second / (first + second)

def slope_of(back, ahead):
    return jnp.maximum(jnp.minimum(back, ahead), 0.0) + jnp.minimum(jnp.maximum(back, ahead), 0.0)

def east_of(cells, k):
    return cells[k + 1] if k + 1 < len(cells) else pltpu.roll(cells[0], 127, 1)

def west_of(cells, k):
    return cells[k - 1] if k > 0 else pltpu.roll(cells[-1], 1, 1)

def step_kernel(
    gathered_ref, inner_ref, outer_ref, salt_ref, recharge_ref, tendency_ref, head_ref, fine_ref, coarse_ref, turn_ref, wide_ref
):
    device = lax.axis_index("gx")
    sub, lane = iotas((8, 128))
    top = sub == 0
    low_g = lane % 2 == 0
    blocks = []
    for e in range(16):
        apart = device ^ e
        place = 0
        for bit, distance in enumerate(ROUNDS):
            place = place + jnp.where((apart & distance) != 0, 1 << bit, 0)
        blocks.append(pl.multiple_of(place * BLOCK, 8))

    cond_rows = jnp.concatenate([gathered_ref[pl.ds(b + 8, 8), :] for b in blocks], axis=0)
    cond_all = cond_rows.T
    cond = [cond_all[8 * k : 8 * k + 8] for k in range(16)]
    code_rows = jnp.concatenate(
        [
            pltpu.roll(jnp.broadcast_to(gathered_ref[pl.ds(b + 17, 1), :], (8, 128)), 121, 1, stride=1, stride_axis=0)
            for b in blocks
        ],
        axis=0,
    )
    code_all = code_rows.T
    means = [gathered_ref[pl.ds(b, 8), :] for b in blocks]
    wets = [gathered_ref[pl.ds(b + 16, 1), :] for b in blocks]

    def by_column(per_device, mask):
        out = []
        for k in range(16):
            a, b = per_device[k // 2], per_device[8 + k // 2]
            out.append(
                jnp.where(mask, a, pltpu.roll(b, 1, 1)) if k % 2 == 0 else jnp.where(mask, pltpu.roll(a, 127, 1), b)
            )
        return out

    salt = by_column(means, low_g)
    wet_frac = by_column(wets, low_g[0:1])

    def coefficients(cells, penalty, hop, vertical, weight_ref):
        count = len(cells)
        face_e, face_n, face_d = [], [], []
        for k in range(count):
            e = harm(cells[k], east_of(cells, k))
            if k == count - 1:
                e = jnp.where(low_g, e, 0.0)
            n = jnp.where(lane < 128 - hop, harm(cells[k], pltpu.roll(cells[k], 128 - hop, 1)), 0.0)
            d = jnp.where(sub < 7, vertical * harm(cells[k], pltpu.roll(cells[k], 7, 0)), 0.0)
            face_e.append(e)
            face_n.append(n)
            face_d.append(d)
        diags = []
        for k in range(count):
            six = (
                west_of(face_e, k),
                face_e[k],
                pltpu.roll(face_n[k], hop, 1),
                face_n[k],
                pltpu.roll(face_d[k], 1, 0),
                face_d[k],
            )
            diag = six[0] + six[1] + six[2] + six[3] + six[4] + six[5] + penalty[k]
            weight = relax_weight / diag
            for number, face in enumerate(six):
                weight_ref[number, k] = weight * face
            weight_ref[6, k] = diag * (1.0 / relax_weight)
            weight_ref[7, k] = weight
            diags.append(weight)
        return face_e, face_n, face_d, diags

    def relaxed(cells, hop, weight_ref, source_ref):
        out = []
        for k in range(len(cells)):
            here = cells[k]
            pairs = (
                west_of(cells, k),
                east_of(cells, k),
                pltpu.roll(here, hop, 1),
                pltpu.roll(here, 128 - hop, 1),
                pltpu.roll(here, 1, 0),
                pltpu.roll(here, 7, 0),
            )
            terms = [weight_ref[number, k] * pair for number, pair in enumerate(pairs)]
            base = (1.0 - relax_weight) * here + source_ref[8, k]
            out.append(((terms[0] + terms[1]) + (terms[2] + terms[3])) + ((terms[4] + terms[5]) + base))
        return out

    odd_y = (lane // 2) % 2 == 1

    def pair_sums(cells):
        out = []
        for k in range(0, len(cells), 2):
            both = cells[k] + cells[k + 1]
            out.append(both + jnp.where(odd_y, pltpu.roll(both, 2, 1), pltpu.roll(both, 126, 1)))
        return out

    penalty, river = [], []
    for k in range(16):
        code = code_all[8 * k : 8 * k + 8]
        river.append(jnp.where(top & (code == 2.0), river_penalty, 0.0))
        penalty.append(jnp.where(top & (code == 1.0), sea_penalty, 0.0) + river[k])
    face_e, face_n, face_d, weights = coefficients(cond, penalty, 2, vertical_ratio, fine_ref)
    drop = []
    for k in range(16):
        below = jnp.where(sub < 7, 0.5 * (salt[k] + pltpu.roll(salt[k], 7, 0)), 0.0)
        drop.append(below)
        pull = face_d[k] * below
        source = jnp.where(top, recharge_rate * wet_frac[k] + river_head * river[k], 0.0)
        fine_ref[8, k] = weights[k] * (pltpu.roll(pull, 1, 0) - pull + source)
        fine_ref[9, k] = face_e[k]
        fine_ref[10, k] = face_n[k]
        fine_ref[11, k] = face_d[k]
        fine_ref[12, k] = below
    coefficients([0.25 * c for c in pair_sums(cond)], pair_sums(penalty), 4, 4.0 * vertical_ratio, coarse_ref)

    head = None
    for cycle_no in range(CYCLES):
        for sweep in range(SMOOTH):
            head = [fine_ref[8, k] for k in range(16)] if head is None else relaxed(head, 2, fine_ref, fine_ref)
        ahead = relaxed(head, 2, fine_ref, fine_ref)
        resid = pair_sums([(ahead[k] - head[k]) * fine_ref[6, k] for k in range(16)])
        correction = []
        for k in range(8):
            correction.append(coarse_ref[7, k] * resid[k])
            coarse_ref[8, k] = correction[k]
        for sweep in range(COARSE_SWEEPS - 1):
            correction = relaxed(correction, 4, coarse_ref, coarse_ref)
        head = [head[k] + correction[k // 2] for k in range(16)]
        for sweep in range(SMOOTH):
            head = relaxed(head, 2, fine_ref, fine_ref)

    turn_ref[...] = jnp.concatenate(head, axis=0).T
    rows = turn_ref[pl.ds(pl.multiple_of(8 * device, 8), 8), :]
    copies = jnp.concatenate([rows] * 8, axis=0)
    row64, lane64 = iotas((64, 128))
    picked = split_dot(
        jnp.where(row64 // 8 == lane64 % 8, copies, 0.0), table_of((128, 128), lambda r, c: r // 8 == c % 16)
    )
    turn_ref[0:64, :] = picked
    lane32 = lax.broadcasted_iota(jnp.int32, (32, 128), 1)
    own = jnp.where(lane32 < 16, turn_ref[pl.ds(0, 32, stride=2), :], turn_ref[pl.ds(1, 32, stride=2), :])[:, 0:32]
    for layer in range(8):
        head_ref[layer] = own[4 * layer : 4 * layer + 4]

    flow_e, flow_n, flow_d = [], [], []
    for k in range(16):
        flow_e.append(fine_ref[9, k] * (head[k] - east_of(head, k)))
        flow_n.append(fine_ref[10, k] * (head[k] - pltpu.roll(head[k], 126, 1)))
        flow_d.append(fine_ref[11, k] * (head[k] - pltpu.roll(head[k], 7, 0) + fine_ref[12, k]))
    largest = None
    for k in range(16):
        vel_x = 0.5 * (west_of(flow_e, k) + flow_e[k])
        vel_y = 0.5 * (pltpu.roll(flow_n[k], 2, 1) + flow_n[k])
        vel_z = 0.5 * (pltpu.roll(flow_d[k], 1, 0) + flow_d[k])
        wide_ref[0, k] = vel_x
        wide_ref[1, k] = vel_y
        wide_ref[2, k] = vel_z
        speed = jnp.abs(vel_x) + jnp.abs(vel_y) + jnp.abs(vel_z)
        largest = speed if largest is None else jnp.maximum(largest, speed)
    step = courant / (jnp.max(largest, axis=(0, 1), keepdims=True) + 1e-06)

    columns = []
    for field, wanted in ((0, (0, 1, 2, 3)), (1, (1, 2)), (2, (1, 2))):
        for j in wanted:
            x = jnp.clip(2 * device - 1 + j, 0, 31)
            columns.append(jnp.where(lane % 2 == x // 16, wide_ref[field, lax.rem(x, 16)], 0.0))
    spread = split_dot(jnp.concatenate(columns, axis=0), table_of((128, 256), lambda r, c: r // 2 == c // 4))
    speed_x = [spread[8 * j : 8 * j + 8] for j in range(4)]
    speed_y = [spread[32 + 8 * j : 40 + 8 * j] for j in range(2)]
    speed_z = [spread[48 + 8 * j : 56 + 8 * j] for j in range(2)]

    layer, column = iotas((8, 256))
    even = lax.rem(device, 2) == 0
    cells = (
        [jnp.where(even, outer_ref[j], inner_ref[j]) for j in range(2)]
        + [salt_ref[:, x, :] for x in range(8)]
        + [jnp.where(even, inner_ref[j], outer_ref[j]) for j in range(2)]
    )
    diffs = [cells[i + 1] - cells[i] for i in range(11)]
    halves = [0.5 * slope_of(diffs[i], diffs[i + 1]) for i in range(10)]
    flux_x = []
    for f in range(9):
        if f % 4 == 0:
            face = 0.5 * (speed_x[f // 4] + speed_x[f // 4 + 1])
            if f == 0:
                face = jnp.where(device == 0, 0.0, face)
            if f == 8:
                face = jnp.where(device == 15, 0.0, face)
        else:
            face = speed_x[1 + f // 4]
        flux_x.append(face * jnp.where(face > 0, cells[f + 1] + halves[f], cells[f + 2] - halves[f + 1]))
    faces_y = [jnp.where(column < 255, 0.5 * (v + pltpu.roll(v, 255, 1)), 0.0) for v in speed_y]
    faces_z = [jnp.where(layer < 7, 0.5 * (v + pltpu.roll(v, 7, 0)), 0.0) for v in speed_z]
    for x in range(8):
        cell = cells[x + 2]
        ahead = jnp.where(layer < 7, pltpu.roll(cell, 7, 0), 0.0) - cell
        half = 0.5 * slope_of(jnp.where(layer > 0, pltpu.roll(ahead, 1, 0), cell), ahead)
        face = faces_z[x // 4]
        flux_z = face * jnp.where(face > 0, cell + half, pltpu.roll(cell - half, 7, 0))
        change = flux_z - pltpu.roll(flux_z, 1, 0)
        change = change + (flux_x[x + 1] - flux_x[x])
        ahead = jnp.where(column < 255, pltpu.roll(cell, 255, 1), 0.0) - cell
        half = 0.5 * slope_of(jnp.where(column > 0, pltpu.roll(ahead, 1, 1), cell), ahead)
        face = faces_y[x // 4]
        flux_y = face * jnp.where(face > 0, cell + half, pltpu.roll(cell - half, 255, 1))
        change = change + (flux_y - pltpu.roll(flux_y, 1, 1))
        wet = recharge_ref[x : x + 1, :].astype(jnp.float32)
        dilution = jnp.where(layer == 0, freshening * wet * cell, 0.0)
        tendency_ref[:, x, :] = -step * change - step * dilution

def local_small(salt, recharge, conductivity, codes):
    vmem = pl.BlockSpec(memory_space=pltpu.VMEM)
    pair = jax.ShapeDtypeStruct((2, 8, 256), jnp.float32)
    block, inner, outer = pl.pallas_call(
        pack_kernel,
        out_shape=(jax.ShapeDtypeStruct((BLOCK, 128), jnp.float32), pair, pair),
        in_specs=[vmem] * 4,
        out_specs=(vmem,) * 3,
        scratch_shapes=[pltpu.VMEM((32, 32), jnp.float32)],
        name="pack",
    )(salt, recharge, conductivity, codes)
    count = lax.axis_size("gx")
    inner = lax.ppermute(inner, "gx", [(i, i ^ 1) for i in range(count)])
    outer_pairs = [(i, i + 1) for i in range(1, count - 1, 2)]
    outer = lax.ppermute(outer, "gx", outer_pairs + [(j, i) for i, j in outer_pairs])
    for distance in ROUNDS:
        other = lax.ppermute(block, "gx", [(i, i ^ distance) for i in range(count)])
        block = jnp.concatenate([block, other], axis=0)
    return pl.pallas_call(
        step_kernel,
        out_shape=(
            jax.ShapeDtypeStruct(salt.shape, jnp.float32),
            jax.ShapeDtypeStruct(conductivity.shape, jnp.float32),
        ),
        in_specs=[vmem] * 5,
        out_specs=(vmem,) * 2,
        scratch_shapes=[
            pltpu.VMEM((13, 16, 8, 128), jnp.float32),
            pltpu.VMEM((9, 8, 8, 128), jnp.float32),
            pltpu.VMEM((128, 128), jnp.float32),
            pltpu.VMEM((3, 16, 8, 128), jnp.float32),
        ],
        compiler_params=pltpu.CompilerParams(vmem_limit_bytes=16 * 1024 * 1024),
        name="step",
    )(block, inner, outer, salt, recharge)

def local(salt, recharge, conductivity, codes):
    small = (
        lax.axis_size("gx") == 16
        and salt.shape == (8, 8, 256)
        and recharge.shape == (8, 256)
        and conductivity.shape == (8, 4, 32)
        and codes.shape == (4, 32)
    )
    return (local_small if small else local_shared)(salt, recharge, conductivity, codes)

def solution(mesh):
    return jax.shard_map(
        local,
        mesh=mesh,
        in_specs=(
            P("parts", "gx", None),
            P("gx", "parts"),
            P("parts", "gx", None),
            P("gx", "parts"),
        ),
        out_specs=(P("parts", "gx", None), P("parts", "gx", None)),
        check_vma=False,
    )
```

```python
import jax
import jax.numpy as jnp
from jax import lax
from jax.experimental import pallas as pl
from jax.experimental.pallas import tpu as pltpu
from jax.sharding import PartitionSpec as P

CYCLES = 2
SMOOTH = 2
COARSE_SWEEPS = 6

relax_weight = 0.8
vertical_ratio = 0.5
sea_penalty = 2.0
river_penalty = 0.5
river_head = 1.0
recharge_rate = 1.0
courant = 0.45
freshening = 1.0

def padded_2(array, sides, width):
    for axis, dim in sides:
        count, length = (lax.axis_size(axis), array.shape[dim])
        up = [(i, (i + 1) % count) for i in range(count - 1)]
        down = [(j, i) for i, j in up]
        last = lax.slice_in_dim(array, length - width, length, axis=dim)
        first = lax.slice_in_dim(array, 0, width, axis=dim)
        before = lax.ppermute(last, axis, up)
        after = lax.ppermute(first, axis, down)
        array = jnp.concatenate([before, array, after], axis=dim)
    return array

def harmonic(first, second):
    total = first + second
    return 2.0 * first * second / (total + jnp.where(total > 0, 0.0, 1.0))

def coefficients(padded, penalty, vertical_scale):
    inner = padded[:, 1:-1, :]
    y_low = harmonic(inner, padded[:, :-2, :])
    y_high = harmonic(inner, padded[:, 2:, :])
    x_face = harmonic(inner[:, :, :-1], inner[:, :, 1:])
    zero_col = jnp.zeros_like(inner[:, :, :1])
    x_low = jnp.concatenate([zero_col, x_face], axis=2)
    x_high = jnp.concatenate([x_face, zero_col], axis=2)
    z_face = vertical_scale * vertical_ratio * harmonic(inner[:-1], inner[1:])
    zero_layer = jnp.zeros_like(inner[:1])
    z_up = jnp.concatenate([zero_layer, z_face], axis=0)
    z_down = jnp.concatenate([z_face, zero_layer], axis=0)
    top_term = jnp.concatenate([penalty[None], jnp.zeros_like(inner[1:])], axis=0)
    diagonal = x_low + x_high + y_low + y_high + z_up + z_down + top_term
    return (x_low, x_high, y_low, y_high, z_up, z_down, diagonal)

def neighbors(padded):
    center = padded[:, 1:-1, :]
    zero_col = jnp.zeros_like(center[:, :, :1])
    west = jnp.concatenate([zero_col, center[:, :, :-1]], axis=2)
    east = jnp.concatenate([center[:, :, 1:], zero_col], axis=2)
    zero_layer = jnp.zeros_like(center[:1])
    upper = jnp.concatenate([zero_layer, center[:-1]], axis=0)
    lower = jnp.concatenate([center[1:], zero_layer], axis=0)
    return (center, west, east, padded[:, :-2, :], padded[:, 2:, :], upper, lower)

def apply_operator(padded, coeffs):
    center, west, east, south, north, upper, lower = neighbors(padded)
    x_low, x_high, y_low, y_high, z_up, z_down, diagonal = coeffs
    return (
        diagonal * center
        - x_low * west
        - x_high * east
        - y_low * south
        - y_high * north
        - z_up * upper
        - z_down * lower
    )

def relax(padded, coeffs, right_side):
    return (
        padded[:, 1:-1, :]
        + relax_weight * (right_side - apply_operator(padded, coeffs)) / coeffs[6]
    )

def block_mean(field):
    leading = field.shape[:-2]
    count_a, count_b = field.shape[-2:]
    grouped = field.reshape(leading + (count_a // 4, 4, count_b // 4, 4))
    return jnp.sum(grouped, axis=(-3, -1)) * 0.0625

def pair_sum(field):
    leading = field.shape[:-2]
    count_a, count_b = field.shape[-2:]
    grouped = field.reshape(leading + (count_a // 2, 2, count_b // 2, 2))
    return jnp.sum(grouped, axis=(-3, -1))

def upsample(field, factor):
    return jnp.repeat(jnp.repeat(field, factor, axis=-2), factor, axis=-1)

def minmod(first, second):
    return 0.5 * (jnp.sign(first) + jnp.sign(second)) * jnp.minimum(jnp.abs(first), jnp.abs(second))

def portion(field, start, stop, axis):
    return lax.slice_in_dim(field, start, stop, axis=axis)

def divergence(cells, speed, axis):
    length = cells.shape[axis]
    widths = [(0, 0)] * cells.ndim
    widths[axis] = (1, 1)
    padded = jnp.pad(cells, widths)
    steps_diff = portion(padded, 1, length + 2, axis) - portion(padded, 0, length + 1, axis)
    slope = minmod(portion(steps_diff, 0, length, axis), portion(steps_diff, 1, length + 1, axis))
    faces = 0.5 * (portion(speed, 0, length - 1, axis) + portion(speed, 1, length, axis))
    left = portion(cells, 0, length - 1, axis) + 0.5 * portion(slope, 0, length - 1, axis)
    right = portion(cells, 1, length, axis) - 0.5 * portion(slope, 1, length, axis)
    flux = jnp.pad(faces * jnp.where(faces > 0, left, right), widths)
    return portion(flux, 1, length + 1, axis) - portion(flux, 0, length, axis)

def divergence_x(extended, faces):
    steps_diff = extended[:, 1:] - extended[:, :-1]
    slope = minmod(steps_diff[:, :-1], steps_diff[:, 1:])
    cells = extended[:, 1:-1]
    left = cells[:, :-1] + 0.5 * slope[:, :-1]
    right = cells[:, 1:] - 0.5 * slope[:, 1:]
    flux = faces * jnp.where(faces > 0, left, right)
    return flux[:, 1:] - flux[:, :-1]

def velocities(padded, coeffs, above, below):
    center, west, east, south, north, upper, lower = neighbors(padded)
    x_low, x_high, y_low, y_high, z_up, z_down, diagonal = coeffs
    vel_x = 0.5 * (x_low * (west - center) + x_high * (center - east))
    vel_y = 0.5 * (y_low * (south - center) + y_high * (center - north))
    vel_z = 0.5 * (z_up * (upper - center + above) + z_down * (center - lower + below))
    return (vel_z, vel_x, vel_y)

def buoyancy_terms(salt_coarse):
    face_salt = 0.5 * (salt_coarse[:-1] + salt_coarse[1:])
    zero_layer = jnp.zeros_like(salt_coarse[:1])
    above = jnp.concatenate([zero_layer, face_salt], axis=0)
    below = jnp.concatenate([face_salt, zero_layer], axis=0)
    return (above, below)

def boundary_penalty(codes):
    return jnp.where(codes == 1, sea_penalty, 0.0) + jnp.where(codes == 2, river_penalty, 0.0)

def source_terms(coeffs, above, below, recharge_frac, codes):
    top_source = recharge_rate * recharge_frac + river_head * jnp.where(
        codes == 2, river_penalty, 0.0
    )
    surface = jnp.concatenate([top_source[None], jnp.zeros_like(above[1:])], axis=0)
    return coeffs[4] * above - coeffs[5] * below + surface

def local_shared(salt, recharge, conductivity, codes):
    layers = salt.shape[0]
    tile = salt.shape[1]
    wet = recharge.astype(jnp.float32)
    blocks = jnp.concatenate([block_mean(salt), block_mean(wet)[None]], axis=0)
    owned = lax.all_to_all(
        jnp.transpose(blocks, (0, 2, 1)), "gx", split_axis=1, concat_axis=2, tiled=True
    )
    salt_coarse = owned[:layers]
    recharge_frac = owned[layers]
    penalty = boundary_penalty(codes)
    cond_padded = padded_2(conductivity, (("gx", 1),), 1)
    coeffs = coefficients(cond_padded, penalty, 1.0)
    above, below = buoyancy_terms(salt_coarse)
    right_side = source_terms(coeffs, above, below, recharge_frac, codes)
    coarse_cond = 0.25 * pair_sum(conductivity)
    coarse_pen = pair_sum(penalty)
    coarse_padded = padded_2(coarse_cond, (("gx", 1),), 1)
    coarse_coeffs = coefficients(coarse_padded, coarse_pen, 4.0)

    def smooth(current):
        padded = padded_2(current, (("gx", 1),), 1)
        return relax(padded, coeffs, right_side)

    head = jnp.zeros_like(conductivity)
    for cycle_no in range(CYCLES):
        for sweep in range(SMOOTH):
            head = smooth(head)
        head_padded = padded_2(head, (("gx", 1),), 1)
        residual = right_side - apply_operator(head_padded, coeffs)
        coarse_resid = pair_sum(residual)
        correction = jnp.zeros_like(coarse_resid)
        for sweep in range(COARSE_SWEEPS):
            corr_padded = padded_2(correction, (("gx", 1),), 1)
            correction = relax(corr_padded, coarse_coeffs, coarse_resid)
        head = head + upsample(correction, 2)
        for sweep in range(SMOOTH):
            head = smooth(head)
    final_padded = padded_2(head, (("gx", 1),), 1)
    vel_z, vel_x, vel_y = velocities(final_padded, coeffs, above, below)
    local_fastest = jnp.max(jnp.abs(vel_x) + jnp.abs(vel_y) + jnp.abs(vel_z))
    fastest = lax.pmax(local_fastest, "gx")
    step = courant / (fastest + 1e-06)
    packed = jnp.stack([vel_z, vel_x, vel_y])
    returned = jnp.transpose(
        lax.all_to_all(packed, "gx", split_axis=3, concat_axis=2, tiled=True), (0, 1, 3, 2)
    )
    fine_x = upsample(returned[1], 4)
    both = padded_2(jnp.stack([salt, fine_x]), (("gx", 2),), 2)
    extended = both[0]
    inner_x = both[1][:, 1:-1]
    faces = 0.5 * (inner_x[:, :-1] + inner_x[:, 1:])
    position = jnp.arange(tile + 1)
    device = lax.axis_index("gx")
    final_device = lax.axis_size("gx") - 1
    edge = (position == 0) & (device == 0) | (position == tile) & (device == final_device)
    faces = jnp.where(edge[None, :, None], 0.0, faces)
    fine_z = upsample(returned[0], 4)
    fine_y = upsample(returned[2], 4)
    change = (
        divergence(salt, fine_z, 0) + divergence_x(extended, faces) + divergence(salt, fine_y, 2)
    )
    dilution = jnp.concatenate(
        [(freshening * wet * salt[0])[None], jnp.zeros_like(salt[1:])], axis=0
    )
    tendency = -step * change - step * dilution
    return (tendency, head)

def split_dot(values, table):
    rows = values.shape[0]
    high = values.astype(jnp.bfloat16)
    rest = values - high.astype(jnp.float32)
    mid = rest.astype(jnp.bfloat16)
    low = (rest - mid.astype(jnp.float32)).astype(jnp.bfloat16)
    stacked = jnp.concatenate([high, mid, low], axis=0)
    out = jnp.dot(stacked, table, preferred_element_type=jnp.float32)
    return out[:rows] + out[rows : 2 * rows] + out[2 * rows :]

def table_of(shape, same):
    row = lax.broadcasted_iota(jnp.int32, shape, 0)
    col = lax.broadcasted_iota(jnp.int32, shape, 1)
    return jnp.where(same(row, col), 1.0, 0.0).astype(jnp.bfloat16)

def iotas(shape):
    return lax.broadcasted_iota(jnp.int32, shape, 0), lax.broadcasted_iota(jnp.int32, shape, 1)

BLOCK = 24
ROUNDS = (8, 4, 2, 1)

def pack_kernel(salt_ref, recharge_ref, cond_ref, codes_ref, block_ref, middle_ref, late_ref, inner_ref, flat_ref):
    device = lax.axis_index("gx")
    even = lax.rem(device, 2) == 0
    inside = (device > 0) & (device < 15)
    crossed = device ^ jnp.where(even, device - 1, device + 1)
    for j in range(2):
        first = salt_ref[:, j, :]
        last = salt_ref[:, 6 + j, :]
        inward = jnp.where(even, last, first)
        outward = jnp.where(even, first, last)
        for half in range(2):
            place = 8 * (2 * j + half)
            part = outward[:, 128 * half : 128 * half + 128]
            inner_ref[place : place + 8, :] = inward[:, 128 * half : 128 * half + 128]
            block_ref[BLOCK + place : BLOCK + place + 8, :] = jnp.where(inside & (crossed == 15), part, 0.0)
            middle_ref[place : place + 8, :] = jnp.where(inside & (crossed == 7), part, 0.0)
            late_ref[place : place + 8, :] = jnp.where(inside & (crossed == 3), part, 0.0)
    sums = table_of((256, 128), lambda r, c: r // 4 == c // 2)
    salt_y = split_dot(salt_ref[...].reshape(64, 256), sums).reshape(8, 8, 128)
    sub, lane = iotas((8, 128))
    mine = sub // 4 == lane % 2
    block_ref[0:8, :] = jnp.sum(jnp.where(mine[None], salt_y, 0.0), axis=1) * 0.0625
    wet_y = jnp.dot(
        recharge_ref[...].astype(jnp.float32).astype(jnp.bfloat16), sums, preferred_element_type=jnp.float32
    )
    wet_row = jnp.sum(jnp.where(mine, wet_y, 0.0), axis=0, keepdims=True) * 0.0625
    for layer in range(8):
        flat_ref[4 * layer : 4 * layer + 4, :] = cond_ref[layer]
    spread = table_of((32, 256), lambda r, c: r == (c // 128) * 16 + (c % 128) // 8)
    cond_x = split_dot(flat_ref[...], spread)
    row32, lane32 = iotas((32, 256))
    cond_x = jnp.where(row32 // 4 == lane32 % 8, cond_x, 0.0)
    summed = cond_x[0:8] + cond_x[8:16] + cond_x[16:24] + cond_x[24:32]
    summed = summed + pltpu.roll(summed, 4, 0)
    block_ref[pl.ds(8, 4, stride=2), :] = summed[0:4, 0:128]
    block_ref[pl.ds(9, 4, stride=2), :] = summed[0:4, 128:256]
    spread_codes = table_of((32, 128), lambda r, c: r == 16 * ((7 - c % 8) % 2) + c // 8)
    code_x = jnp.dot(
        codes_ref[...].astype(jnp.float32).astype(jnp.bfloat16), spread_codes, preferred_element_type=jnp.float32
    )
    row4, lane4 = iotas((4, 128))
    code_row = jnp.sum(jnp.where(row4 == (7 - lane4 % 8) // 2, code_x, 0.0), axis=0, keepdims=True)
    block_ref[16:24, :] = jnp.where(sub == 0, wet_row, jnp.where(sub == 1, code_row, 0.0))

def harm(first, second):
    return 2.0 * first * second / (first + second)

def slope_of(back, ahead):
    return jnp.maximum(jnp.minimum(back, ahead), 0.0) + jnp.minimum(jnp.maximum(back, ahead), 0.0)

def east_of(cells, k):
    return cells[k + 1] if k + 1 < len(cells) else pltpu.roll(cells[0], 127, 1)

def west_of(cells, k):
    return cells[k - 1] if k > 0 else pltpu.roll(cells[-1], 1, 1)

def step_kernel(
    near_ref, far_ref, salt_ref, recharge_ref, tendency_ref, head_ref, fine_ref, coarse_ref, turn_ref, wide_ref
):
    device = lax.axis_index("gx")
    sub, lane = iotas((8, 128))
    top = sub == 0
    low_g = lane % 2 == 0
    even = lax.rem(device, 2) == 0
    blocks = []
    for e in range(0, 16, 2):
        apart = device ^ e
        place = 0
        for bit, distance in enumerate(ROUNDS[:3]):
            place = place + jnp.where((apart & distance) != 0, 1 << bit, 0)
        start = pl.multiple_of(place * BLOCK, 8)
        near = near_ref[pl.ds(start, BLOCK), :]
        far = far_ref[pl.ds(start, BLOCK), :]
        blocks += [jnp.where(even, near, far), jnp.where(even, far, near)]

    cond_rows = jnp.concatenate([b[8:16] for b in blocks], axis=0)
    cond_all = cond_rows.T
    cond = [cond_all[8 * k : 8 * k + 8] for k in range(16)]
    code_rows = jnp.concatenate(
        [
            pltpu.roll(jnp.broadcast_to(b[17:18], (8, 128)), 121, 1, stride=1, stride_axis=0)
            for b in blocks
        ],
        axis=0,
    )
    code_all = code_rows.T
    means = [b[0:8] for b in blocks]
    wets = [b[16:17] for b in blocks]

    def by_column(per_device, mask):
        out = []
        for k in range(16):
            a, b = per_device[k // 2], per_device[8 + k // 2]
            out.append(
                jnp.where(mask, a, pltpu.roll(b, 1, 1)) if k % 2 == 0 else jnp.where(mask, pltpu.roll(a, 127, 1), b)
            )
        return out

    salt = by_column(means, low_g)
    wet_frac = by_column(wets, low_g[0:1])

    def coefficients(cells, penalty, hop, vertical, weight_ref):
        count = len(cells)
        face_e, face_n, face_d = [], [], []
        for k in range(count):
            e = harm(cells[k], east_of(cells, k))
            if k == count - 1:
                e = jnp.where(low_g, e, 0.0)
            n = jnp.where(lane < 128 - hop, harm(cells[k], pltpu.roll(cells[k], 128 - hop, 1)), 0.0)
            d = jnp.where(sub < 7, vertical * harm(cells[k], pltpu.roll(cells[k], 7, 0)), 0.0)
            face_e.append(e)
            face_n.append(n)
            face_d.append(d)
        diags = []
        for k in range(count):
            six = (
                west_of(face_e, k),
                face_e[k],
                pltpu.roll(face_n[k], hop, 1),
                face_n[k],
                pltpu.roll(face_d[k], 1, 0),
                face_d[k],
            )
            diag = six[0] + six[1] + six[2] + six[3] + six[4] + six[5] + penalty[k]
            weight = relax_weight / diag
            for number, face in enumerate(six):
                weight_ref[number, k] = weight * face
            weight_ref[6, k] = diag * (1.0 / relax_weight)
            weight_ref[7, k] = weight
            diags.append(weight)
        return face_e, face_n, face_d, diags

    def relaxed(cells, hop, weight_ref, source_ref):
        out = []
        for k in range(len(cells)):
            here = cells[k]
            pairs = (
                west_of(cells, k),
                east_of(cells, k),
                pltpu.roll(here, hop, 1),
                pltpu.roll(here, 128 - hop, 1),
                pltpu.roll(here, 1, 0),
                pltpu.roll(here, 7, 0),
            )
            terms = [weight_ref[number, k] * pair for number, pair in enumerate(pairs)]
            base = (1.0 - relax_weight) * here + source_ref[8, k]
            out.append(((terms[0] + terms[1]) + (terms[2] + terms[3])) + ((terms[4] + terms[5]) + base))
        return out

    odd_y = (lane // 2) % 2 == 1

    def pair_sums(cells):
        out = []
        for k in range(0, len(cells), 2):
            both = cells[k] + cells[k + 1]
            out.append(both + jnp.where(odd_y, pltpu.roll(both, 2, 1), pltpu.roll(both, 126, 1)))
        return out

    penalty, river = [], []
    for k in range(16):
        code = code_all[8 * k : 8 * k + 8]
        river.append(jnp.where(top & (code == 2.0), river_penalty, 0.0))
        penalty.append(jnp.where(top & (code == 1.0), sea_penalty, 0.0) + river[k])
    face_e, face_n, face_d, weights = coefficients(cond, penalty, 2, vertical_ratio, fine_ref)
    drop = []
    for k in range(16):
        below = jnp.where(sub < 7, 0.5 * (salt[k] + pltpu.roll(salt[k], 7, 0)), 0.0)
        drop.append(below)
        pull = face_d[k] * below
        source = jnp.where(top, recharge_rate * wet_frac[k] + river_head * river[k], 0.0)
        fine_ref[8, k] = weights[k] * (pltpu.roll(pull, 1, 0) - pull + source)
        fine_ref[9, k] = face_e[k]
        fine_ref[10, k] = face_n[k]
        fine_ref[11, k] = face_d[k]
        fine_ref[12, k] = below
    coefficients([0.25 * c for c in pair_sums(cond)], pair_sums(penalty), 4, 4.0 * vertical_ratio, coarse_ref)

    head = None
    for cycle_no in range(CYCLES):
        for sweep in range(SMOOTH):
            head = [fine_ref[8, k] for k in range(16)] if head is None else relaxed(head, 2, fine_ref, fine_ref)
        ahead = relaxed(head, 2, fine_ref, fine_ref)
        resid = pair_sums([(ahead[k] - head[k]) * fine_ref[6, k] for k in range(16)])
        correction = []
        for k in range(8):
            correction.append(coarse_ref[7, k] * resid[k])
            coarse_ref[8, k] = correction[k]
        for sweep in range(COARSE_SWEEPS - 1):
            correction = relaxed(correction, 4, coarse_ref, coarse_ref)
        head = [head[k] + correction[k // 2] for k in range(16)]
        for sweep in range(SMOOTH):
            head = relaxed(head, 2, fine_ref, fine_ref)

    turn_ref[...] = jnp.concatenate(head, axis=0).T
    rows = turn_ref[pl.ds(pl.multiple_of(8 * device, 8), 8), :]
    copies = jnp.concatenate([rows] * 8, axis=0)
    row64, lane64 = iotas((64, 128))
    picked = split_dot(
        jnp.where(row64 // 8 == lane64 % 8, copies, 0.0), table_of((128, 128), lambda r, c: r // 8 == c % 16)
    )
    turn_ref[0:64, :] = picked
    lane32 = lax.broadcasted_iota(jnp.int32, (32, 128), 1)
    own = jnp.where(lane32 < 16, turn_ref[pl.ds(0, 32, stride=2), :], turn_ref[pl.ds(1, 32, stride=2), :])[:, 0:32]
    for layer in range(8):
        head_ref[layer] = own[4 * layer : 4 * layer + 4]

    flow_e, flow_n, flow_d = [], [], []
    for k in range(16):
        flow_e.append(fine_ref[9, k] * (head[k] - east_of(head, k)))
        flow_n.append(fine_ref[10, k] * (head[k] - pltpu.roll(head[k], 126, 1)))
        flow_d.append(fine_ref[11, k] * (head[k] - pltpu.roll(head[k], 7, 0) + fine_ref[12, k]))
    largest = None
    for k in range(16):
        vel_x = 0.5 * (west_of(flow_e, k) + flow_e[k])
        vel_y = 0.5 * (pltpu.roll(flow_n[k], 2, 1) + flow_n[k])
        vel_z = 0.5 * (pltpu.roll(flow_d[k], 1, 0) + flow_d[k])
        wide_ref[0, k] = vel_x
        wide_ref[1, k] = vel_y
        wide_ref[2, k] = vel_z
        speed = jnp.abs(vel_x) + jnp.abs(vel_y) + jnp.abs(vel_z)
        largest = speed if largest is None else jnp.maximum(largest, speed)
    step = courant / (jnp.max(largest, axis=(0, 1), keepdims=True) + 1e-06)

    columns = []
    for field, wanted in ((0, (0, 1, 2, 3)), (1, (1, 2)), (2, (1, 2))):
        for j in wanted:
            x = jnp.clip(2 * device - 1 + j, 0, 31)
            columns.append(jnp.where(lane % 2 == x // 16, wide_ref[field, lax.rem(x, 16)], 0.0))
    spread = split_dot(jnp.concatenate(columns, axis=0), table_of((128, 256), lambda r, c: r // 2 == c // 4))
    speed_x = [spread[8 * j : 8 * j + 8] for j in range(4)]
    speed_y = [spread[32 + 8 * j : 40 + 8 * j] for j in range(2)]
    speed_z = [spread[48 + 8 * j : 56 + 8 * j] for j in range(2)]

    layer, column = iotas((8, 256))
    halo = [
        jnp.concatenate([far_ref[192 + 16 * i : 200 + 16 * i, :], far_ref[200 + 16 * i : 208 + 16 * i, :]], axis=1)
        for i in range(4)
    ]
    cells = (
        [jnp.where(even, halo[j], halo[2 + j]) for j in range(2)]
        + [salt_ref[:, x, :] for x in range(8)]
        + [jnp.where(even, halo[2 + j], halo[j]) for j in range(2)]
    )
    diffs = [cells[i + 1] - cells[i] for i in range(11)]
    halves = [0.5 * slope_of(diffs[i], diffs[i + 1]) for i in range(10)]
    flux_x = []
    for f in range(9):
        if f % 4 == 0:
            face = 0.5 * (speed_x[f // 4] + speed_x[f // 4 + 1])
            if f == 0:
                face = jnp.where(device == 0, 0.0, face)
            if f == 8:
                face = jnp.where(device == 15, 0.0, face)
        else:
            face = speed_x[1 + f // 4]
        flux_x.append(face * jnp.where(face > 0, cells[f + 1] + halves[f], cells[f + 2] - halves[f + 1]))
    faces_y = [jnp.where(column < 255, 0.5 * (v + pltpu.roll(v, 255, 1)), 0.0) for v in speed_y]
    faces_z = [jnp.where(layer < 7, 0.5 * (v + pltpu.roll(v, 7, 0)), 0.0) for v in speed_z]
    for x in range(8):
        cell = cells[x + 2]
        ahead = jnp.where(layer < 7, pltpu.roll(cell, 7, 0), 0.0) - cell
        half = 0.5 * slope_of(jnp.where(layer > 0, pltpu.roll(ahead, 1, 0), cell), ahead)
        face = faces_z[x // 4]
        flux_z = face * jnp.where(face > 0, cell + half, pltpu.roll(cell - half, 7, 0))
        change = flux_z - pltpu.roll(flux_z, 1, 0)
        change = change + (flux_x[x + 1] - flux_x[x])
        ahead = jnp.where(column < 255, pltpu.roll(cell, 255, 1), 0.0) - cell
        half = 0.5 * slope_of(jnp.where(column > 0, pltpu.roll(ahead, 1, 1), cell), ahead)
        face = faces_y[x // 4]
        flux_y = face * jnp.where(face > 0, cell + half, pltpu.roll(cell - half, 255, 1))
        change = change + (flux_y - pltpu.roll(flux_y, 1, 1))
        wet = recharge_ref[x : x + 1, :].astype(jnp.float32)
        dilution = jnp.where(layer == 0, freshening * wet * cell, 0.0)
        tendency_ref[:, x, :] = -step * change - step * dilution

def local_small(salt, recharge, conductivity, codes):
    vmem = pl.BlockSpec(memory_space=pltpu.VMEM)
    columns = jax.ShapeDtypeStruct((32, 128), jnp.float32)
    block, middle, late, inner = pl.pallas_call(
        pack_kernel,
        out_shape=(jax.ShapeDtypeStruct((BLOCK + 32, 128), jnp.float32), columns, columns, columns),
        in_specs=[vmem] * 4,
        out_specs=(vmem,) * 4,
        scratch_shapes=[pltpu.VMEM((32, 32), jnp.float32)],
        name="pack",
    )(salt, recharge, conductivity, codes)

    def swapped(array, distance):
        return lax.ppermute(array, "gx", [(i, i ^ distance) for i in range(lax.axis_size("gx"))])

    other = swapped(block, ROUNDS[0])
    block = jnp.concatenate([block[:BLOCK], other[:BLOCK], other[BLOCK:] + middle])
    other = swapped(block, ROUNDS[1])
    block = jnp.concatenate([block[: 2 * BLOCK], other[: 2 * BLOCK], other[2 * BLOCK :] + late])
    other = swapped(block, ROUNDS[2])
    block = jnp.concatenate([block[: 4 * BLOCK], other, inner])
    other = swapped(block, ROUNDS[3])
    return pl.pallas_call(
        step_kernel,
        out_shape=(
            jax.ShapeDtypeStruct(salt.shape, jnp.float32),
            jax.ShapeDtypeStruct(conductivity.shape, jnp.float32),
        ),
        in_specs=[vmem] * 4,
        out_specs=(vmem,) * 2,
        scratch_shapes=[
            pltpu.VMEM((13, 16, 8, 128), jnp.float32),
            pltpu.VMEM((9, 8, 8, 128), jnp.float32),
            pltpu.VMEM((128, 128), jnp.float32),
            pltpu.VMEM((3, 16, 8, 128), jnp.float32),
        ],
        compiler_params=pltpu.CompilerParams(vmem_limit_bytes=16 * 1024 * 1024),
        name="step",
    )(block, other, salt, recharge)

def local(salt, recharge, conductivity, codes):
    small = (
        lax.axis_size("gx") == 16
        and salt.shape == (8, 8, 256)
        and recharge.shape == (8, 256)
        and conductivity.shape == (8, 4, 32)
        and codes.shape == (4, 32)
    )
    return (local_small if small else local_shared)(salt, recharge, conductivity, codes)

def solution(mesh):
    return jax.shard_map(
        local,
        mesh=mesh,
        in_specs=(
            P("parts", "gx", None),
            P("gx", "parts"),
            P("parts", "gx", None),
            P("gx", "parts"),
        ),
        out_specs=(P("parts", "gx", None), P("parts", "gx", None)),
        check_vma=False,
    )
```

```python
import jax
import jax.numpy as jnp
from jax import lax
from jax.experimental import pallas as pl
from jax.experimental.pallas import tpu as pltpu
from jax.sharding import PartitionSpec as P

CYCLES = 2
SMOOTH = 2
COARSE_SWEEPS = 6

relax_weight = 0.8
vertical_ratio = 0.5
sea_penalty = 2.0
river_penalty = 0.5
river_head = 1.0
recharge_rate = 1.0
courant = 0.45
freshening = 1.0

def padded_2(array, sides, width):
    for axis, dim in sides:
        count, length = (lax.axis_size(axis), array.shape[dim])
        up = [(i, (i + 1) % count) for i in range(count - 1)]
        down = [(j, i) for i, j in up]
        last = lax.slice_in_dim(array, length - width, length, axis=dim)
        first = lax.slice_in_dim(array, 0, width, axis=dim)
        before = lax.ppermute(last, axis, up)
        after = lax.ppermute(first, axis, down)
        array = jnp.concatenate([before, array, after], axis=dim)
    return array

def harmonic(first, second):
    total = first + second
    return 2.0 * first * second / (total + jnp.where(total > 0, 0.0, 1.0))

def coefficients(padded, penalty, vertical_scale):
    inner = padded[:, 1:-1, :]
    y_low = harmonic(inner, padded[:, :-2, :])
    y_high = harmonic(inner, padded[:, 2:, :])
    x_face = harmonic(inner[:, :, :-1], inner[:, :, 1:])
    zero_col = jnp.zeros_like(inner[:, :, :1])
    x_low = jnp.concatenate([zero_col, x_face], axis=2)
    x_high = jnp.concatenate([x_face, zero_col], axis=2)
    z_face = vertical_scale * vertical_ratio * harmonic(inner[:-1], inner[1:])
    zero_layer = jnp.zeros_like(inner[:1])
    z_up = jnp.concatenate([zero_layer, z_face], axis=0)
    z_down = jnp.concatenate([z_face, zero_layer], axis=0)
    top_term = jnp.concatenate([penalty[None], jnp.zeros_like(inner[1:])], axis=0)
    diagonal = x_low + x_high + y_low + y_high + z_up + z_down + top_term
    return (x_low, x_high, y_low, y_high, z_up, z_down, diagonal)

def neighbors(padded):
    center = padded[:, 1:-1, :]
    zero_col = jnp.zeros_like(center[:, :, :1])
    west = jnp.concatenate([zero_col, center[:, :, :-1]], axis=2)
    east = jnp.concatenate([center[:, :, 1:], zero_col], axis=2)
    zero_layer = jnp.zeros_like(center[:1])
    upper = jnp.concatenate([zero_layer, center[:-1]], axis=0)
    lower = jnp.concatenate([center[1:], zero_layer], axis=0)
    return (center, west, east, padded[:, :-2, :], padded[:, 2:, :], upper, lower)

def apply_operator(padded, coeffs):
    center, west, east, south, north, upper, lower = neighbors(padded)
    x_low, x_high, y_low, y_high, z_up, z_down, diagonal = coeffs
    return (
        diagonal * center
        - x_low * west
        - x_high * east
        - y_low * south
        - y_high * north
        - z_up * upper
        - z_down * lower
    )

def relax(padded, coeffs, right_side):
    return (
        padded[:, 1:-1, :]
        + relax_weight * (right_side - apply_operator(padded, coeffs)) / coeffs[6]
    )

def block_mean(field):
    leading = field.shape[:-2]
    count_a, count_b = field.shape[-2:]
    grouped = field.reshape(leading + (count_a // 4, 4, count_b // 4, 4))
    return jnp.sum(grouped, axis=(-3, -1)) * 0.0625

def pair_sum(field):
    leading = field.shape[:-2]
    count_a, count_b = field.shape[-2:]
    grouped = field.reshape(leading + (count_a // 2, 2, count_b // 2, 2))
    return jnp.sum(grouped, axis=(-3, -1))

def upsample(field, factor):
    return jnp.repeat(jnp.repeat(field, factor, axis=-2), factor, axis=-1)

def minmod(first, second):
    return 0.5 * (jnp.sign(first) + jnp.sign(second)) * jnp.minimum(jnp.abs(first), jnp.abs(second))

def portion(field, start, stop, axis):
    return lax.slice_in_dim(field, start, stop, axis=axis)

def divergence(cells, speed, axis):
    length = cells.shape[axis]
    widths = [(0, 0)] * cells.ndim
    widths[axis] = (1, 1)
    padded = jnp.pad(cells, widths)
    steps_diff = portion(padded, 1, length + 2, axis) - portion(padded, 0, length + 1, axis)
    slope = minmod(portion(steps_diff, 0, length, axis), portion(steps_diff, 1, length + 1, axis))
    faces = 0.5 * (portion(speed, 0, length - 1, axis) + portion(speed, 1, length, axis))
    left = portion(cells, 0, length - 1, axis) + 0.5 * portion(slope, 0, length - 1, axis)
    right = portion(cells, 1, length, axis) - 0.5 * portion(slope, 1, length, axis)
    flux = jnp.pad(faces * jnp.where(faces > 0, left, right), widths)
    return portion(flux, 1, length + 1, axis) - portion(flux, 0, length, axis)

def divergence_x(extended, faces):
    steps_diff = extended[:, 1:] - extended[:, :-1]
    slope = minmod(steps_diff[:, :-1], steps_diff[:, 1:])
    cells = extended[:, 1:-1]
    left = cells[:, :-1] + 0.5 * slope[:, :-1]
    right = cells[:, 1:] - 0.5 * slope[:, 1:]
    flux = faces * jnp.where(faces > 0, left, right)
    return flux[:, 1:] - flux[:, :-1]

def velocities(padded, coeffs, above, below):
    center, west, east, south, north, upper, lower = neighbors(padded)
    x_low, x_high, y_low, y_high, z_up, z_down, diagonal = coeffs
    vel_x = 0.5 * (x_low * (west - center) + x_high * (center - east))
    vel_y = 0.5 * (y_low * (south - center) + y_high * (center - north))
    vel_z = 0.5 * (z_up * (upper - center + above) + z_down * (center - lower + below))
    return (vel_z, vel_x, vel_y)

def buoyancy_terms(salt_coarse):
    face_salt = 0.5 * (salt_coarse[:-1] + salt_coarse[1:])
    zero_layer = jnp.zeros_like(salt_coarse[:1])
    above = jnp.concatenate([zero_layer, face_salt], axis=0)
    below = jnp.concatenate([face_salt, zero_layer], axis=0)
    return (above, below)

def boundary_penalty(codes):
    return jnp.where(codes == 1, sea_penalty, 0.0) + jnp.where(codes == 2, river_penalty, 0.0)

def source_terms(coeffs, above, below, recharge_frac, codes):
    top_source = recharge_rate * recharge_frac + river_head * jnp.where(
        codes == 2, river_penalty, 0.0
    )
    surface = jnp.concatenate([top_source[None], jnp.zeros_like(above[1:])], axis=0)
    return coeffs[4] * above - coeffs[5] * below + surface

def local_shared(salt, recharge, conductivity, codes):
    layers = salt.shape[0]
    tile = salt.shape[1]
    wet = recharge.astype(jnp.float32)
    blocks = jnp.concatenate([block_mean(salt), block_mean(wet)[None]], axis=0)
    owned = lax.all_to_all(
        jnp.transpose(blocks, (0, 2, 1)), "gx", split_axis=1, concat_axis=2, tiled=True
    )
    salt_coarse = owned[:layers]
    recharge_frac = owned[layers]
    penalty = boundary_penalty(codes)
    cond_padded = padded_2(conductivity, (("gx", 1),), 1)
    coeffs = coefficients(cond_padded, penalty, 1.0)
    above, below = buoyancy_terms(salt_coarse)
    right_side = source_terms(coeffs, above, below, recharge_frac, codes)
    coarse_cond = 0.25 * pair_sum(conductivity)
    coarse_pen = pair_sum(penalty)
    coarse_padded = padded_2(coarse_cond, (("gx", 1),), 1)
    coarse_coeffs = coefficients(coarse_padded, coarse_pen, 4.0)

    def smooth(current):
        padded = padded_2(current, (("gx", 1),), 1)
        return relax(padded, coeffs, right_side)

    head = jnp.zeros_like(conductivity)
    for cycle_no in range(CYCLES):
        for sweep in range(SMOOTH):
            head = smooth(head)
        head_padded = padded_2(head, (("gx", 1),), 1)
        residual = right_side - apply_operator(head_padded, coeffs)
        coarse_resid = pair_sum(residual)
        correction = jnp.zeros_like(coarse_resid)
        for sweep in range(COARSE_SWEEPS):
            corr_padded = padded_2(correction, (("gx", 1),), 1)
            correction = relax(corr_padded, coarse_coeffs, coarse_resid)
        head = head + upsample(correction, 2)
        for sweep in range(SMOOTH):
            head = smooth(head)
    final_padded = padded_2(head, (("gx", 1),), 1)
    vel_z, vel_x, vel_y = velocities(final_padded, coeffs, above, below)
    local_fastest = jnp.max(jnp.abs(vel_x) + jnp.abs(vel_y) + jnp.abs(vel_z))
    fastest = lax.pmax(local_fastest, "gx")
    step = courant / (fastest + 1e-06)
    packed = jnp.stack([vel_z, vel_x, vel_y])
    returned = jnp.transpose(
        lax.all_to_all(packed, "gx", split_axis=3, concat_axis=2, tiled=True), (0, 1, 3, 2)
    )
    fine_x = upsample(returned[1], 4)
    both = padded_2(jnp.stack([salt, fine_x]), (("gx", 2),), 2)
    extended = both[0]
    inner_x = both[1][:, 1:-1]
    faces = 0.5 * (inner_x[:, :-1] + inner_x[:, 1:])
    position = jnp.arange(tile + 1)
    device = lax.axis_index("gx")
    final_device = lax.axis_size("gx") - 1
    edge = (position == 0) & (device == 0) | (position == tile) & (device == final_device)
    faces = jnp.where(edge[None, :, None], 0.0, faces)
    fine_z = upsample(returned[0], 4)
    fine_y = upsample(returned[2], 4)
    change = (
        divergence(salt, fine_z, 0) + divergence_x(extended, faces) + divergence(salt, fine_y, 2)
    )
    dilution = jnp.concatenate(
        [(freshening * wet * salt[0])[None], jnp.zeros_like(salt[1:])], axis=0
    )
    tendency = -step * change - step * dilution
    return (tendency, head)

def split_dot(values, table):
    rows = values.shape[0]
    high = values.astype(jnp.bfloat16)
    rest = values - high.astype(jnp.float32)
    mid = rest.astype(jnp.bfloat16)
    low = (rest - mid.astype(jnp.float32)).astype(jnp.bfloat16)
    stacked = jnp.concatenate([high, mid, low], axis=0)
    out = jnp.dot(stacked, table, preferred_element_type=jnp.float32)
    return out[:rows] + out[rows : 2 * rows] + out[2 * rows :]

def table_of(shape, same):
    row = lax.broadcasted_iota(jnp.int32, shape, 0)
    col = lax.broadcasted_iota(jnp.int32, shape, 1)
    return jnp.where(same(row, col), 1.0, 0.0).astype(jnp.bfloat16)

def iotas(shape):
    return lax.broadcasted_iota(jnp.int32, shape, 0), lax.broadcasted_iota(jnp.int32, shape, 1)

MAIN, SMALL, COLUMNS = 16, 8, 32
ROUNDS = (3, 9, 5, 1)

def pack_kernel(salt_ref, recharge_ref, cond_ref, codes_ref, block_ref, inner_ref, relay_ref, flat_ref):
    device = lax.axis_index("gx")
    even = lax.rem(device, 2) == 0
    for j in range(2):
        first = salt_ref[:, j, :]
        last = salt_ref[:, 6 + j, :]
        inward = jnp.where(even, last, first)
        outward = jnp.where(even, first, last)
        for half in range(2):
            place = 8 * (2 * j + half)
            inner_ref[place : place + 8, :] = inward[:, 128 * half : 128 * half + 128]
            place = place + MAIN + SMALL
            block_ref[place : place + 8, :] = outward[:, 128 * half : 128 * half + 128]
    relay_ref[...] = jnp.broadcast_to(jnp.where((device == 2) | (device == 13), 1.0, 0.0), (8, 128))
    sums = table_of((256, 128), lambda r, c: r // 4 == c // 2)
    salt_y = split_dot(salt_ref[...].reshape(64, 256), sums).reshape(8, 8, 128)
    sub, lane = iotas((8, 128))
    mine = sub // 4 == lane % 2
    block_ref[0:8, :] = jnp.sum(jnp.where(mine[None], salt_y, 0.0), axis=1) * 0.0625
    wet_y = jnp.dot(
        recharge_ref[...].astype(jnp.float32).astype(jnp.bfloat16), sums, preferred_element_type=jnp.float32
    )
    wet_row = jnp.sum(jnp.where(mine, wet_y, 0.0), axis=0, keepdims=True) * 0.0625
    for layer in range(8):
        flat_ref[4 * layer : 4 * layer + 4, :] = cond_ref[layer]
    spread = table_of((32, 256), lambda r, c: r == (c // 128) * 16 + (c % 128) // 8)
    cond_x = split_dot(flat_ref[...], spread)
    row32, lane32 = iotas((32, 256))
    cond_x = jnp.where(row32 // 4 == lane32 % 8, cond_x, 0.0)
    summed = cond_x[0:8] + cond_x[8:16] + cond_x[16:24] + cond_x[24:32]
    summed = summed + pltpu.roll(summed, 4, 0)
    block_ref[pl.ds(8, 4, stride=2), :] = summed[0:4, 0:128]
    block_ref[pl.ds(9, 4, stride=2), :] = summed[0:4, 128:256]
    spread_codes = table_of((32, 128), lambda r, c: r == 16 * ((7 - c % 8) % 2) + c // 8)
    code_x = jnp.dot(
        codes_ref[...].astype(jnp.float32).astype(jnp.bfloat16), spread_codes, preferred_element_type=jnp.float32
    )
    row4, lane4 = iotas((4, 128))
    code_row = jnp.sum(jnp.where(row4 == (7 - lane4 % 8) // 2, code_x, 0.0), axis=0, keepdims=True)
    slot = 2 * ((device // 2) % 2) + 4 * (device // 8)
    block_ref[16:24, :] = jnp.where(sub == slot, wet_row, jnp.where(sub == slot + 1, code_row, 0.0))

def harm(first, second):
    return 2.0 * first * second / (first + second)

def slope_of(back, ahead):
    return jnp.maximum(jnp.minimum(back, ahead), 0.0) + jnp.minimum(jnp.maximum(back, ahead), 0.0)

def east_of(cells, k):
    return cells[k + 1] if k + 1 < len(cells) else pltpu.roll(cells[0], 127, 1)

def west_of(cells, k):
    return cells[k - 1] if k > 0 else pltpu.roll(cells[-1], 1, 1)

def step_kernel(
    near_ref, far_ref, early_ref, salt_ref, recharge_ref, tendency_ref, head_ref, fine_ref, coarse_ref, turn_ref, wide_ref
):
    device = lax.axis_index("gx")
    sub, lane = iotas((8, 128))
    top = sub == 0
    low_g = lane % 2 == 0
    even = lax.rem(device, 2) == 0
    parity = lax.rem(device + device // 2 + device // 4 + device // 8, 2)
    means, conds, smalls = [], [], []
    for e in range(0, 16, 2):
        apart = device ^ e
        place = (apart // 2) % 2 + 2 * (apart // 8) + 4 * ((apart // 4) % 2)
        mine = parity == bin(e).count("1") % 2

        def block_pair(start, rows):
            near, far = near_ref[pl.ds(start, rows), :], far_ref[pl.ds(start, rows), :]
            return [jnp.where(mine, near, far), jnp.where(mine, far, near)]

        start = pl.multiple_of(MAIN * place, 8)
        means += block_pair(start, 8)
        conds += block_pair(start + 8, 8)
        smalls += block_pair(pl.multiple_of(8 * MAIN + SMALL * ((apart // 4) % 2), 8), 8)

    slots = [2 * ((e // 2) % 2) + 4 * (e // 8) for e in range(16)]
    wets = [smalls[e][slots[e] : slots[e] + 1] for e in range(16)]
    codes = [smalls[e][slots[e] + 1 : slots[e] + 2] for e in range(16)]
    cond_all = jnp.concatenate(conds, axis=0).T
    cond = [cond_all[8 * k : 8 * k + 8] for k in range(16)]
    codes = [pltpu.roll(jnp.broadcast_to(c, (8, 128)), 121, 1, stride=1, stride_axis=0) for c in codes]
    code_all = jnp.concatenate(codes, axis=0).T

    def by_column(per_device, mask):
        out = []
        for k in range(16):
            a, b = per_device[k // 2], per_device[8 + k // 2]
            out.append(
                jnp.where(mask, a, pltpu.roll(b, 1, 1)) if k % 2 == 0 else jnp.where(mask, pltpu.roll(a, 127, 1), b)
            )
        return out

    salt = by_column(means, low_g)
    wet_frac = by_column(wets, low_g[0:1])

    def coefficients(cells, penalty, hop, vertical, weight_ref):
        count = len(cells)
        face_e, face_n, face_d = [], [], []
        for k in range(count):
            e = harm(cells[k], east_of(cells, k))
            if k == count - 1:
                e = jnp.where(low_g, e, 0.0)
            n = jnp.where(lane < 128 - hop, harm(cells[k], pltpu.roll(cells[k], 128 - hop, 1)), 0.0)
            d = jnp.where(sub < 7, vertical * harm(cells[k], pltpu.roll(cells[k], 7, 0)), 0.0)
            face_e.append(e)
            face_n.append(n)
            face_d.append(d)
        diags = []
        for k in range(count):
            six = (
                west_of(face_e, k),
                face_e[k],
                pltpu.roll(face_n[k], hop, 1),
                face_n[k],
                pltpu.roll(face_d[k], 1, 0),
                face_d[k],
            )
            diag = six[0] + six[1] + six[2] + six[3] + six[4] + six[5] + penalty[k]
            weight = relax_weight / diag
            for number, face in enumerate(six):
                weight_ref[number, k] = weight * face
            weight_ref[6, k] = diag * (1.0 / relax_weight)
            weight_ref[7, k] = weight
            diags.append(weight)
        return face_e, face_n, face_d, diags

    def relaxed(cells, hop, weight_ref, source_ref):
        out = []
        for k in range(len(cells)):
            here = cells[k]
            pairs = (
                west_of(cells, k),
                east_of(cells, k),
                pltpu.roll(here, hop, 1),
                pltpu.roll(here, 128 - hop, 1),
                pltpu.roll(here, 1, 0),
                pltpu.roll(here, 7, 0),
            )
            terms = [weight_ref[number, k] * pair for number, pair in enumerate(pairs)]
            base = (1.0 - relax_weight) * here + source_ref[8, k]
            out.append(((terms[0] + terms[1]) + (terms[2] + terms[3])) + ((terms[4] + terms[5]) + base))
        return out

    odd_y = (lane // 2) % 2 == 1

    def pair_sums(cells):
        out = []
        for k in range(0, len(cells), 2):
            both = cells[k] + cells[k + 1]
            out.append(both + jnp.where(odd_y, pltpu.roll(both, 2, 1), pltpu.roll(both, 126, 1)))
        return out

    penalty, river = [], []
    for k in range(16):
        code = code_all[8 * k : 8 * k + 8]
        river.append(jnp.where(top & (code == 2.0), river_penalty, 0.0))
        penalty.append(jnp.where(top & (code == 1.0), sea_penalty, 0.0) + river[k])
    face_e, face_n, face_d, weights = coefficients(cond, penalty, 2, vertical_ratio, fine_ref)
    drop = []
    for k in range(16):
        below = jnp.where(sub < 7, 0.5 * (salt[k] + pltpu.roll(salt[k], 7, 0)), 0.0)
        drop.append(below)
        pull = face_d[k] * below
        source = jnp.where(top, recharge_rate * wet_frac[k] + river_head * river[k], 0.0)
        fine_ref[8, k] = weights[k] * (pltpu.roll(pull, 1, 0) - pull + source)
        fine_ref[9, k] = face_e[k]
        fine_ref[10, k] = face_n[k]
        fine_ref[11, k] = face_d[k]
        fine_ref[12, k] = below
    coefficients([0.25 * c for c in pair_sums(cond)], pair_sums(penalty), 4, 4.0 * vertical_ratio, coarse_ref)

    head = None
    for cycle_no in range(CYCLES):
        for sweep in range(SMOOTH):
            head = [fine_ref[8, k] for k in range(16)] if head is None else relaxed(head, 2, fine_ref, fine_ref)
        ahead = relaxed(head, 2, fine_ref, fine_ref)
        resid = pair_sums([(ahead[k] - head[k]) * fine_ref[6, k] for k in range(16)])
        correction = []
        for k in range(8):
            correction.append(coarse_ref[7, k] * resid[k])
            coarse_ref[8, k] = correction[k]
        for sweep in range(COARSE_SWEEPS - 1):
            correction = relaxed(correction, 4, coarse_ref, coarse_ref)
        head = [head[k] + correction[k // 2] for k in range(16)]
        for sweep in range(SMOOTH):
            head = relaxed(head, 2, fine_ref, fine_ref)

    turn_ref[...] = jnp.concatenate(head, axis=0).T
    rows = turn_ref[pl.ds(pl.multiple_of(8 * device, 8), 8), :]
    copies = jnp.concatenate([rows] * 8, axis=0)
    row64, lane64 = iotas((64, 128))
    picked = split_dot(
        jnp.where(row64 // 8 == lane64 % 8, copies, 0.0), table_of((128, 128), lambda r, c: r // 8 == c % 16)
    )
    turn_ref[0:64, :] = picked
    lane32 = lax.broadcasted_iota(jnp.int32, (32, 128), 1)
    own = jnp.where(lane32 < 16, turn_ref[pl.ds(0, 32, stride=2), :], turn_ref[pl.ds(1, 32, stride=2), :])[:, 0:32]
    for layer in range(8):
        head_ref[layer] = own[4 * layer : 4 * layer + 4]

    flow_e, flow_n, flow_d = [], [], []
    for k in range(16):
        flow_e.append(fine_ref[9, k] * (head[k] - east_of(head, k)))
        flow_n.append(fine_ref[10, k] * (head[k] - pltpu.roll(head[k], 126, 1)))
        flow_d.append(fine_ref[11, k] * (head[k] - pltpu.roll(head[k], 7, 0) + fine_ref[12, k]))
    largest = None
    for k in range(16):
        vel_x = 0.5 * (west_of(flow_e, k) + flow_e[k])
        vel_y = 0.5 * (pltpu.roll(flow_n[k], 2, 1) + flow_n[k])
        vel_z = 0.5 * (pltpu.roll(flow_d[k], 1, 0) + flow_d[k])
        wide_ref[0, k] = vel_x
        wide_ref[1, k] = vel_y
        wide_ref[2, k] = vel_z
        speed = jnp.abs(vel_x) + jnp.abs(vel_y) + jnp.abs(vel_z)
        largest = speed if largest is None else jnp.maximum(largest, speed)
    step = courant / (jnp.max(largest, axis=(0, 1), keepdims=True) + 1e-06)

    columns = []
    for field, wanted in ((0, (0, 1, 2, 3)), (1, (1, 2)), (2, (1, 2))):
        for j in wanted:
            x = jnp.clip(2 * device - 1 + j, 0, 31)
            columns.append(jnp.where(lane % 2 == x // 16, wide_ref[field, lax.rem(x, 16)], 0.0))
    spread = split_dot(jnp.concatenate(columns, axis=0), table_of((128, 256), lambda r, c: r // 2 == c // 4))
    speed_x = [spread[8 * j : 8 * j + 8] for j in range(4)]
    speed_y = [spread[32 + 8 * j : 40 + 8 * j] for j in range(2)]
    speed_z = [spread[48 + 8 * j : 56 + 8 * j] for j in range(2)]

    layer, column = iotas((8, 256))
    crossed = device ^ jnp.where(even, device - 1, device + 1)
    halo = []
    for i in range(4):
        parts = []
        for half in range(2):
            place = 8 * (2 * i + half)
            here = 8 * (MAIN + 2) + place
            part = far_ref[here : here + 8, :]
            if i < 2:
                straight = early_ref[MAIN + SMALL + place : MAIN + SMALL + place + 8, :]
                part = jnp.where(crossed == 7, part, jnp.where(crossed == 15, near_ref[here : here + 8, :], 0.0))
                part = jnp.where(crossed == 3, straight, part)
            parts.append(part)
        halo.append(jnp.concatenate(parts, axis=1))
    cells = (
        [jnp.where(even, halo[j], halo[2 + j]) for j in range(2)]
        + [salt_ref[:, x, :] for x in range(8)]
        + [jnp.where(even, halo[2 + j], halo[j]) for j in range(2)]
    )
    diffs = [cells[i + 1] - cells[i] for i in range(11)]
    halves = [0.5 * slope_of(diffs[i], diffs[i + 1]) for i in range(10)]
    flux_x = []
    for f in range(9):
        if f % 4 == 0:
            face = 0.5 * (speed_x[f // 4] + speed_x[f // 4 + 1])
            if f == 0:
                face = jnp.where(device == 0, 0.0, face)
            if f == 8:
                face = jnp.where(device == 15, 0.0, face)
        else:
            face = speed_x[1 + f // 4]
        flux_x.append(face * jnp.where(face > 0, cells[f + 1] + halves[f], cells[f + 2] - halves[f + 1]))
    faces_y = [jnp.where(column < 255, 0.5 * (v + pltpu.roll(v, 255, 1)), 0.0) for v in speed_y]
    faces_z = [jnp.where(layer < 7, 0.5 * (v + pltpu.roll(v, 7, 0)), 0.0) for v in speed_z]
    for x in range(8):
        cell = cells[x + 2]
        ahead = jnp.where(layer < 7, pltpu.roll(cell, 7, 0), 0.0) - cell
        half = 0.5 * slope_of(jnp.where(layer > 0, pltpu.roll(ahead, 1, 0), cell), ahead)
        face = faces_z[x // 4]
        flux_z = face * jnp.where(face > 0, cell + half, pltpu.roll(cell - half, 7, 0))
        change = flux_z - pltpu.roll(flux_z, 1, 0)
        change = change + (flux_x[x + 1] - flux_x[x])
        ahead = jnp.where(column < 255, pltpu.roll(cell, 255, 1), 0.0) - cell
        half = 0.5 * slope_of(jnp.where(column > 0, pltpu.roll(ahead, 1, 1), cell), ahead)
        face = faces_y[x // 4]
        flux_y = face * jnp.where(face > 0, cell + half, pltpu.roll(cell - half, 255, 1))
        change = change + (flux_y - pltpu.roll(flux_y, 1, 1))
        wet = recharge_ref[x : x + 1, :].astype(jnp.float32)
        dilution = jnp.where(layer == 0, freshening * wet * cell, 0.0)
        tendency_ref[:, x, :] = -step * change - step * dilution

def local_small(salt, recharge, conductivity, codes):
    vmem = pl.BlockSpec(memory_space=pltpu.VMEM)
    block, inner, relay = pl.pallas_call(
        pack_kernel,
        out_shape=(
            pltpu.VMEM((MAIN + SMALL + COLUMNS, 128), jnp.float32),
            pltpu.VMEM((COLUMNS, 128), jnp.float32),
            pltpu.VMEM((8, 128), jnp.float32),
        ),
        in_specs=[vmem] * 4,
        out_specs=(vmem,) * 3,
        scratch_shapes=[pltpu.VMEM((32, 32), jnp.float32)],
        name="pack",
    )(salt, recharge, conductivity, codes)

    def swapped(array, distance):
        return lax.ppermute(array, "gx", [(i, i ^ distance) for i in range(lax.axis_size("gx"))])

    def small(array, count):
        return array[count * MAIN : count * MAIN + SMALL]

    def columns(array, count):
        return array[count * MAIN + SMALL :]

    first = swapped(block, ROUNDS[0])
    block = jnp.concatenate(
        [block[:MAIN], first[:MAIN], small(block, 1) + small(first, 1), columns(first, 1)]
    )
    other = swapped(block, ROUNDS[1])
    handed = jnp.where(jnp.tile(relay, (COLUMNS // 8, 1)) > 0, columns(other, 2), columns(first, 1))
    block = jnp.concatenate(
        [block[: 2 * MAIN], other[: 2 * MAIN], small(block, 2) + small(other, 2), handed]
    )
    other = swapped(block, ROUNDS[2])
    block = jnp.concatenate(
        [block[: 4 * MAIN], other[: 4 * MAIN], small(block, 4), small(other, 4), columns(other, 4), inner]
    )
    other = swapped(block, ROUNDS[3])
    return pl.pallas_call(
        step_kernel,
        out_shape=(
            jax.ShapeDtypeStruct(salt.shape, jnp.float32),
            jax.ShapeDtypeStruct(conductivity.shape, jnp.float32),
        ),
        in_specs=[vmem] * 5,
        out_specs=(vmem,) * 2,
        scratch_shapes=[
            pltpu.VMEM((13, 16, 8, 128), jnp.float32),
            pltpu.VMEM((9, 8, 8, 128), jnp.float32),
            pltpu.VMEM((128, 128), jnp.float32),
            pltpu.VMEM((3, 16, 8, 128), jnp.float32),
        ],
        compiler_params=pltpu.CompilerParams(vmem_limit_bytes=16 * 1024 * 1024),
        name="step",
    )(block, other, first, salt, recharge)

def local(salt, recharge, conductivity, codes):
    small = (
        lax.axis_size("gx") == 16
        and salt.shape == (8, 8, 256)
        and recharge.shape == (8, 256)
        and conductivity.shape == (8, 4, 32)
        and codes.shape == (4, 32)
    )
    return (local_small if small else local_shared)(salt, recharge, conductivity, codes)

def solution(mesh):
    return jax.shard_map(
        local,
        mesh=mesh,
        in_specs=(
            P("parts", "gx", None),
            P("gx", "parts"),
            P("parts", "gx", None),
            P("gx", "parts"),
        ),
        out_specs=(P("parts", "gx", None), P("parts", "gx", None)),
        check_vma=False,
    )
```

```python
import jax
import jax.numpy as jnp
from jax import lax
from jax.experimental import pallas as pl
from jax.experimental.pallas import tpu as pltpu
from jax.sharding import PartitionSpec as P

CYCLES = 2
SMOOTH = 2
COARSE_SWEEPS = 6

relax_weight = 0.8
vertical_ratio = 0.5
sea_penalty = 2.0
river_penalty = 0.5
river_head = 1.0
recharge_rate = 1.0
courant = 0.45
freshening = 1.0

def padded_2(array, sides, width):
    for axis, dim in sides:
        count, length = (lax.axis_size(axis), array.shape[dim])
        up = [(i, (i + 1) % count) for i in range(count - 1)]
        down = [(j, i) for i, j in up]
        last = lax.slice_in_dim(array, length - width, length, axis=dim)
        first = lax.slice_in_dim(array, 0, width, axis=dim)
        before = lax.ppermute(last, axis, up)
        after = lax.ppermute(first, axis, down)
        array = jnp.concatenate([before, array, after], axis=dim)
    return array

def harmonic(first, second):
    total = first + second
    return 2.0 * first * second / (total + jnp.where(total > 0, 0.0, 1.0))

def coefficients(padded, penalty, vertical_scale):
    inner = padded[:, 1:-1, :]
    y_low = harmonic(inner, padded[:, :-2, :])
    y_high = harmonic(inner, padded[:, 2:, :])
    x_face = harmonic(inner[:, :, :-1], inner[:, :, 1:])
    zero_col = jnp.zeros_like(inner[:, :, :1])
    x_low = jnp.concatenate([zero_col, x_face], axis=2)
    x_high = jnp.concatenate([x_face, zero_col], axis=2)
    z_face = vertical_scale * vertical_ratio * harmonic(inner[:-1], inner[1:])
    zero_layer = jnp.zeros_like(inner[:1])
    z_up = jnp.concatenate([zero_layer, z_face], axis=0)
    z_down = jnp.concatenate([z_face, zero_layer], axis=0)
    top_term = jnp.concatenate([penalty[None], jnp.zeros_like(inner[1:])], axis=0)
    diagonal = x_low + x_high + y_low + y_high + z_up + z_down + top_term
    return (x_low, x_high, y_low, y_high, z_up, z_down, diagonal)

def neighbors(padded):
    center = padded[:, 1:-1, :]
    zero_col = jnp.zeros_like(center[:, :, :1])
    west = jnp.concatenate([zero_col, center[:, :, :-1]], axis=2)
    east = jnp.concatenate([center[:, :, 1:], zero_col], axis=2)
    zero_layer = jnp.zeros_like(center[:1])
    upper = jnp.concatenate([zero_layer, center[:-1]], axis=0)
    lower = jnp.concatenate([center[1:], zero_layer], axis=0)
    return (center, west, east, padded[:, :-2, :], padded[:, 2:, :], upper, lower)

def apply_operator(padded, coeffs):
    center, west, east, south, north, upper, lower = neighbors(padded)
    x_low, x_high, y_low, y_high, z_up, z_down, diagonal = coeffs
    return (
        diagonal * center
        - x_low * west
        - x_high * east
        - y_low * south
        - y_high * north
        - z_up * upper
        - z_down * lower
    )

def relax(padded, coeffs, right_side):
    return (
        padded[:, 1:-1, :]
        + relax_weight * (right_side - apply_operator(padded, coeffs)) / coeffs[6]
    )

def block_mean(field):
    leading = field.shape[:-2]
    count_a, count_b = field.shape[-2:]
    grouped = field.reshape(leading + (count_a // 4, 4, count_b // 4, 4))
    return jnp.sum(grouped, axis=(-3, -1)) * 0.0625

def pair_sum(field):
    leading = field.shape[:-2]
    count_a, count_b = field.shape[-2:]
    grouped = field.reshape(leading + (count_a // 2, 2, count_b // 2, 2))
    return jnp.sum(grouped, axis=(-3, -1))

def upsample(field, factor):
    return jnp.repeat(jnp.repeat(field, factor, axis=-2), factor, axis=-1)

def minmod(first, second):
    return 0.5 * (jnp.sign(first) + jnp.sign(second)) * jnp.minimum(jnp.abs(first), jnp.abs(second))

def portion(field, start, stop, axis):
    return lax.slice_in_dim(field, start, stop, axis=axis)

def divergence(cells, speed, axis):
    length = cells.shape[axis]
    widths = [(0, 0)] * cells.ndim
    widths[axis] = (1, 1)
    padded = jnp.pad(cells, widths)
    steps_diff = portion(padded, 1, length + 2, axis) - portion(padded, 0, length + 1, axis)
    slope = minmod(portion(steps_diff, 0, length, axis), portion(steps_diff, 1, length + 1, axis))
    faces = 0.5 * (portion(speed, 0, length - 1, axis) + portion(speed, 1, length, axis))
    left = portion(cells, 0, length - 1, axis) + 0.5 * portion(slope, 0, length - 1, axis)
    right = portion(cells, 1, length, axis) - 0.5 * portion(slope, 1, length, axis)
    flux = jnp.pad(faces * jnp.where(faces > 0, left, right), widths)
    return portion(flux, 1, length + 1, axis) - portion(flux, 0, length, axis)

def divergence_x(extended, faces):
    steps_diff = extended[:, 1:] - extended[:, :-1]
    slope = minmod(steps_diff[:, :-1], steps_diff[:, 1:])
    cells = extended[:, 1:-1]
    left = cells[:, :-1] + 0.5 * slope[:, :-1]
    right = cells[:, 1:] - 0.5 * slope[:, 1:]
    flux = faces * jnp.where(faces > 0, left, right)
    return flux[:, 1:] - flux[:, :-1]

def velocities(padded, coeffs, above, below):
    center, west, east, south, north, upper, lower = neighbors(padded)
    x_low, x_high, y_low, y_high, z_up, z_down, diagonal = coeffs
    vel_x = 0.5 * (x_low * (west - center) + x_high * (center - east))
    vel_y = 0.5 * (y_low * (south - center) + y_high * (center - north))
    vel_z = 0.5 * (z_up * (upper - center + above) + z_down * (center - lower + below))
    return (vel_z, vel_x, vel_y)

def buoyancy_terms(salt_coarse):
    face_salt = 0.5 * (salt_coarse[:-1] + salt_coarse[1:])
    zero_layer = jnp.zeros_like(salt_coarse[:1])
    above = jnp.concatenate([zero_layer, face_salt], axis=0)
    below = jnp.concatenate([face_salt, zero_layer], axis=0)
    return (above, below)

def boundary_penalty(codes):
    return jnp.where(codes == 1, sea_penalty, 0.0) + jnp.where(codes == 2, river_penalty, 0.0)

def source_terms(coeffs, above, below, recharge_frac, codes):
    top_source = recharge_rate * recharge_frac + river_head * jnp.where(
        codes == 2, river_penalty, 0.0
    )
    surface = jnp.concatenate([top_source[None], jnp.zeros_like(above[1:])], axis=0)
    return coeffs[4] * above - coeffs[5] * below + surface

def local_shared(salt, recharge, conductivity, codes):
    layers = salt.shape[0]
    tile = salt.shape[1]
    wet = recharge.astype(jnp.float32)
    blocks = jnp.concatenate([block_mean(salt), block_mean(wet)[None]], axis=0)
    owned = lax.all_to_all(
        jnp.transpose(blocks, (0, 2, 1)), "gx", split_axis=1, concat_axis=2, tiled=True
    )
    salt_coarse = owned[:layers]
    recharge_frac = owned[layers]
    penalty = boundary_penalty(codes)
    cond_padded = padded_2(conductivity, (("gx", 1),), 1)
    coeffs = coefficients(cond_padded, penalty, 1.0)
    above, below = buoyancy_terms(salt_coarse)
    right_side = source_terms(coeffs, above, below, recharge_frac, codes)
    coarse_cond = 0.25 * pair_sum(conductivity)
    coarse_pen = pair_sum(penalty)
    coarse_padded = padded_2(coarse_cond, (("gx", 1),), 1)
    coarse_coeffs = coefficients(coarse_padded, coarse_pen, 4.0)

    def smooth(current):
        padded = padded_2(current, (("gx", 1),), 1)
        return relax(padded, coeffs, right_side)

    head = jnp.zeros_like(conductivity)
    for cycle_no in range(CYCLES):
        for sweep in range(SMOOTH):
            head = smooth(head)
        head_padded = padded_2(head, (("gx", 1),), 1)
        residual = right_side - apply_operator(head_padded, coeffs)
        coarse_resid = pair_sum(residual)
        correction = jnp.zeros_like(coarse_resid)
        for sweep in range(COARSE_SWEEPS):
            corr_padded = padded_2(correction, (("gx", 1),), 1)
            correction = relax(corr_padded, coarse_coeffs, coarse_resid)
        head = head + upsample(correction, 2)
        for sweep in range(SMOOTH):
            head = smooth(head)
    final_padded = padded_2(head, (("gx", 1),), 1)
    vel_z, vel_x, vel_y = velocities(final_padded, coeffs, above, below)
    local_fastest = jnp.max(jnp.abs(vel_x) + jnp.abs(vel_y) + jnp.abs(vel_z))
    fastest = lax.pmax(local_fastest, "gx")
    step = courant / (fastest + 1e-06)
    packed = jnp.stack([vel_z, vel_x, vel_y])
    returned = jnp.transpose(
        lax.all_to_all(packed, "gx", split_axis=3, concat_axis=2, tiled=True), (0, 1, 3, 2)
    )
    fine_x = upsample(returned[1], 4)
    both = padded_2(jnp.stack([salt, fine_x]), (("gx", 2),), 2)
    extended = both[0]
    inner_x = both[1][:, 1:-1]
    faces = 0.5 * (inner_x[:, :-1] + inner_x[:, 1:])
    position = jnp.arange(tile + 1)
    device = lax.axis_index("gx")
    final_device = lax.axis_size("gx") - 1
    edge = (position == 0) & (device == 0) | (position == tile) & (device == final_device)
    faces = jnp.where(edge[None, :, None], 0.0, faces)
    fine_z = upsample(returned[0], 4)
    fine_y = upsample(returned[2], 4)
    change = (
        divergence(salt, fine_z, 0) + divergence_x(extended, faces) + divergence(salt, fine_y, 2)
    )
    dilution = jnp.concatenate(
        [(freshening * wet * salt[0])[None], jnp.zeros_like(salt[1:])], axis=0
    )
    tendency = -step * change - step * dilution
    return (tendency, head)

def split_dot(values, table):
    rows = values.shape[0]
    high = values.astype(jnp.bfloat16)
    rest = values - high.astype(jnp.float32)
    mid = rest.astype(jnp.bfloat16)
    low = (rest - mid.astype(jnp.float32)).astype(jnp.bfloat16)
    stacked = jnp.concatenate([high, mid, low], axis=0)
    out = jnp.dot(stacked, table, preferred_element_type=jnp.float32)
    return out[:rows] + out[rows : 2 * rows] + out[2 * rows :]

def table_of(shape, same):
    row = lax.broadcasted_iota(jnp.int32, shape, 0)
    col = lax.broadcasted_iota(jnp.int32, shape, 1)
    return jnp.where(same(row, col), 1.0, 0.0).astype(jnp.bfloat16)

def iotas(shape):
    return lax.broadcasted_iota(jnp.int32, shape, 0), lax.broadcasted_iota(jnp.int32, shape, 1)

MAIN, SMALL, COLUMNS = 16, 8, 32
ROUNDS = ((9, 3, 5, 1), (3, 9, 5, 1))

def odd_ones(device):
    return lax.rem(device + device // 2 + device // 4 + device // 8, 2) == 1

def pack_kernel(salt_ref, recharge_ref, cond_ref, codes_ref, block_ref, inner_ref, relay_ref, flat_ref, turn_ref):
    device = lax.axis_index("gx")
    even = lax.rem(device, 2) == 0
    for j in range(2):
        first = salt_ref[:, j, :]
        last = salt_ref[:, 6 + j, :]
        inward = jnp.where(even, last, first)
        outward = jnp.where(even, first, last)
        for half in range(2):
            place = 8 * (2 * j + half)
            inner_ref[place : place + 8, :] = inward[:, 128 * half : 128 * half + 128]
            place = place + MAIN + SMALL
            block_ref[place : place + 8, :] = outward[:, 128 * half : 128 * half + 128]
    relay = jnp.where(odd_ones(device), jnp.where((device == 2) | (device == 13), 1.0, 0.0), 2.0)
    relay_ref[...] = jnp.broadcast_to(relay, (8, 128))
    turned = device // 2
    sums = table_of((256, 128), lambda r, c: r // 4 == 4 * (c // 8) + ((c - turned) % 8) // 2)
    salt_y = split_dot(salt_ref[...].reshape(64, 256), sums).reshape(8, 8, 128)
    sub, lane = iotas((8, 128))
    mine = sub // 4 == (lane - turned) % 2
    block_ref[0:8, :] = jnp.sum(jnp.where(mine[None], salt_y, 0.0), axis=1) * 0.0625
    wet_y = jnp.dot(
        recharge_ref[...].astype(jnp.float32).astype(jnp.bfloat16), sums, preferred_element_type=jnp.float32
    )
    wet_row = jnp.sum(jnp.where(mine, wet_y, 0.0), axis=0, keepdims=True) * 0.0625
    for layer in range(8):
        flat_ref[4 * layer : 4 * layer + 4, 0:32] = cond_ref[layer]
    spread = table_of((32, 128), lambda r, c: r == 4 * (c % 8) + (c // 8 - device) % 4)
    turn_ref[...] = split_dot(flat_ref[:, 0:32], spread)
    packed = jnp.zeros((8, 128), jnp.float32)
    for j in range(4):
        packed = jnp.where((lane // 8 - device) % 16 // 4 == j, turn_ref[pl.ds(j, 8, stride=4), :], packed)
    block_ref[8:16, :] = packed
    code_x = jnp.dot(
        codes_ref[...].astype(jnp.float32).astype(jnp.bfloat16), spread, preferred_element_type=jnp.float32
    )
    row4, lane4 = iotas((4, 128))
    code_row = jnp.sum(jnp.where(row4 == (lane4 // 8 - device) % 16 // 4, code_x, 0.0), axis=0, keepdims=True)
    slot = 2 * ((device // 2) % 2) + 4 * (device // 8)
    block_ref[16:24, :] = jnp.where(sub == slot, wet_row, jnp.where(sub == slot + 1, code_row, 0.0))

def harm(first, second):
    return 2.0 * first * second / (first + second)

def slope_of(back, ahead):
    return jnp.maximum(jnp.minimum(back, ahead), 0.0) + jnp.minimum(jnp.maximum(back, ahead), 0.0)

def east_of(cells, k, side):
    return cells[k + 1] if k % side < side - 1 else pltpu.roll(cells[k + 1 - side], 127, 1)

def west_of(cells, k, side):
    return cells[k - 1] if k % side > 0 else pltpu.roll(cells[k - 1 + side], 1, 1)

def north_of(cells, k, side):
    return cells[k + side] if k < side * (side - 1) else pltpu.roll(cells[k % side], 120, 1)

def south_of(cells, k, side):
    return cells[k - side] if k >= side else pltpu.roll(cells[k + side * (side - 1)], 8, 1)

def upper_of(cell):
    return pltpu.roll(cell, 1, 0)

def lower_of(cell):
    return pltpu.roll(cell, 7, 0)

def step_kernel(
    near_ref, far_ref, first_ref, second_ref, salt_ref, recharge_ref, tendency_ref, head_ref, fine_ref, coarse_ref, wide_ref
):
    device = lax.axis_index("gx")
    sub, lane = iotas((8, 128))
    top = sub == 0
    even = lax.rem(device, 2) == 0
    odd = odd_ones(device)
    means, conds, smalls = [], [], []
    for e in range(0, 16, 2):
        apart = device ^ e
        ones, nines, fives = (apart // 2) % 2, apart // 8, (apart // 4) % 2
        places = [nines + 2 * ones + 4 * fives, ones + 2 * nines + 4 * fives]
        here = jnp.where(odd, places[1], places[0])
        there = jnp.where(odd, places[0], places[1])
        mine = odd == (bin(e).count("1") % 2 == 1)

        def block_pair(here, there):
            near = near_ref[pl.ds(pl.multiple_of(here, 8), 8), :]
            far = far_ref[pl.ds(pl.multiple_of(there, 8), 8), :]
            return [jnp.where(mine, near, far), jnp.where(mine, far, near)]

        means += block_pair(MAIN * here, MAIN * there)
        conds += block_pair(MAIN * here + 8, MAIN * there + 8)
        smalls += block_pair(8 * MAIN + SMALL * fives, 8 * MAIN + SMALL * fives)

    slots = [2 * ((e // 2) % 2) + 4 * (e // 8) for e in range(16)]
    wets = [smalls[e][slots[e] : slots[e] + 1] for e in range(16)]
    codes = [smalls[e][slots[e] + 1 : slots[e] + 2] for e in range(16)]

    def diagonals(fields, index):
        count = len(fields)
        bit = 1
        while bit < count:
            high = (index & bit) != 0
            fields = [jnp.where(high, fields[(m + bit) % count], fields[m]) for m in range(count)]
            bit *= 2
        return fields

    def by_block(fields):
        group = lane[0 : fields[0].shape[0]] // 8
        picked = diagonals(fields, group)
        return [pltpu.roll(picked[-k % 16], (128 - 8 * k) % 128, 1) for k in range(16)]

    def by_lane(fields):
        within = lane % 8
        out = []
        picked = diagonals(fields, within)
        for s in range(8):
            here = picked[-s % 8]
            if s > 0:
                here = jnp.where(within < 8 - s, pltpu.roll(here, 128 - s, 1), pltpu.roll(here, 8 - s, 1))
            out.append(here)
        return out

    cond = by_block(conds)
    codes = by_block(codes)
    salt = [None] * 16
    wet_frac = [None] * 16
    wet_pairs = by_lane([jnp.where(top, wets[2 * b], wets[2 * b + 1]) for b in range(8)])
    for half in range(2):
        columns = by_lane(means[half::2])
        for s in range(8):
            k = 4 * (s // 2) + 2 * half + s % 2
            salt[k] = columns[s]
            wet_frac[k] = wet_pairs[s] if half == 0 else lower_of(wet_pairs[s])

    def coefficients(cells, penalty, side, vertical, weight_ref):
        face_w, face_e, face_s, face_n, face_d = [], [], [], [], []
        for k in range(side * side):
            e = harm(cells[k], east_of(cells, k, side))
            if k % side == side - 1:
                e = jnp.where(lane % 8 < 7, e, 0.0)
            n = harm(cells[k], north_of(cells, k, side))
            if k >= side * (side - 1):
                n = jnp.where(lane < 120, n, 0.0)
            w = face_e[k - 1] if k % side > 0 else None
            if w is None:
                w = jnp.where(lane % 8 > 0, harm(west_of(cells, k, side), cells[k]), 0.0)
            s = face_n[k - side] if k >= side else None
            if s is None:
                s = jnp.where(lane >= 8, harm(south_of(cells, k, side), cells[k]), 0.0)
            face_w.append(w)
            face_e.append(e)
            face_s.append(s)
            face_n.append(n)
            face_d.append(jnp.where(sub < 7, vertical * harm(cells[k], lower_of(cells[k])), 0.0))
        weights = []
        for k in range(side * side):
            six = (face_w[k], face_e[k], face_s[k], face_n[k], upper_of(face_d[k]), face_d[k])
            diag = six[0] + six[1] + six[2] + six[3] + six[4] + six[5] + penalty[k]
            weight = relax_weight / diag
            for number, face in enumerate(six):
                weight_ref[number, k] = weight * face
            weight_ref[6, k] = diag * (1.0 / relax_weight)
            weight_ref[7, k] = weight
            weights.append(weight)
        return (face_w, face_e, face_s, face_n, face_d), weights

    def relaxed(cells, side, weight_ref):
        out = []
        for k in range(side * side):
            here = cells[k]
            pairs = (
                west_of(cells, k, side),
                east_of(cells, k, side),
                south_of(cells, k, side),
                north_of(cells, k, side),
                upper_of(here),
                lower_of(here),
            )
            terms = [weight_ref[number, k] * pair for number, pair in enumerate(pairs)]
            base = (1.0 - relax_weight) * here + weight_ref[8, k]
            out.append(((terms[0] + terms[1]) + (terms[2] + terms[3])) + ((terms[4] + terms[5]) + base))
        return out

    def pair_sums(cells):
        return [(cells[k] + cells[k + 1]) + (cells[k + 4] + cells[k + 5]) for k in (0, 2, 8, 10)]

    penalty, river = [], []
    for k in range(16):
        code = codes[k]
        river.append(jnp.where(top & (code == 2.0), river_penalty, 0.0))
        penalty.append(jnp.where(top & (code == 1.0), sea_penalty, 0.0) + river[k])
    faces, weights = coefficients(cond, penalty, 4, vertical_ratio, fine_ref)
    for k in range(16):
        below = jnp.where(sub < 7, 0.5 * (salt[k] + lower_of(salt[k])), 0.0)
        pull = faces[4][k] * below
        source = jnp.where(top, recharge_rate * wet_frac[k] + river_head * river[k], 0.0)
        fine_ref[8, k] = weights[k] * (upper_of(pull) - pull + source)
        fine_ref[9, k] = below
        for number, face in enumerate(faces):
            fine_ref[10 + number, k] = face[k]
    coefficients([0.25 * c for c in pair_sums(cond)], pair_sums(penalty), 2, 4.0 * vertical_ratio, coarse_ref)

    head = None
    for cycle_no in range(CYCLES):
        for sweep in range(SMOOTH):
            head = [fine_ref[8, k] for k in range(16)] if head is None else relaxed(head, 4, fine_ref)
        ahead = relaxed(head, 4, fine_ref)
        resid = pair_sums([(ahead[k] - head[k]) * fine_ref[6, k] for k in range(16)])
        correction = []
        for k in range(4):
            correction.append(coarse_ref[7, k] * resid[k])
            coarse_ref[8, k] = correction[k]
        for sweep in range(COARSE_SWEEPS - 1):
            correction = relaxed(correction, 2, coarse_ref)
        head = [head[k] + correction[2 * (k // 8) + (k % 4) // 2] for k in range(16)]
        for sweep in range(SMOOTH):
            head = relaxed(head, 4, fine_ref)

    rows = []
    for j in range(4):
        row = jnp.zeros((8, 128), jnp.float32)
        for i in range(4):
            row = jnp.where(lane // 8 == i, pltpu.roll(head[4 * j + i], lax.rem(8 * i - 8 * device + 128, 128), 1), row)
        rows.append(row)
    own = split_dot(
        jnp.concatenate(rows, axis=0), table_of((128, 128), lambda r, c: (r < 32) & (c == 4 * (r % 8) + r // 8))
    )
    for j in range(4):
        head_ref[:, j, :] = own[8 * j : 8 * j + 8, 0:32]

    largest = None
    for k in range(16):
        here = head[k]
        west, east = west_of(head, k, 4) - here, here - east_of(head, k, 4)
        south, north = south_of(head, k, 4) - here, here - north_of(head, k, 4)
        vel_x = 0.5 * (fine_ref[10, k] * west + fine_ref[11, k] * east)
        vel_y = 0.5 * (fine_ref[12, k] * south + fine_ref[13, k] * north)
        flow_d = fine_ref[14, k] * (here - lower_of(here) + fine_ref[9, k])
        vel_z = 0.5 * (upper_of(flow_d) + flow_d)
        wide_ref[0, k] = vel_x
        wide_ref[1, k] = vel_y
        wide_ref[2, k] = vel_z
        speed = jnp.abs(vel_x) + jnp.abs(vel_y) + jnp.abs(vel_z)
        largest = speed if largest is None else jnp.maximum(largest, speed)
    step = courant / (jnp.max(largest, axis=(0, 1), keepdims=True) + 1e-06)

    columns = []
    for field, wanted in ((0, (0, 1, 2, 3)), (1, (1, 2)), (2, (1, 2))):
        for j in wanted:
            x = jnp.clip(2 * device - 1 + j, 0, 31)
            column = jnp.zeros((8, 128), jnp.float32)
            for i in range(4):
                turned = pltpu.roll(wide_ref[field, 4 * i + lax.rem(x, 4)], lax.rem(128 + i - x // 4, 128), 1)
                column = jnp.where(lane % 8 == i, turned, column)
            columns.append(column)

    def along(r, c):
        return (r % 8 < 4) & (c // 4 == 4 * (r // 8) + r % 8)

    spread = split_dot(jnp.concatenate(columns[:4] + columns[6:], axis=0), table_of((128, 256), along))
    speed_x = [spread[8 * j : 8 * j + 8] for j in range(4)]
    speed_z = [spread[32 + 8 * j : 40 + 8 * j] for j in range(2)]
    row, col = iotas((128, 512))
    col = jnp.where(col < 256, col, col - 257)
    inner = (col >= 0) & (col < 255)
    sides = jnp.where(inner & along(row, col), 1.0, 0.0) + jnp.where(inner & along(row, col + 1), 1.0, 0.0)
    spread = split_dot(jnp.concatenate(columns[4:6], axis=0), sides.astype(jnp.bfloat16))
    faces_n = [0.5 * spread[8 * j : 8 * j + 8, 0:256] for j in range(2)]
    faces_s = [0.5 * spread[8 * j : 8 * j + 8, 256:512] for j in range(2)]

    layer, column = iotas((8, 256))
    crossed = device ^ jnp.where(even, device - 1, device + 1)
    halo = []
    for i in range(4):
        parts = []
        for half in range(2):
            place = 8 * (2 * i + half)
            here = 8 * (MAIN + 2) + place
            part = far_ref[here : here + 8, :]
            if i < 2:
                start = MAIN + SMALL + place
                straight = first_ref[start : start + 8, :]
                straight = jnp.where(odd, straight, second_ref[MAIN + start : MAIN + start + 8, :])
                part = jnp.where(crossed == 7, part, jnp.where(crossed == 15, near_ref[here : here + 8, :], 0.0))
                part = jnp.where(crossed == 3, straight, part)
            parts.append(part)
        halo.append(jnp.concatenate(parts, axis=1))
    cells = (
        [jnp.where(even, halo[j], halo[2 + j]) for j in range(2)]
        + [salt_ref[:, x, :] for x in range(8)]
        + [jnp.where(even, halo[2 + j], halo[j]) for j in range(2)]
    )
    diffs = [cells[i + 1] - cells[i] for i in range(11)]
    halves = [0.5 * slope_of(diffs[i], diffs[i + 1]) for i in range(10)]
    flux_x = []
    for f in range(9):
        if f % 4 == 0:
            face = 0.5 * (speed_x[f // 4] + speed_x[f // 4 + 1])
            if f == 0:
                face = jnp.where(device == 0, 0.0, face)
            if f == 8:
                face = jnp.where(device == 15, 0.0, face)
        else:
            face = speed_x[1 + f // 4]
        flux_x.append(face * jnp.where(face > 0, cells[f + 1] + halves[f], cells[f + 2] - halves[f + 1]))
    faces_z = [jnp.where(layer < 7, 0.5 * (v + pltpu.roll(v, 7, 0)), 0.0) for v in speed_z]
    for x in range(8):
        cell = cells[x + 2]
        ahead = jnp.where(layer < 7, pltpu.roll(cell, 7, 0), 0.0) - cell
        half = 0.5 * slope_of(jnp.where(layer > 0, pltpu.roll(ahead, 1, 0), cell), ahead)
        face = faces_z[x // 4]
        flux_z = face * jnp.where(face > 0, cell + half, pltpu.roll(cell - half, 7, 0))
        change = flux_z - pltpu.roll(flux_z, 1, 0)
        change = change + (flux_x[x + 1] - flux_x[x])
        ahead = jnp.where(column < 255, pltpu.roll(cell, 255, 1), 0.0) - cell
        half = 0.5 * slope_of(jnp.where(column > 0, pltpu.roll(ahead, 1, 1), cell), ahead)
        below, above = cell + half, cell - half
        face = faces_n[x // 4]
        flux_n = face * jnp.where(face > 0, below, pltpu.roll(above, 255, 1))
        face = faces_s[x // 4]
        flux_s = face * jnp.where(face > 0, pltpu.roll(below, 1, 1), above)
        change = change + (flux_n - flux_s)
        wet = recharge_ref[x : x + 1, :].astype(jnp.float32)
        dilution = jnp.where(layer == 0, freshening * wet * cell, 0.0)
        tendency_ref[:, x, :] = -step * change - step * dilution

def local_small(salt, recharge, conductivity, codes):
    vmem = pl.BlockSpec(memory_space=pltpu.VMEM)
    block, inner, relay = pl.pallas_call(
        pack_kernel,
        out_shape=(
            pltpu.VMEM((MAIN + SMALL + COLUMNS, 128), jnp.float32),
            pltpu.VMEM((COLUMNS, 128), jnp.float32),
            pltpu.VMEM((8, 128), jnp.float32),
        ),
        in_specs=[vmem] * 4,
        out_specs=(vmem,) * 3,
        scratch_shapes=[pltpu.VMEM((32, 128), jnp.float32), pltpu.VMEM((32, 128), jnp.float32)],
        name="pack",
    )(salt, recharge, conductivity, codes)

    def swapped(array, turn):
        pairs = [(i, i ^ ROUNDS[bin(i).count("1") % 2][turn]) for i in range(lax.axis_size("gx"))]
        return lax.ppermute(array, "gx", pairs)

    def small(array, count):
        return array[count * MAIN : count * MAIN + SMALL]

    def columns(array, count):
        return array[count * MAIN + SMALL :]

    relay = jnp.tile(relay, (COLUMNS // 8, 1))
    first = swapped(block, 0)
    handed = jnp.where(relay > 1.5, columns(block, 1), columns(first, 1))
    block = jnp.concatenate([block[:MAIN], first[:MAIN], small(block, 1) + small(first, 1), handed])
    second = swapped(block, 1)
    handed = jnp.where(relay > 0.5, columns(second, 2), columns(first, 1))
    block = jnp.concatenate(
        [block[: 2 * MAIN], second[: 2 * MAIN], small(block, 2) + small(second, 2), handed]
    )
    other = swapped(block, 2)
    block = jnp.concatenate(
        [block[: 4 * MAIN], other[: 4 * MAIN], small(block, 4), small(other, 4), columns(other, 4), inner]
    )
    other = swapped(block, 3)
    return pl.pallas_call(
        step_kernel,
        out_shape=(
            jax.ShapeDtypeStruct(salt.shape, jnp.float32),
            jax.ShapeDtypeStruct(conductivity.shape, jnp.float32),
        ),
        in_specs=[vmem] * 6,
        out_specs=(vmem,) * 2,
        scratch_shapes=[
            pltpu.VMEM((15, 16, 8, 128), jnp.float32),
            pltpu.VMEM((9, 4, 8, 128), jnp.float32),
            pltpu.VMEM((3, 16, 8, 128), jnp.float32),
        ],
        compiler_params=pltpu.CompilerParams(vmem_limit_bytes=16 * 1024 * 1024),
        name="step",
    )(block, other, first, second, salt, recharge)

def local(salt, recharge, conductivity, codes):
    small = (
        lax.axis_size("gx") == 16
        and salt.shape == (8, 8, 256)
        and recharge.shape == (8, 256)
        and conductivity.shape == (8, 4, 32)
        and codes.shape == (4, 32)
    )
    return (local_small if small else local_shared)(salt, recharge, conductivity, codes)

def solution(mesh):
    return jax.shard_map(
        local,
        mesh=mesh,
        in_specs=(
            P("parts", "gx", None),
            P("gx", "parts"),
            P("parts", "gx", None),
            P("gx", "parts"),
        ),
        out_specs=(P("parts", "gx", None), P("parts", "gx", None)),
        check_vma=False,
    )
```

```python
import jax
import jax.numpy as jnp
from jax import lax
from jax.experimental import pallas as pl
from jax.experimental.pallas import tpu as pltpu
from jax.sharding import PartitionSpec as P

CYCLES = 2
SMOOTH = 2
COARSE_SWEEPS = 6

relax_weight = 0.8
vertical_ratio = 0.5
sea_penalty = 2.0
river_penalty = 0.5
river_head = 1.0
recharge_rate = 1.0
courant = 0.45
freshening = 1.0

def padded_2(array, sides, width):
    for axis, dim in sides:
        count, length = (lax.axis_size(axis), array.shape[dim])
        up = [(i, (i + 1) % count) for i in range(count - 1)]
        down = [(j, i) for i, j in up]
        last = lax.slice_in_dim(array, length - width, length, axis=dim)
        first = lax.slice_in_dim(array, 0, width, axis=dim)
        before = lax.ppermute(last, axis, up)
        after = lax.ppermute(first, axis, down)
        array = jnp.concatenate([before, array, after], axis=dim)
    return array

def harmonic(first, second):
    total = first + second
    return 2.0 * first * second / (total + jnp.where(total > 0, 0.0, 1.0))

def coefficients(padded, penalty, vertical_scale):
    inner = padded[:, 1:-1, :]
    y_low = harmonic(inner, padded[:, :-2, :])
    y_high = harmonic(inner, padded[:, 2:, :])
    x_face = harmonic(inner[:, :, :-1], inner[:, :, 1:])
    zero_col = jnp.zeros_like(inner[:, :, :1])
    x_low = jnp.concatenate([zero_col, x_face], axis=2)
    x_high = jnp.concatenate([x_face, zero_col], axis=2)
    z_face = vertical_scale * vertical_ratio * harmonic(inner[:-1], inner[1:])
    zero_layer = jnp.zeros_like(inner[:1])
    z_up = jnp.concatenate([zero_layer, z_face], axis=0)
    z_down = jnp.concatenate([z_face, zero_layer], axis=0)
    top_term = jnp.concatenate([penalty[None], jnp.zeros_like(inner[1:])], axis=0)
    diagonal = x_low + x_high + y_low + y_high + z_up + z_down + top_term
    return (x_low, x_high, y_low, y_high, z_up, z_down, diagonal)

def neighbors(padded):
    center = padded[:, 1:-1, :]
    zero_col = jnp.zeros_like(center[:, :, :1])
    west = jnp.concatenate([zero_col, center[:, :, :-1]], axis=2)
    east = jnp.concatenate([center[:, :, 1:], zero_col], axis=2)
    zero_layer = jnp.zeros_like(center[:1])
    upper = jnp.concatenate([zero_layer, center[:-1]], axis=0)
    lower = jnp.concatenate([center[1:], zero_layer], axis=0)
    return (center, west, east, padded[:, :-2, :], padded[:, 2:, :], upper, lower)

def apply_operator(padded, coeffs):
    center, west, east, south, north, upper, lower = neighbors(padded)
    x_low, x_high, y_low, y_high, z_up, z_down, diagonal = coeffs
    return (
        diagonal * center
        - x_low * west
        - x_high * east
        - y_low * south
        - y_high * north
        - z_up * upper
        - z_down * lower
    )

def relax(padded, coeffs, right_side):
    return (
        padded[:, 1:-1, :]
        + relax_weight * (right_side - apply_operator(padded, coeffs)) / coeffs[6]
    )

def block_mean(field):
    leading = field.shape[:-2]
    count_a, count_b = field.shape[-2:]
    grouped = field.reshape(leading + (count_a // 4, 4, count_b // 4, 4))
    return jnp.sum(grouped, axis=(-3, -1)) * 0.0625

def pair_sum(field):
    leading = field.shape[:-2]
    count_a, count_b = field.shape[-2:]
    grouped = field.reshape(leading + (count_a // 2, 2, count_b // 2, 2))
    return jnp.sum(grouped, axis=(-3, -1))

def upsample(field, factor):
    return jnp.repeat(jnp.repeat(field, factor, axis=-2), factor, axis=-1)

def minmod(first, second):
    return 0.5 * (jnp.sign(first) + jnp.sign(second)) * jnp.minimum(jnp.abs(first), jnp.abs(second))

def portion(field, start, stop, axis):
    return lax.slice_in_dim(field, start, stop, axis=axis)

def divergence(cells, speed, axis):
    length = cells.shape[axis]
    widths = [(0, 0)] * cells.ndim
    widths[axis] = (1, 1)
    padded = jnp.pad(cells, widths)
    steps_diff = portion(padded, 1, length + 2, axis) - portion(padded, 0, length + 1, axis)
    slope = minmod(portion(steps_diff, 0, length, axis), portion(steps_diff, 1, length + 1, axis))
    faces = 0.5 * (portion(speed, 0, length - 1, axis) + portion(speed, 1, length, axis))
    left = portion(cells, 0, length - 1, axis) + 0.5 * portion(slope, 0, length - 1, axis)
    right = portion(cells, 1, length, axis) - 0.5 * portion(slope, 1, length, axis)
    flux = jnp.pad(faces * jnp.where(faces > 0, left, right), widths)
    return portion(flux, 1, length + 1, axis) - portion(flux, 0, length, axis)

def divergence_x(extended, faces):
    steps_diff = extended[:, 1:] - extended[:, :-1]
    slope = minmod(steps_diff[:, :-1], steps_diff[:, 1:])
    cells = extended[:, 1:-1]
    left = cells[:, :-1] + 0.5 * slope[:, :-1]
    right = cells[:, 1:] - 0.5 * slope[:, 1:]
    flux = faces * jnp.where(faces > 0, left, right)
    return flux[:, 1:] - flux[:, :-1]

def velocities(padded, coeffs, above, below):
    center, west, east, south, north, upper, lower = neighbors(padded)
    x_low, x_high, y_low, y_high, z_up, z_down, diagonal = coeffs
    vel_x = 0.5 * (x_low * (west - center) + x_high * (center - east))
    vel_y = 0.5 * (y_low * (south - center) + y_high * (center - north))
    vel_z = 0.5 * (z_up * (upper - center + above) + z_down * (center - lower + below))
    return (vel_z, vel_x, vel_y)

def buoyancy_terms(salt_coarse):
    face_salt = 0.5 * (salt_coarse[:-1] + salt_coarse[1:])
    zero_layer = jnp.zeros_like(salt_coarse[:1])
    above = jnp.concatenate([zero_layer, face_salt], axis=0)
    below = jnp.concatenate([face_salt, zero_layer], axis=0)
    return (above, below)

def boundary_penalty(codes):
    return jnp.where(codes == 1, sea_penalty, 0.0) + jnp.where(codes == 2, river_penalty, 0.0)

def source_terms(coeffs, above, below, recharge_frac, codes):
    top_source = recharge_rate * recharge_frac + river_head * jnp.where(
        codes == 2, river_penalty, 0.0
    )
    surface = jnp.concatenate([top_source[None], jnp.zeros_like(above[1:])], axis=0)
    return coeffs[4] * above - coeffs[5] * below + surface

def local_shared(salt, recharge, conductivity, codes):
    layers = salt.shape[0]
    tile = salt.shape[1]
    wet = recharge.astype(jnp.float32)
    blocks = jnp.concatenate([block_mean(salt), block_mean(wet)[None]], axis=0)
    owned = lax.all_to_all(
        jnp.transpose(blocks, (0, 2, 1)), "gx", split_axis=1, concat_axis=2, tiled=True
    )
    salt_coarse = owned[:layers]
    recharge_frac = owned[layers]
    penalty = boundary_penalty(codes)
    cond_padded = padded_2(conductivity, (("gx", 1),), 1)
    coeffs = coefficients(cond_padded, penalty, 1.0)
    above, below = buoyancy_terms(salt_coarse)
    right_side = source_terms(coeffs, above, below, recharge_frac, codes)
    coarse_cond = 0.25 * pair_sum(conductivity)
    coarse_pen = pair_sum(penalty)
    coarse_padded = padded_2(coarse_cond, (("gx", 1),), 1)
    coarse_coeffs = coefficients(coarse_padded, coarse_pen, 4.0)

    def smooth(current):
        padded = padded_2(current, (("gx", 1),), 1)
        return relax(padded, coeffs, right_side)

    head = jnp.zeros_like(conductivity)
    for cycle_no in range(CYCLES):
        for sweep in range(SMOOTH):
            head = smooth(head)
        head_padded = padded_2(head, (("gx", 1),), 1)
        residual = right_side - apply_operator(head_padded, coeffs)
        coarse_resid = pair_sum(residual)
        correction = jnp.zeros_like(coarse_resid)
        for sweep in range(COARSE_SWEEPS):
            corr_padded = padded_2(correction, (("gx", 1),), 1)
            correction = relax(corr_padded, coarse_coeffs, coarse_resid)
        head = head + upsample(correction, 2)
        for sweep in range(SMOOTH):
            head = smooth(head)
    final_padded = padded_2(head, (("gx", 1),), 1)
    vel_z, vel_x, vel_y = velocities(final_padded, coeffs, above, below)
    local_fastest = jnp.max(jnp.abs(vel_x) + jnp.abs(vel_y) + jnp.abs(vel_z))
    fastest = lax.pmax(local_fastest, "gx")
    step = courant / (fastest + 1e-06)
    packed = jnp.stack([vel_z, vel_x, vel_y])
    returned = jnp.transpose(
        lax.all_to_all(packed, "gx", split_axis=3, concat_axis=2, tiled=True), (0, 1, 3, 2)
    )
    fine_x = upsample(returned[1], 4)
    both = padded_2(jnp.stack([salt, fine_x]), (("gx", 2),), 2)
    extended = both[0]
    inner_x = both[1][:, 1:-1]
    faces = 0.5 * (inner_x[:, :-1] + inner_x[:, 1:])
    position = jnp.arange(tile + 1)
    device = lax.axis_index("gx")
    final_device = lax.axis_size("gx") - 1
    edge = (position == 0) & (device == 0) | (position == tile) & (device == final_device)
    faces = jnp.where(edge[None, :, None], 0.0, faces)
    fine_z = upsample(returned[0], 4)
    fine_y = upsample(returned[2], 4)
    change = (
        divergence(salt, fine_z, 0) + divergence_x(extended, faces) + divergence(salt, fine_y, 2)
    )
    dilution = jnp.concatenate(
        [(freshening * wet * salt[0])[None], jnp.zeros_like(salt[1:])], axis=0
    )
    tendency = -step * change - step * dilution
    return (tendency, head)

def split_dot(values, table, terms=3):
    rows = values.shape[0]
    parts = []
    for _ in range(terms):
        parts.append(values.astype(jnp.bfloat16))
        values = values - parts[-1].astype(jnp.float32)
    out = jnp.dot(jnp.concatenate(parts, axis=0), table, preferred_element_type=jnp.float32)
    return sum(out[rows * i : rows * (i + 1)] for i in range(1, terms)) + out[:rows]

def table_of(shape, same):
    row = lax.broadcasted_iota(jnp.int32, shape, 0)
    col = lax.broadcasted_iota(jnp.int32, shape, 1)
    return jnp.where(same(row, col), 1.0, 0.0).astype(jnp.bfloat16)

def iotas(shape):
    return lax.broadcasted_iota(jnp.int32, shape, 0), lax.broadcasted_iota(jnp.int32, shape, 1)

MAIN, SMALL, COLUMNS = 16, 8, 32
ROUNDS = ((9, 3, 5, 1), (3, 9, 5, 1))

def odd_ones(device):
    return ((device ^ (device >> 1) ^ (device >> 2) ^ (device >> 3)) & 1) == 1

def pack_kernel(salt_ref, recharge_ref, cond_ref, codes_ref, block_ref, inner_ref, relay_ref, flat_ref, turn_ref):
    device = lax.axis_index("gx")
    even = (device & 1) == 0
    for j in range(2):
        first = salt_ref[:, j, :]
        last = salt_ref[:, 6 + j, :]
        inward = jnp.where(even, last, first)
        outward = jnp.where(even, first, last)
        for half in range(2):
            place = 8 * (2 * j + half)
            inner_ref[place : place + 8, :] = inward[:, 128 * half : 128 * half + 128]
            place = place + MAIN + SMALL
            block_ref[place : place + 8, :] = outward[:, 128 * half : 128 * half + 128]
    relay = jnp.where(odd_ones(device), jnp.where((device == 2) | (device == 13), 1.0, 0.0), 2.0)
    relay_ref[...] = jnp.broadcast_to(relay, (8, 128))
    turned = device >> 1
    sums = table_of((256, 128), lambda r, c: (r >> 2) == ((c >> 3) << 2) + (((c - turned) & 7) >> 1))
    salt_y = split_dot(salt_ref[...].reshape(64, 256), sums).reshape(8, 8, 128)
    sub, lane = iotas((8, 128))
    mine = (sub >> 2) == ((lane - turned) & 1)
    block_ref[0:8, :] = jnp.sum(jnp.where(mine[None], salt_y, 0.0), axis=1) * 0.0625
    wet_y = jnp.dot(
        recharge_ref[...].astype(jnp.float32).astype(jnp.bfloat16), sums, preferred_element_type=jnp.float32
    )
    wet_row = jnp.sum(jnp.where(mine, wet_y, 0.0), axis=0, keepdims=True) * 0.0625
    for layer in range(8):
        flat_ref[4 * layer : 4 * layer + 4, 0:32] = cond_ref[layer]
    spread = table_of((32, 128), lambda r, c: r == ((c & 7) << 2) + (((c >> 3) - device) & 3))
    turn_ref[...] = split_dot(flat_ref[:, 0:32], spread)
    packed = jnp.zeros((8, 128), jnp.float32)
    for j in range(4):
        packed = jnp.where(((((lane >> 3) - device) & 15) >> 2) == j, turn_ref[pl.ds(j, 8, stride=4), :], packed)
    block_ref[8:16, :] = packed
    code_x = jnp.dot(
        codes_ref[...].astype(jnp.float32).astype(jnp.bfloat16), spread, preferred_element_type=jnp.float32
    )
    row4, lane4 = iotas((4, 128))
    code_row = jnp.sum(jnp.where(row4 == ((((lane4 >> 3) - device) & 15) >> 2), code_x, 0.0), axis=0, keepdims=True)
    slot = (device & 2) + ((device & 8) >> 1)
    block_ref[16:24, :] = jnp.where(sub == slot, wet_row, jnp.where(sub == slot + 1, code_row, 0.0))

def harm(first, second):
    return 2.0 * first * second / (first + second)

def slope_of(back, ahead):
    return jnp.maximum(jnp.minimum(back, ahead), 0.0) + jnp.minimum(jnp.maximum(back, ahead), 0.0)

def east_of(cells, k, side):
    return cells[k + 1] if k % side < side - 1 else pltpu.roll(cells[k + 1 - side], 127, 1)

def west_of(cells, k, side):
    return cells[k - 1] if k % side > 0 else pltpu.roll(cells[k - 1 + side], 1, 1)

def north_of(cells, k, side):
    return cells[k + side] if k < side * (side - 1) else pltpu.roll(cells[k % side], 120, 1)

def south_of(cells, k, side):
    return cells[k - side] if k >= side else pltpu.roll(cells[k + side * (side - 1)], 8, 1)

def upper_of(cell):
    return pltpu.roll(cell, 1, 0)

def lower_of(cell):
    return pltpu.roll(cell, 7, 0)

def step_kernel(
    near_ref, far_ref, first_ref, second_ref, salt_ref, recharge_ref, tendency_ref, head_ref, fine_ref, coarse_ref, ring_ref, wide_ref
):
    device = lax.axis_index("gx")
    sub, lane = iotas((8, 128))
    top = sub == 0
    even = (device & 1) == 0
    odd = odd_ones(device)
    orders = [lambda e: ((e >> 3) & 1) + (e & 2) + (e & 4), lambda e: ((e >> 1) & 1) + ((e & 8) >> 2) + (e & 4)]
    here = jnp.where(odd, orders[1](device), orders[0](device))
    there = jnp.where(odd, orders[0](device), orders[1](device))
    flip = (device & 4) != 0
    small = []
    for ref in (near_ref, far_ref):
        halves = [ref[8 * MAIN + SMALL * i : 8 * MAIN + SMALL * (i + 1), :] for i in range(2)]
        small.append([jnp.where(flip, halves[1 - i], halves[i]) for i in range(2)])
    means, conds, smalls = [], [], []
    for e in range(16):
        mine = odd == (bin(e).count("1") % 2 == 1)
        if e % 2 == 0:
            start = pl.multiple_of((here ^ jnp.where(odd, orders[1](e), orders[0](e))) * MAIN, 8)
            near = [near_ref[pl.ds(start, 8), :], near_ref[pl.ds(pl.multiple_of(start + 8, 8), 8), :]]
            start = pl.multiple_of((there ^ jnp.where(odd, orders[0](e), orders[1](e))) * MAIN, 8)
            far = [far_ref[pl.ds(start, 8), :], far_ref[pl.ds(pl.multiple_of(start + 8, 8), 8), :]]
        means.append(jnp.where(mine, near[0], far[0]))
        conds.append(jnp.where(mine, near[1], far[1]))
        smalls.append(jnp.where(mine, small[0][(e >> 2) & 1], small[1][(e >> 2) & 1]))

    slots = [2 * ((e // 2) % 2) + 4 * (e // 8) for e in range(16)]
    wets = [smalls[e][slots[e] : slots[e] + 1] for e in range(16)]
    codes = [smalls[e][slots[e] + 1 : slots[e] + 2] for e in range(16)]

    def diagonals(fields, index):
        count = len(fields)
        bit = 1
        while bit < count:
            high = (index & bit) != 0
            fields = [jnp.where(high, fields[(m + bit) % count], fields[m]) for m in range(count)]
            bit *= 2
        return fields

    def by_block(fields):
        group = lane[0 : fields[0].shape[0]] >> 3
        picked = diagonals(fields, group)
        return [pltpu.roll(picked[-k % 16], (128 - 8 * k) % 128, 1) for k in range(16)]

    def by_lane(fields):
        within = lane & 7
        out = []
        picked = diagonals(fields, within)
        for s in range(8):
            here = picked[-s % 8]
            if s > 0:
                here = jnp.where(within < 8 - s, pltpu.roll(here, 128 - s, 1), pltpu.roll(here, 8 - s, 1))
            out.append(here)
        return out

    cond = by_block(conds)
    codes = by_block(codes)
    salt = [None] * 16
    wet_frac = [None] * 16
    wet_pairs = by_lane([jnp.where(top, wets[2 * b], wets[2 * b + 1]) for b in range(8)])
    for half in range(2):
        columns = by_lane(means[half::2])
        for s in range(8):
            k = 4 * (s // 2) + 2 * half + s % 2
            salt[k] = columns[s]
            wet_frac[k] = wet_pairs[s] if half == 0 else lower_of(wet_pairs[s])

    def coefficients(cells, penalty, side, vertical, weight_ref):
        face_w, face_e, face_s, face_n, face_d = [], [], [], [], []
        for k in range(side * side):
            e = harm(cells[k], east_of(cells, k, side))
            if k % side == side - 1:
                e = jnp.where((lane & 7) < 7, e, 0.0)
            n = harm(cells[k], north_of(cells, k, side))
            if k >= side * (side - 1):
                n = jnp.where(lane < 120, n, 0.0)
            w = face_e[k - 1] if k % side > 0 else None
            if w is None:
                w = jnp.where((lane & 7) > 0, harm(west_of(cells, k, side), cells[k]), 0.0)
            s = face_n[k - side] if k >= side else None
            if s is None:
                s = jnp.where(lane >= 8, harm(south_of(cells, k, side), cells[k]), 0.0)
            face_w.append(w)
            face_e.append(e)
            face_s.append(s)
            face_n.append(n)
            face_d.append(jnp.where(sub < 7, vertical * harm(cells[k], lower_of(cells[k])), 0.0))
        weights = []
        for k in range(side * side):
            six = (face_w[k], face_e[k], face_s[k], face_n[k], upper_of(face_d[k]), face_d[k])
            diag = six[0] + six[1] + six[2] + six[3] + six[4] + six[5] + penalty[k]
            weight = relax_weight / diag
            for number, face in enumerate(six):
                weight_ref[number, k] = weight * face
            weight_ref[6, k] = diag * (1.0 / relax_weight)
            weight_ref[7, k] = weight
            weights.append(weight)
        return (face_w, face_e, face_s, face_n, face_d), weights

    def relaxed(cells, side, weight_ref):
        out = []
        for k in range(side * side):
            here = cells[k]
            pairs = (
                west_of(cells, k, side),
                east_of(cells, k, side),
                south_of(cells, k, side),
                north_of(cells, k, side),
                upper_of(here),
                lower_of(here),
            )
            terms = [weight_ref[number, k] * pair for number, pair in enumerate(pairs)]
            base = (1.0 - relax_weight) * here + weight_ref[8, k]
            out.append(((terms[0] + terms[1]) + (terms[2] + terms[3])) + ((terms[4] + terms[5]) + base))
        return out

    ring = [(j, i) for j in range(-1, 3) for i in range(-1, 3) if (j in (0, 1)) != (i in (0, 1))]

    def beyond(cells, j, i):
        shift = -(8 * (j // 2) + i // 2) % 128
        cell = cells[2 * (j % 2) + i % 2]
        return pltpu.roll(cell, shift, 1) if shift else cell

    def relaxed_twice(cells):
        def step(at, j, i, weights):
            here = at(j, i)
            pairs = (at(j, i - 1), at(j, i + 1), at(j - 1, i), at(j + 1, i), upper_of(here), lower_of(here))
            terms = [weights(number) * pair for number, pair in enumerate(pairs)]
            base = (1.0 - relax_weight) * here + weights(8)
            return ((terms[0] + terms[1]) + (terms[2] + terms[3])) + ((terms[4] + terms[5]) + base)

        old, new = {}, {}

        def at_old(j, i):
            if (j, i) not in old:
                old[j, i] = beyond(cells, j, i)
            return old[j, i]

        for q, (j, i) in enumerate(ring):
            new[j, i] = step(at_old, j, i, lambda number, q=q: ring_ref[number, q])
        for k in range(4):
            new[k // 2, k % 2] = step(at_old, k // 2, k % 2, lambda number, k=k: coarse_ref[number, k])
        return [
            step(lambda j, i: new[j, i], k // 2, k % 2, lambda number, k=k: coarse_ref[number, k]) for k in range(4)
        ]

    def pair_sums(cells):
        return [(cells[k] + cells[k + 1]) + (cells[k + 4] + cells[k + 5]) for k in (0, 2, 8, 10)]

    penalty, river = [], []
    for k in range(16):
        code = codes[k]
        river.append(jnp.where(top & (code == 2.0), river_penalty, 0.0))
        penalty.append(jnp.where(top & (code == 1.0), sea_penalty, 0.0) + river[k])
    faces, weights = coefficients(cond, penalty, 4, vertical_ratio, fine_ref)
    for k in range(16):
        below = jnp.where(sub < 7, 0.5 * (salt[k] + lower_of(salt[k])), 0.0)
        pull = faces[4][k] * below
        source = jnp.where(top, recharge_rate * wet_frac[k] + river_head * river[k], 0.0)
        fine_ref[8, k] = weights[k] * (upper_of(pull) - pull + source)
        fine_ref[9, k] = below
        for number, face in enumerate(faces):
            fine_ref[10 + number, k] = face[k]
    coefficients([0.25 * c for c in pair_sums(cond)], pair_sums(penalty), 2, 4.0 * vertical_ratio, coarse_ref)
    for number in range(6):
        cells = [coarse_ref[number, k] for k in range(4)]
        for q, (j, i) in enumerate(ring):
            ring_ref[number, q] = beyond(cells, j, i)

    head = None
    for cycle_no in range(CYCLES):
        for sweep in range(SMOOTH):
            head = [fine_ref[8, k] for k in range(16)] if head is None else relaxed(head, 4, fine_ref)
        ahead = relaxed(head, 4, fine_ref)
        resid = pair_sums([(ahead[k] - head[k]) * fine_ref[6, k] for k in range(16)])
        correction = []
        for k in range(4):
            correction.append(coarse_ref[7, k] * resid[k])
            coarse_ref[8, k] = correction[k]
        for q, (j, i) in enumerate(ring):
            ring_ref[8, q] = beyond(correction, j, i)
        for sweep in range((COARSE_SWEEPS - 1) // 2):
            correction = relaxed_twice(correction)
        for sweep in range((COARSE_SWEEPS - 1) % 2):
            correction = relaxed(correction, 2, coarse_ref)
        head = [head[k] + correction[2 * (k // 8) + (k % 4) // 2] for k in range(16)]
        for sweep in range(SMOOTH):
            head = relaxed(head, 4, fine_ref)

    own = 8 * device + ((lane & 31) >> 2)
    for j in range(4):
        row = jnp.take_along_axis(head[4 * j], own, axis=1)
        for i in range(1, 4):
            row = jnp.where((lane & 3) == i, jnp.take_along_axis(head[4 * j + i], own, axis=1), row)
        head_ref[:, j, :] = row[:, 0:32]

    largest = None
    for k in range(16):
        here = head[k]
        west, east = west_of(head, k, 4) - here, here - east_of(head, k, 4)
        south, north = south_of(head, k, 4) - here, here - north_of(head, k, 4)
        vel_x = 0.5 * (fine_ref[10, k] * west + fine_ref[11, k] * east)
        vel_y = 0.5 * (fine_ref[12, k] * south + fine_ref[13, k] * north)
        flow_d = fine_ref[14, k] * (here - lower_of(here) + fine_ref[9, k])
        vel_z = 0.5 * (upper_of(flow_d) + flow_d)
        wide_ref[0, k] = vel_x
        wide_ref[1, k] = vel_y
        wide_ref[2, k] = vel_z
        speed = jnp.abs(vel_x) + jnp.abs(vel_y) + jnp.abs(vel_z)
        largest = speed if largest is None else jnp.maximum(largest, speed)
    step = courant / (jnp.max(largest, axis=(0, 1), keepdims=True) + 1e-06)

    def along(field, x, shift=0):
        halves = []
        for half in range(2):
            y = jnp.clip(128 * half + lane + shift, 0, 255) >> 2
            source = ((y >> 2) << 3) + (x >> 2)
            part = jnp.take_along_axis(wide_ref[field, x & 3], source, axis=1)
            for j in range(1, 4):
                part = jnp.where((y & 3) == j, jnp.take_along_axis(wide_ref[field, 4 * j + (x & 3)], source, axis=1), part)
            halves.append(part)
        return jnp.concatenate(halves, axis=1)

    xs = [jnp.clip(2 * device - 1 + j, 0, 31) for j in range(4)]
    speed_x = [along(0, x) for x in xs]
    speed_z = [along(2, x) for x in xs[1:3]]
    speed_y = [along(1, x) for x in xs[1:3]]
    north_y = [along(1, x, 1) for x in xs[1:3]]
    south_y = [along(1, x, -1) for x in xs[1:3]]

    layer, column = iotas((8, 256))
    crossed = device ^ jnp.where(even, device - 1, device + 1)
    halo = []
    for i in range(4):
        parts = []
        for half in range(2):
            place = 8 * (2 * i + half)
            here = 8 * (MAIN + 2) + place
            part = far_ref[here : here + 8, :]
            if i < 2:
                start = MAIN + SMALL + place
                straight = first_ref[start : start + 8, :]
                straight = jnp.where(odd, straight, second_ref[MAIN + start : MAIN + start + 8, :])
                part = jnp.where(crossed == 7, part, jnp.where(crossed == 15, near_ref[here : here + 8, :], 0.0))
                part = jnp.where(crossed == 3, straight, part)
            parts.append(part)
        halo.append(jnp.concatenate(parts, axis=1))
    cells = (
        [jnp.where(even, halo[j], halo[2 + j]) for j in range(2)]
        + [salt_ref[:, x, :] for x in range(8)]
        + [jnp.where(even, halo[2 + j], halo[j]) for j in range(2)]
    )
    diffs = [cells[i + 1] - cells[i] for i in range(11)]
    halves = [0.5 * slope_of(diffs[i], diffs[i + 1]) for i in range(10)]
    flux_x = []
    for f in range(9):
        if f % 4 == 0:
            face = 0.5 * (speed_x[f // 4] + speed_x[f // 4 + 1])
            if f == 0:
                face = jnp.where(device == 0, 0.0, face)
            if f == 8:
                face = jnp.where(device == 15, 0.0, face)
        else:
            face = speed_x[1 + f // 4]
        flux_x.append(face * jnp.where(face > 0, cells[f + 1] + halves[f], cells[f + 2] - halves[f + 1]))
    faces_z = [jnp.where(layer < 7, 0.5 * (v + pltpu.roll(v, 7, 0)), 0.0) for v in speed_z]
    faces_n = [jnp.where(column < 255, 0.5 * (v + beside), 0.0) for v, beside in zip(speed_y, north_y)]
    faces_s = [jnp.where(column > 0, 0.5 * (beside + v), 0.0) for v, beside in zip(speed_y, south_y)]
    for x in range(8):
        cell = cells[x + 2]
        ahead = jnp.where(layer < 7, pltpu.roll(cell, 7, 0), 0.0) - cell
        half = 0.5 * slope_of(jnp.where(layer > 0, pltpu.roll(ahead, 1, 0), cell), ahead)
        face = faces_z[x // 4]
        flux_z = face * jnp.where(face > 0, cell + half, pltpu.roll(cell - half, 7, 0))
        change = flux_z - pltpu.roll(flux_z, 1, 0)
        change = change + (flux_x[x + 1] - flux_x[x])
        ahead = jnp.where(column < 255, pltpu.roll(cell, 255, 1), 0.0) - cell
        half = 0.5 * slope_of(jnp.where(column > 0, pltpu.roll(ahead, 1, 1), cell), ahead)
        below, above = cell + half, cell - half
        face = faces_n[x // 4]
        flux_n = face * jnp.where(face > 0, below, pltpu.roll(above, 255, 1))
        face = faces_s[x // 4]
        flux_s = face * jnp.where(face > 0, pltpu.roll(below, 1, 1), above)
        change = change + (flux_n - flux_s)
        wet = recharge_ref[x : x + 1, :].astype(jnp.float32)
        dilution = jnp.where(layer == 0, freshening * wet * cell, 0.0)
        tendency_ref[:, x, :] = -step * change - step * dilution

def local_small(salt, recharge, conductivity, codes):
    vmem = pl.BlockSpec(memory_space=pltpu.VMEM)
    block, inner, relay = pl.pallas_call(
        pack_kernel,
        out_shape=(
            pltpu.VMEM((MAIN + SMALL + COLUMNS, 128), jnp.float32),
            pltpu.VMEM((COLUMNS, 128), jnp.float32),
            pltpu.VMEM((8, 128), jnp.float32),
        ),
        in_specs=[vmem] * 4,
        out_specs=(vmem,) * 3,
        scratch_shapes=[pltpu.VMEM((32, 128), jnp.float32), pltpu.VMEM((32, 128), jnp.float32)],
        name="pack",
    )(salt, recharge, conductivity, codes)

    def swapped(array, turn):
        pairs = [(i, i ^ ROUNDS[bin(i).count("1") % 2][turn]) for i in range(lax.axis_size("gx"))]
        return lax.ppermute(array, "gx", pairs)

    def small(array, count):
        return array[count * MAIN : count * MAIN + SMALL]

    def columns(array, count):
        return array[count * MAIN + SMALL :]

    relay = jnp.tile(relay, (COLUMNS // 8, 1))
    first = swapped(block, 0)
    handed = jnp.where(relay > 1.5, columns(block, 1), columns(first, 1))
    block = jnp.concatenate([block[:MAIN], first[:MAIN], small(block, 1) + small(first, 1), handed])
    second = swapped(block, 1)
    handed = jnp.where(relay > 0.5, columns(second, 2), columns(first, 1))
    block = jnp.concatenate(
        [block[: 2 * MAIN], second[: 2 * MAIN], small(block, 2) + small(second, 2), handed]
    )
    other = swapped(block, 2)
    block = jnp.concatenate(
        [block[: 4 * MAIN], other[: 4 * MAIN], small(block, 4), small(other, 4), columns(other, 4), inner]
    )
    other = swapped(block, 3)
    return pl.pallas_call(
        step_kernel,
        out_shape=(
            jax.ShapeDtypeStruct(salt.shape, jnp.float32),
            jax.ShapeDtypeStruct(conductivity.shape, jnp.float32),
        ),
        in_specs=[vmem] * 6,
        out_specs=(vmem,) * 2,
        scratch_shapes=[
            pltpu.VMEM((15, 16, 8, 128), jnp.float32),
            pltpu.VMEM((9, 4, 8, 128), jnp.float32),
            pltpu.VMEM((9, 8, 8, 128), jnp.float32),
            pltpu.VMEM((3, 16, 8, 128), jnp.float32),
        ],
        compiler_params=pltpu.CompilerParams(vmem_limit_bytes=16 * 1024 * 1024),
        name="step",
    )(block, other, first, second, salt, recharge)

def local(salt, recharge, conductivity, codes):
    small = (
        lax.axis_size("gx") == 16
        and salt.shape == (8, 8, 256)
        and recharge.shape == (8, 256)
        and conductivity.shape == (8, 4, 32)
        and codes.shape == (4, 32)
    )
    return (local_small if small else local_shared)(salt, recharge, conductivity, codes)

def solution(mesh):
    return jax.shard_map(
        local,
        mesh=mesh,
        in_specs=(
            P("parts", "gx", None),
            P("gx", "parts"),
            P("parts", "gx", None),
            P("gx", "parts"),
        ),
        out_specs=(P("parts", "gx", None), P("parts", "gx", None)),
        check_vma=False,
    )
```

```python
import jax
import jax.numpy as jnp
from jax import lax
from jax.experimental import pallas as pl
from jax.experimental.pallas import tpu as pltpu
from jax.sharding import PartitionSpec as P

CYCLES = 2
SMOOTH = 2
COARSE_SWEEPS = 6

relax_weight = 0.8
vertical_ratio = 0.5
sea_penalty = 2.0
river_penalty = 0.5
river_head = 1.0
recharge_rate = 1.0
courant = 0.45
freshening = 1.0

def padded_2(array, sides, width):
    for axis, dim in sides:
        count, length = (lax.axis_size(axis), array.shape[dim])
        up = [(i, (i + 1) % count) for i in range(count - 1)]
        down = [(j, i) for i, j in up]
        last = lax.slice_in_dim(array, length - width, length, axis=dim)
        first = lax.slice_in_dim(array, 0, width, axis=dim)
        before = lax.ppermute(last, axis, up)
        after = lax.ppermute(first, axis, down)
        array = jnp.concatenate([before, array, after], axis=dim)
    return array

def harmonic(first, second):
    total = first + second
    return 2.0 * first * second / (total + jnp.where(total > 0, 0.0, 1.0))

def coefficients(padded, penalty, vertical_scale):
    inner = padded[:, 1:-1, :]
    y_low = harmonic(inner, padded[:, :-2, :])
    y_high = harmonic(inner, padded[:, 2:, :])
    x_face = harmonic(inner[:, :, :-1], inner[:, :, 1:])
    zero_col = jnp.zeros_like(inner[:, :, :1])
    x_low = jnp.concatenate([zero_col, x_face], axis=2)
    x_high = jnp.concatenate([x_face, zero_col], axis=2)
    z_face = vertical_scale * vertical_ratio * harmonic(inner[:-1], inner[1:])
    zero_layer = jnp.zeros_like(inner[:1])
    z_up = jnp.concatenate([zero_layer, z_face], axis=0)
    z_down = jnp.concatenate([z_face, zero_layer], axis=0)
    top_term = jnp.concatenate([penalty[None], jnp.zeros_like(inner[1:])], axis=0)
    diagonal = x_low + x_high + y_low + y_high + z_up + z_down + top_term
    return (x_low, x_high, y_low, y_high, z_up, z_down, diagonal)

def neighbors(padded):
    center = padded[:, 1:-1, :]
    zero_col = jnp.zeros_like(center[:, :, :1])
    west = jnp.concatenate([zero_col, center[:, :, :-1]], axis=2)
    east = jnp.concatenate([center[:, :, 1:], zero_col], axis=2)
    zero_layer = jnp.zeros_like(center[:1])
    upper = jnp.concatenate([zero_layer, center[:-1]], axis=0)
    lower = jnp.concatenate([center[1:], zero_layer], axis=0)
    return (center, west, east, padded[:, :-2, :], padded[:, 2:, :], upper, lower)

def apply_operator(padded, coeffs):
    center, west, east, south, north, upper, lower = neighbors(padded)
    x_low, x_high, y_low, y_high, z_up, z_down, diagonal = coeffs
    return (
        diagonal * center
        - x_low * west
        - x_high * east
        - y_low * south
        - y_high * north
        - z_up * upper
        - z_down * lower
    )

def relax(padded, coeffs, right_side):
    return (
        padded[:, 1:-1, :]
        + relax_weight * (right_side - apply_operator(padded, coeffs)) / coeffs[6]
    )

def block_mean(field):
    leading = field.shape[:-2]
    count_a, count_b = field.shape[-2:]
    grouped = field.reshape(leading + (count_a // 4, 4, count_b // 4, 4))
    return jnp.sum(grouped, axis=(-3, -1)) * 0.0625

def pair_sum(field):
    leading = field.shape[:-2]
    count_a, count_b = field.shape[-2:]
    grouped = field.reshape(leading + (count_a // 2, 2, count_b // 2, 2))
    return jnp.sum(grouped, axis=(-3, -1))

def upsample(field, factor):
    return jnp.repeat(jnp.repeat(field, factor, axis=-2), factor, axis=-1)

def minmod(first, second):
    return 0.5 * (jnp.sign(first) + jnp.sign(second)) * jnp.minimum(jnp.abs(first), jnp.abs(second))

def portion(field, start, stop, axis):
    return lax.slice_in_dim(field, start, stop, axis=axis)

def divergence(cells, speed, axis):
    length = cells.shape[axis]
    widths = [(0, 0)] * cells.ndim
    widths[axis] = (1, 1)
    padded = jnp.pad(cells, widths)
    steps_diff = portion(padded, 1, length + 2, axis) - portion(padded, 0, length + 1, axis)
    slope = minmod(portion(steps_diff, 0, length, axis), portion(steps_diff, 1, length + 1, axis))
    faces = 0.5 * (portion(speed, 0, length - 1, axis) + portion(speed, 1, length, axis))
    left = portion(cells, 0, length - 1, axis) + 0.5 * portion(slope, 0, length - 1, axis)
    right = portion(cells, 1, length, axis) - 0.5 * portion(slope, 1, length, axis)
    flux = jnp.pad(faces * jnp.where(faces > 0, left, right), widths)
    return portion(flux, 1, length + 1, axis) - portion(flux, 0, length, axis)

def divergence_x(extended, faces):
    steps_diff = extended[:, 1:] - extended[:, :-1]
    slope = minmod(steps_diff[:, :-1], steps_diff[:, 1:])
    cells = extended[:, 1:-1]
    left = cells[:, :-1] + 0.5 * slope[:, :-1]
    right = cells[:, 1:] - 0.5 * slope[:, 1:]
    flux = faces * jnp.where(faces > 0, left, right)
    return flux[:, 1:] - flux[:, :-1]

def velocities(padded, coeffs, above, below):
    center, west, east, south, north, upper, lower = neighbors(padded)
    x_low, x_high, y_low, y_high, z_up, z_down, diagonal = coeffs
    vel_x = 0.5 * (x_low * (west - center) + x_high * (center - east))
    vel_y = 0.5 * (y_low * (south - center) + y_high * (center - north))
    vel_z = 0.5 * (z_up * (upper - center + above) + z_down * (center - lower + below))
    return (vel_z, vel_x, vel_y)

def buoyancy_terms(salt_coarse):
    face_salt = 0.5 * (salt_coarse[:-1] + salt_coarse[1:])
    zero_layer = jnp.zeros_like(salt_coarse[:1])
    above = jnp.concatenate([zero_layer, face_salt], axis=0)
    below = jnp.concatenate([face_salt, zero_layer], axis=0)
    return (above, below)

def boundary_penalty(codes):
    return jnp.where(codes == 1, sea_penalty, 0.0) + jnp.where(codes == 2, river_penalty, 0.0)

def source_terms(coeffs, above, below, recharge_frac, codes):
    top_source = recharge_rate * recharge_frac + river_head * jnp.where(
        codes == 2, river_penalty, 0.0
    )
    surface = jnp.concatenate([top_source[None], jnp.zeros_like(above[1:])], axis=0)
    return coeffs[4] * above - coeffs[5] * below + surface

def local_shared(salt, recharge, conductivity, codes):
    layers = salt.shape[0]
    tile = salt.shape[1]
    wet = recharge.astype(jnp.float32)
    blocks = jnp.concatenate([block_mean(salt), block_mean(wet)[None]], axis=0)
    owned = lax.all_to_all(
        jnp.transpose(blocks, (0, 2, 1)), "gx", split_axis=1, concat_axis=2, tiled=True
    )
    salt_coarse = owned[:layers]
    recharge_frac = owned[layers]
    penalty = boundary_penalty(codes)
    cond_padded = padded_2(conductivity, (("gx", 1),), 1)
    coeffs = coefficients(cond_padded, penalty, 1.0)
    above, below = buoyancy_terms(salt_coarse)
    right_side = source_terms(coeffs, above, below, recharge_frac, codes)
    coarse_cond = 0.25 * pair_sum(conductivity)
    coarse_pen = pair_sum(penalty)
    coarse_padded = padded_2(coarse_cond, (("gx", 1),), 1)
    coarse_coeffs = coefficients(coarse_padded, coarse_pen, 4.0)

    def smooth(current):
        padded = padded_2(current, (("gx", 1),), 1)
        return relax(padded, coeffs, right_side)

    head = jnp.zeros_like(conductivity)
    for cycle_no in range(CYCLES):
        for sweep in range(SMOOTH):
            head = smooth(head)
        head_padded = padded_2(head, (("gx", 1),), 1)
        residual = right_side - apply_operator(head_padded, coeffs)
        coarse_resid = pair_sum(residual)
        correction = jnp.zeros_like(coarse_resid)
        for sweep in range(COARSE_SWEEPS):
            corr_padded = padded_2(correction, (("gx", 1),), 1)
            correction = relax(corr_padded, coarse_coeffs, coarse_resid)
        head = head + upsample(correction, 2)
        for sweep in range(SMOOTH):
            head = smooth(head)
    final_padded = padded_2(head, (("gx", 1),), 1)
    vel_z, vel_x, vel_y = velocities(final_padded, coeffs, above, below)
    local_fastest = jnp.max(jnp.abs(vel_x) + jnp.abs(vel_y) + jnp.abs(vel_z))
    fastest = lax.pmax(local_fastest, "gx")
    step = courant / (fastest + 1e-06)
    packed = jnp.stack([vel_z, vel_x, vel_y])
    returned = jnp.transpose(
        lax.all_to_all(packed, "gx", split_axis=3, concat_axis=2, tiled=True), (0, 1, 3, 2)
    )
    fine_x = upsample(returned[1], 4)
    both = padded_2(jnp.stack([salt, fine_x]), (("gx", 2),), 2)
    extended = both[0]
    inner_x = both[1][:, 1:-1]
    faces = 0.5 * (inner_x[:, :-1] + inner_x[:, 1:])
    position = jnp.arange(tile + 1)
    device = lax.axis_index("gx")
    final_device = lax.axis_size("gx") - 1
    edge = (position == 0) & (device == 0) | (position == tile) & (device == final_device)
    faces = jnp.where(edge[None, :, None], 0.0, faces)
    fine_z = upsample(returned[0], 4)
    fine_y = upsample(returned[2], 4)
    change = (
        divergence(salt, fine_z, 0) + divergence_x(extended, faces) + divergence(salt, fine_y, 2)
    )
    dilution = jnp.concatenate(
        [(freshening * wet * salt[0])[None], jnp.zeros_like(salt[1:])], axis=0
    )
    tendency = -step * change - step * dilution
    return (tendency, head)

def split_dot(values, table, terms=3):
    rows = values.shape[0]
    parts = []
    for _ in range(terms):
        parts.append(values.astype(jnp.bfloat16))
        values = values - parts[-1].astype(jnp.float32)
    out = jnp.dot(jnp.concatenate(parts, axis=0), table, preferred_element_type=jnp.float32)
    return sum(out[rows * i : rows * (i + 1)] for i in range(1, terms)) + out[:rows]

def table_of(shape, same):
    row = lax.broadcasted_iota(jnp.int32, shape, 0)
    col = lax.broadcasted_iota(jnp.int32, shape, 1)
    return jnp.where(same(row, col), 1.0, 0.0).astype(jnp.bfloat16)

def iotas(shape):
    return lax.broadcasted_iota(jnp.int32, shape, 0), lax.broadcasted_iota(jnp.int32, shape, 1)

MAIN, SMALL, COLUMNS = 16, 8, 32
ROUNDS = ((9, 3, 5, 1), (3, 9, 5, 1))

def odd_ones(device):
    return ((device ^ (device >> 1) ^ (device >> 2) ^ (device >> 3)) & 1) == 1

def pack_kernel(salt_ref, recharge_ref, cond_ref, codes_ref, block_ref, inner_ref, relay_ref, flat_ref, turn_ref):
    device = lax.axis_index("gx")
    even = (device & 1) == 0
    for j in range(2):
        first = salt_ref[:, j, :]
        last = salt_ref[:, 6 + j, :]
        inward = jnp.where(even, last, first)
        outward = jnp.where(even, first, last)
        for half in range(2):
            place = 8 * (2 * j + half)
            inner_ref[place : place + 8, :] = inward[:, 128 * half : 128 * half + 128]
            place = place + MAIN + SMALL
            block_ref[place : place + 8, :] = outward[:, 128 * half : 128 * half + 128]
    relay = jnp.where(odd_ones(device), jnp.where((device == 2) | (device == 13), 1.0, 0.0), 2.0)
    relay_ref[...] = jnp.broadcast_to(relay, (8, 128))
    turned = device >> 1
    sums = table_of((256, 128), lambda r, c: (r >> 2) == ((c >> 3) << 2) + (((c - turned) & 7) >> 1))
    for i in range(8):
        four = salt_ref[i] + pltpu.roll(salt_ref[i], 7, 0)
        four = four + pltpu.roll(four, 6, 0)
        flat_ref[0, 8 * i : 8 * i + 8, :] = four[:, 0:128]
        flat_ref[1, 8 * i : 8 * i + 8, :] = four[:, 128:256]
    rows = [
        jnp.concatenate([flat_ref[half, pl.ds(start, 8, stride=8), :] for half in range(2)], axis=1) for start in (0, 4)
    ]
    means = split_dot(jnp.concatenate(rows, axis=0), sums) * 0.0625
    sub, lane = iotas((8, 128))
    mine = (sub >> 2) == ((lane - turned) & 1)
    block_ref[0:8, :] = jnp.where(((lane - turned) & 1) == 0, means[0:8], means[8:16])
    wet_y = jnp.dot(
        recharge_ref[...].astype(jnp.float32).astype(jnp.bfloat16), sums, preferred_element_type=jnp.float32
    )
    wet_row = jnp.sum(jnp.where(mine, wet_y, 0.0), axis=0, keepdims=True) * 0.0625
    for layer in range(8):
        turn_ref[4 * layer : 4 * layer + 4, 0:32] = cond_ref[layer]
    spread = table_of((32, 128), lambda r, c: r == ((c & 7) << 2) + (((c >> 3) - device) & 3))
    turn_ref[...] = split_dot(turn_ref[:, 0:32], spread)
    packed = jnp.zeros((8, 128), jnp.float32)
    for j in range(4):
        packed = jnp.where(((((lane >> 3) - device) & 15) >> 2) == j, turn_ref[pl.ds(j, 8, stride=4), :], packed)
    block_ref[8:16, :] = packed
    codes = codes_ref[...]
    penalty = jnp.where(codes == 1, sea_penalty, 0.0) + jnp.where(codes == 2, river_penalty, 0.0)
    penalty_x = jnp.dot(penalty.astype(jnp.bfloat16), spread, preferred_element_type=jnp.float32)
    row4, lane4 = iotas((4, 128))
    penalty_row = jnp.sum(jnp.where(row4 == ((((lane4 >> 3) - device) & 15) >> 2), penalty_x, 0.0), axis=0, keepdims=True)
    slot = (device & 2) + ((device & 8) >> 1)
    block_ref[16:24, :] = jnp.where(sub == slot, wet_row, jnp.where(sub == slot + 1, penalty_row, 0.0))

def harm(first, second):
    return 2.0 * first * second / (first + second)

def slope_of(back, ahead):
    return jnp.maximum(jnp.minimum(back, ahead), 0.0) + jnp.minimum(jnp.maximum(back, ahead), 0.0)

def east_of(cells, k, side):
    return cells[k + 1] if k % side < side - 1 else pltpu.roll(cells[k + 1 - side], 127, 1)

def west_of(cells, k, side):
    return cells[k - 1] if k % side > 0 else pltpu.roll(cells[k - 1 + side], 1, 1)

def north_of(cells, k, side):
    return cells[k + side] if k < side * (side - 1) else pltpu.roll(cells[k % side], 120, 1)

def south_of(cells, k, side):
    return cells[k - side] if k >= side else pltpu.roll(cells[k + side * (side - 1)], 8, 1)

def upper_of(cell):
    return pltpu.roll(cell, 1, 0)

def lower_of(cell):
    return pltpu.roll(cell, 7, 0)

def step_kernel(
    near_ref, far_ref, first_ref, second_ref, salt_ref, recharge_ref, tendency_ref, head_ref, fine_ref, coarse_ref, ring_ref, wide_ref
):
    device = lax.axis_index("gx")
    sub, lane = iotas((8, 128))
    top = sub == 0
    even = (device & 1) == 0
    odd = odd_ones(device)
    orders = [lambda e: ((e >> 3) & 1) + (e & 2) + (e & 4), lambda e: ((e >> 1) & 1) + ((e & 8) >> 2) + (e & 4)]
    here = jnp.where(odd, orders[1](device), orders[0](device))
    there = jnp.where(odd, orders[0](device), orders[1](device))
    flip = (device & 4) != 0
    small = []
    for ref in (near_ref, far_ref):
        halves = [ref[8 * MAIN + SMALL * i : 8 * MAIN + SMALL * (i + 1), :] for i in range(2)]
        small.append([jnp.where(flip, halves[1 - i], halves[i]) for i in range(2)])
    means, conds, smalls = [], [], []
    for e in range(16):
        mine = odd == (bin(e).count("1") % 2 == 1)
        if e % 2 == 0:
            start = pl.multiple_of((here ^ jnp.where(odd, orders[1](e), orders[0](e))) * MAIN, 8)
            near = [near_ref[pl.ds(start, 8), :], near_ref[pl.ds(pl.multiple_of(start + 8, 8), 8), :]]
            start = pl.multiple_of((there ^ jnp.where(odd, orders[0](e), orders[1](e))) * MAIN, 8)
            far = [far_ref[pl.ds(start, 8), :], far_ref[pl.ds(pl.multiple_of(start + 8, 8), 8), :]]
        means.append(jnp.where(mine, near[0], far[0]))
        conds.append(jnp.where(mine, near[1], far[1]))
        smalls.append(jnp.where(mine, small[0][(e >> 2) & 1], small[1][(e >> 2) & 1]))

    slots = [2 * ((e // 2) % 2) + 4 * (e // 8) for e in range(16)]
    wets = [smalls[e][slots[e] : slots[e] + 1] for e in range(16)]
    penalties = [smalls[e][slots[e] + 1 : slots[e] + 2] for e in range(16)]

    def diagonals(fields, index):
        count = len(fields)
        bit = 1
        while bit < count:
            high = (index & bit) != 0
            fields = [jnp.where(high, fields[(m + bit) % count], fields[m]) for m in range(count)]
            bit *= 2
        return fields

    def by_block(fields):
        group = lane[0 : fields[0].shape[0]] >> 3
        picked = diagonals(fields, group)
        return [pltpu.roll(picked[-k % 16], (128 - 8 * k) % 128, 1) for k in range(16)]

    def by_lane(fields):
        within = lane & 7
        out = []
        picked = diagonals(fields, within)
        for s in range(8):
            here = picked[-s % 8]
            if s > 0:
                here = jnp.where(within < 8 - s, pltpu.roll(here, 128 - s, 1), pltpu.roll(here, 8 - s, 1))
            out.append(here)
        return out

    cond = by_block(conds)
    penalties = by_block(penalties)
    salt = [None] * 16
    wet_frac = [None] * 16
    wet_pairs = by_lane([jnp.where(top, wets[2 * b], wets[2 * b + 1]) for b in range(8)])
    for half in range(2):
        columns = by_lane(means[half::2])
        for s in range(8):
            k = 4 * (s // 2) + 2 * half + s % 2
            salt[k] = columns[s]
            wet_frac[k] = wet_pairs[s] if half == 0 else lower_of(wet_pairs[s])

    def coefficients(cells, penalty, side, vertical, weight_ref):
        face_w, face_e, face_s, face_n, face_d = [], [], [], [], []
        for k in range(side * side):
            e = harm(cells[k], east_of(cells, k, side))
            if k % side == side - 1:
                e = jnp.where((lane & 7) < 7, e, 0.0)
            n = harm(cells[k], north_of(cells, k, side))
            if k >= side * (side - 1):
                n = jnp.where(lane < 120, n, 0.0)
            w = face_e[k - 1] if k % side > 0 else None
            if w is None:
                w = jnp.where((lane & 7) > 0, harm(west_of(cells, k, side), cells[k]), 0.0)
            s = face_n[k - side] if k >= side else None
            if s is None:
                s = jnp.where(lane >= 8, harm(south_of(cells, k, side), cells[k]), 0.0)
            face_w.append(w)
            face_e.append(e)
            face_s.append(s)
            face_n.append(n)
            face_d.append(jnp.where(sub < 7, vertical * harm(cells[k], lower_of(cells[k])), 0.0))
        weights = []
        for k in range(side * side):
            six = (face_w[k], face_e[k], face_s[k], face_n[k], upper_of(face_d[k]), face_d[k])
            diag = six[0] + six[1] + six[2] + six[3] + six[4] + six[5] + penalty[k]
            weight = relax_weight / diag
            for number, face in enumerate(six):
                weight_ref[number, k] = weight * face
            weight_ref[6, k] = diag * (1.0 / relax_weight)
            weight_ref[7, k] = weight
            weights.append(weight)
        return (face_w, face_e, face_s, face_n, face_d), weights

    def relaxed(cells, side, weight_ref):
        out = []
        for k in range(side * side):
            here = cells[k]
            pairs = (
                west_of(cells, k, side),
                east_of(cells, k, side),
                south_of(cells, k, side),
                north_of(cells, k, side),
                upper_of(here),
                lower_of(here),
            )
            terms = [weight_ref[number, k] * pair for number, pair in enumerate(pairs)]
            base = (1.0 - relax_weight) * here + weight_ref[8, k]
            out.append(((terms[0] + terms[1]) + (terms[2] + terms[3])) + ((terms[4] + terms[5]) + base))
        return out

    ring = [(j, i) for j in range(-1, 3) for i in range(-1, 3) if (j in (0, 1)) != (i in (0, 1))]

    def beyond(cells, j, i):
        shift = -(8 * (j // 2) + i // 2) % 128
        cell = cells[2 * (j % 2) + i % 2]
        return pltpu.roll(cell, shift, 1) if shift else cell

    def relaxed_twice(cells):
        def step(at, j, i, weights):
            here = at(j, i)
            pairs = (at(j, i - 1), at(j, i + 1), at(j - 1, i), at(j + 1, i), upper_of(here), lower_of(here))
            terms = [weights(number) * pair for number, pair in enumerate(pairs)]
            base = (1.0 - relax_weight) * here + weights(8)
            return ((terms[0] + terms[1]) + (terms[2] + terms[3])) + ((terms[4] + terms[5]) + base)

        old, new = {}, {}

        def at_old(j, i):
            if (j, i) not in old:
                old[j, i] = beyond(cells, j, i)
            return old[j, i]

        for q, (j, i) in enumerate(ring):
            new[j, i] = step(at_old, j, i, lambda number, q=q: ring_ref[number, q])
        for k in range(4):
            new[k // 2, k % 2] = step(at_old, k // 2, k % 2, lambda number, k=k: coarse_ref[number, k])
        return [
            step(lambda j, i: new[j, i], k // 2, k % 2, lambda number, k=k: coarse_ref[number, k]) for k in range(4)
        ]

    def pair_sums(cells):
        return [(cells[k] + cells[k + 1]) + (cells[k + 4] + cells[k + 5]) for k in (0, 2, 8, 10)]

    penalty, river = [], []
    for k in range(16):
        penalty.append(jnp.where(top, penalties[k], 0.0))
        river.append(jnp.where(penalties[k] == river_penalty, river_penalty, 0.0))
    faces, weights = coefficients(cond, penalty, 4, vertical_ratio, fine_ref)
    for k in range(16):
        below = jnp.where(sub < 7, 0.5 * (salt[k] + lower_of(salt[k])), 0.0)
        pull = faces[4][k] * below
        source = jnp.where(top, recharge_rate * wet_frac[k] + river_head * river[k], 0.0)
        fine_ref[8, k] = weights[k] * (upper_of(pull) - pull + source)
        fine_ref[9, k] = below
        for number, face in enumerate(faces):
            fine_ref[10 + number, k] = face[k]
    coefficients([0.25 * c for c in pair_sums(cond)], pair_sums(penalty), 2, 4.0 * vertical_ratio, coarse_ref)
    for number in range(6):
        cells = [coarse_ref[number, k] for k in range(4)]
        for q, (j, i) in enumerate(ring):
            ring_ref[number, q] = beyond(cells, j, i)

    head = None
    for cycle_no in range(CYCLES):
        for sweep in range(SMOOTH):
            head = [fine_ref[8, k] for k in range(16)] if head is None else relaxed(head, 4, fine_ref)
        ahead = relaxed(head, 4, fine_ref)
        resid = pair_sums([(ahead[k] - head[k]) * fine_ref[6, k] for k in range(16)])
        correction = []
        for k in range(4):
            correction.append(coarse_ref[7, k] * resid[k])
            coarse_ref[8, k] = correction[k]
        for q, (j, i) in enumerate(ring):
            ring_ref[8, q] = beyond(correction, j, i)
        for sweep in range((COARSE_SWEEPS - 1) // 2):
            correction = relaxed_twice(correction)
        for sweep in range((COARSE_SWEEPS - 1) % 2):
            correction = relaxed(correction, 2, coarse_ref)
        head = [head[k] + correction[2 * (k // 8) + (k % 4) // 2] for k in range(16)]
        for sweep in range(SMOOTH):
            head = relaxed(head, 4, fine_ref)

    largest = None
    for k in range(16):
        here = head[k]
        west, east = west_of(head, k, 4) - here, here - east_of(head, k, 4)
        south, north = south_of(head, k, 4) - here, here - north_of(head, k, 4)
        vel_x = 0.5 * (fine_ref[10, k] * west + fine_ref[11, k] * east)
        vel_y = 0.5 * (fine_ref[12, k] * south + fine_ref[13, k] * north)
        flow_d = fine_ref[14, k] * (here - lower_of(here) + fine_ref[9, k])
        vel_z = 0.5 * (upper_of(flow_d) + flow_d)
        wide_ref[0, k] = vel_x
        wide_ref[1, k] = vel_y
        wide_ref[2, k] = vel_z
        speed = jnp.abs(vel_x) + jnp.abs(vel_y) + jnp.abs(vel_z)
        largest = speed if largest is None else jnp.maximum(largest, speed)
    step = courant / (jnp.max(largest, axis=(0, 1), keepdims=True) + 1e-06)

    def along(field, x, beside=False):
        halves = []
        for half in range(2):
            y = 128 * half + lane
            if beside:
                y = jnp.clip(y + jnp.where((lane & 3) == 3, 1, jnp.where((lane & 3) == 0, -1, 0)), 0, 255)
            y = y >> 2
            source = ((y >> 2) << 3) + (x >> 2)
            part = jnp.take_along_axis(wide_ref[field, x & 3], source, axis=1)
            for j in range(1, 4):
                part = jnp.where((y & 3) == j, jnp.take_along_axis(wide_ref[field, 4 * j + (x & 3)], source, axis=1), part)
            halves.append(part)
        return jnp.concatenate(halves, axis=1)

    xs = [jnp.clip(2 * device - 1 + j, 0, 31) for j in range(4)]
    speed_x = [along(0, x) for x in xs]
    speed_z = [along(2, x) for x in xs[1:3]]
    speed_y = [along(1, x) for x in xs[1:3]]
    beside_y = [along(1, x, True) for x in xs[1:3]]

    layer, column = iotas((8, 256))
    crossed = device ^ jnp.where(even, device - 1, device + 1)
    halo = []
    for i in range(4):
        parts = []
        for half in range(2):
            place = 8 * (2 * i + half)
            here = 8 * (MAIN + 2) + place
            part = far_ref[here : here + 8, :]
            if i < 2:
                start = MAIN + SMALL + place
                straight = first_ref[start : start + 8, :]
                straight = jnp.where(odd, straight, second_ref[MAIN + start : MAIN + start + 8, :])
                part = jnp.where(crossed == 7, part, jnp.where(crossed == 15, near_ref[here : here + 8, :], 0.0))
                part = jnp.where(crossed == 3, straight, part)
            parts.append(part)
        halo.append(jnp.concatenate(parts, axis=1))
    cells = (
        [jnp.where(even, halo[j], halo[2 + j]) for j in range(2)]
        + [salt_ref[:, x, :] for x in range(8)]
        + [jnp.where(even, halo[2 + j], halo[j]) for j in range(2)]
    )
    diffs = [cells[i + 1] - cells[i] for i in range(11)]
    halves = [0.5 * slope_of(diffs[i], diffs[i + 1]) for i in range(10)]
    flux_x = []
    for f in range(9):
        if f % 4 == 0:
            face = 0.5 * (speed_x[f // 4] + speed_x[f // 4 + 1])
            if f == 0:
                face = jnp.where(device == 0, 0.0, face)
            if f == 8:
                face = jnp.where(device == 15, 0.0, face)
        else:
            face = speed_x[1 + f // 4]
        flux_x.append(face * jnp.where(face > 0, cells[f + 1] + halves[f], cells[f + 2] - halves[f + 1]))
    faces_z = [jnp.where(layer < 7, 0.5 * (v + pltpu.roll(v, 7, 0)), 0.0) for v in speed_z]
    between = [0.5 * (v + beside) for v, beside in zip(speed_y, beside_y)]
    faces_n = [jnp.where((column & 3) == 3, b, v) for v, b in zip(speed_y, between)]
    faces_n = [jnp.where(column < 255, face, 0.0) for face in faces_n]
    faces_s = [jnp.where((column & 3) == 0, b, v) for v, b in zip(speed_y, between)]
    faces_s = [jnp.where(column > 0, face, 0.0) for face in faces_s]
    for x in range(8):
        cell = cells[x + 2]
        ahead = jnp.where(layer < 7, pltpu.roll(cell, 7, 0), 0.0) - cell
        half = 0.5 * slope_of(jnp.where(layer > 0, pltpu.roll(ahead, 1, 0), cell), ahead)
        face = faces_z[x // 4]
        flux_z = face * jnp.where(face > 0, cell + half, pltpu.roll(cell - half, 7, 0))
        change = flux_z - pltpu.roll(flux_z, 1, 0)
        change = change + (flux_x[x + 1] - flux_x[x])
        ahead = jnp.where(column < 255, pltpu.roll(cell, 255, 1), 0.0) - cell
        half = 0.5 * slope_of(jnp.where(column > 0, pltpu.roll(ahead, 1, 1), cell), ahead)
        below, above = cell + half, cell - half
        face = faces_n[x // 4]
        flux_n = face * jnp.where(face > 0, below, pltpu.roll(above, 255, 1))
        face = faces_s[x // 4]
        flux_s = face * jnp.where(face > 0, pltpu.roll(below, 1, 1), above)
        change = change + (flux_n - flux_s)
        wet = recharge_ref[x : x + 1, :].astype(jnp.float32)
        dilution = jnp.where(layer == 0, freshening * wet * cell, 0.0)
        tendency_ref[:, x, :] = -step * change - step * dilution

    own = 8 * device + ((lane & 31) >> 2)
    for j in range(4):
        row = jnp.take_along_axis(head[4 * j], own, axis=1)
        for i in range(1, 4):
            row = jnp.where((lane & 3) == i, jnp.take_along_axis(head[4 * j + i], own, axis=1), row)
        head_ref[:, j, :] = row[:, 0:32]

def local_small(salt, recharge, conductivity, codes):
    vmem = pl.BlockSpec(memory_space=pltpu.VMEM)
    block, inner, relay = pl.pallas_call(
        pack_kernel,
        out_shape=(
            pltpu.VMEM((MAIN + SMALL + COLUMNS, 128), jnp.float32),
            pltpu.VMEM((COLUMNS, 128), jnp.float32),
            pltpu.VMEM((8, 128), jnp.float32),
        ),
        in_specs=[vmem] * 4,
        out_specs=(vmem,) * 3,
        scratch_shapes=[pltpu.VMEM((2, 64, 128), jnp.float32), pltpu.VMEM((32, 128), jnp.float32)],
        name="pack",
    )(salt, recharge, conductivity, codes)

    def swapped(array, turn):
        pairs = [(i, i ^ ROUNDS[bin(i).count("1") % 2][turn]) for i in range(lax.axis_size("gx"))]
        return lax.ppermute(array, "gx", pairs)

    def small(array, count):
        return array[count * MAIN : count * MAIN + SMALL]

    def columns(array, count):
        return array[count * MAIN + SMALL :]

    relay = jnp.tile(relay, (COLUMNS // 8, 1))
    first = swapped(block, 0)
    handed = jnp.where(relay > 1.5, columns(block, 1), columns(first, 1))
    block = jnp.concatenate([block[:MAIN], first[:MAIN], small(block, 1) + small(first, 1), handed])
    second = swapped(block, 1)
    handed = jnp.where(relay > 0.5, columns(second, 2), columns(first, 1))
    block = jnp.concatenate(
        [block[: 2 * MAIN], second[: 2 * MAIN], small(block, 2) + small(second, 2), handed]
    )
    other = swapped(block, 2)
    block = jnp.concatenate(
        [block[: 4 * MAIN], other[: 4 * MAIN], small(block, 4), small(other, 4), columns(other, 4), inner]
    )
    other = swapped(block, 3)
    return pl.pallas_call(
        step_kernel,
        out_shape=(
            jax.ShapeDtypeStruct(salt.shape, jnp.float32),
            jax.ShapeDtypeStruct(conductivity.shape, jnp.float32),
        ),
        in_specs=[vmem] * 6,
        out_specs=(vmem,) * 2,
        scratch_shapes=[
            pltpu.VMEM((15, 16, 8, 128), jnp.float32),
            pltpu.VMEM((9, 4, 8, 128), jnp.float32),
            pltpu.VMEM((9, 8, 8, 128), jnp.float32),
            pltpu.VMEM((3, 16, 8, 128), jnp.float32),
        ],
        compiler_params=pltpu.CompilerParams(vmem_limit_bytes=16 * 1024 * 1024),
        name="step",
    )(block, other, first, second, salt, recharge)

def local(salt, recharge, conductivity, codes):
    small = (
        lax.axis_size("gx") == 16
        and salt.shape == (8, 8, 256)
        and recharge.shape == (8, 256)
        and conductivity.shape == (8, 4, 32)
        and codes.shape == (4, 32)
    )
    return (local_small if small else local_shared)(salt, recharge, conductivity, codes)

def solution(mesh):
    return jax.shard_map(
        local,
        mesh=mesh,
        in_specs=(
            P("parts", "gx", None),
            P("gx", "parts"),
            P("parts", "gx", None),
            P("gx", "parts"),
        ),
        out_specs=(P("parts", "gx", None), P("parts", "gx", None)),
        check_vma=False,
    )
```

```python
import jax
import jax.numpy as jnp
from jax import lax
from jax.experimental import pallas as pl
from jax.experimental.pallas import tpu as pltpu
from jax.sharding import PartitionSpec as P

CYCLES = 2
SMOOTH = 2
COARSE_SWEEPS = 6

relax_weight = 0.8
vertical_ratio = 0.5
sea_penalty = 2.0
river_penalty = 0.5
river_head = 1.0
recharge_rate = 1.0
courant = 0.45
freshening = 1.0

def padded_2(array, sides, width):
    for axis, dim in sides:
        count, length = (lax.axis_size(axis), array.shape[dim])
        up = [(i, (i + 1) % count) for i in range(count - 1)]
        down = [(j, i) for i, j in up]
        last = lax.slice_in_dim(array, length - width, length, axis=dim)
        first = lax.slice_in_dim(array, 0, width, axis=dim)
        before = lax.ppermute(last, axis, up)
        after = lax.ppermute(first, axis, down)
        array = jnp.concatenate([before, array, after], axis=dim)
    return array

def harmonic(first, second):
    total = first + second
    return 2.0 * first * second / (total + jnp.where(total > 0, 0.0, 1.0))

def coefficients(padded, penalty, vertical_scale):
    inner = padded[:, 1:-1, :]
    y_low = harmonic(inner, padded[:, :-2, :])
    y_high = harmonic(inner, padded[:, 2:, :])
    x_face = harmonic(inner[:, :, :-1], inner[:, :, 1:])
    zero_col = jnp.zeros_like(inner[:, :, :1])
    x_low = jnp.concatenate([zero_col, x_face], axis=2)
    x_high = jnp.concatenate([x_face, zero_col], axis=2)
    z_face = vertical_scale * vertical_ratio * harmonic(inner[:-1], inner[1:])
    zero_layer = jnp.zeros_like(inner[:1])
    z_up = jnp.concatenate([zero_layer, z_face], axis=0)
    z_down = jnp.concatenate([z_face, zero_layer], axis=0)
    top_term = jnp.concatenate([penalty[None], jnp.zeros_like(inner[1:])], axis=0)
    diagonal = x_low + x_high + y_low + y_high + z_up + z_down + top_term
    return (x_low, x_high, y_low, y_high, z_up, z_down, diagonal)

def neighbors(padded):
    center = padded[:, 1:-1, :]
    zero_col = jnp.zeros_like(center[:, :, :1])
    west = jnp.concatenate([zero_col, center[:, :, :-1]], axis=2)
    east = jnp.concatenate([center[:, :, 1:], zero_col], axis=2)
    zero_layer = jnp.zeros_like(center[:1])
    upper = jnp.concatenate([zero_layer, center[:-1]], axis=0)
    lower = jnp.concatenate([center[1:], zero_layer], axis=0)
    return (center, west, east, padded[:, :-2, :], padded[:, 2:, :], upper, lower)

def apply_operator(padded, coeffs):
    center, west, east, south, north, upper, lower = neighbors(padded)
    x_low, x_high, y_low, y_high, z_up, z_down, diagonal = coeffs
    return (
        diagonal * center
        - x_low * west
        - x_high * east
        - y_low * south
        - y_high * north
        - z_up * upper
        - z_down * lower
    )

def relax(padded, coeffs, right_side):
    return (
        padded[:, 1:-1, :]
        + relax_weight * (right_side - apply_operator(padded, coeffs)) / coeffs[6]
    )

def block_mean(field):
    leading = field.shape[:-2]
    count_a, count_b = field.shape[-2:]
    grouped = field.reshape(leading + (count_a // 4, 4, count_b // 4, 4))
    return jnp.sum(grouped, axis=(-3, -1)) * 0.0625

def pair_sum(field):
    leading = field.shape[:-2]
    count_a, count_b = field.shape[-2:]
    grouped = field.reshape(leading + (count_a // 2, 2, count_b // 2, 2))
    return jnp.sum(grouped, axis=(-3, -1))

def upsample(field, factor):
    return jnp.repeat(jnp.repeat(field, factor, axis=-2), factor, axis=-1)

def minmod(first, second):
    return 0.5 * (jnp.sign(first) + jnp.sign(second)) * jnp.minimum(jnp.abs(first), jnp.abs(second))

def portion(field, start, stop, axis):
    return lax.slice_in_dim(field, start, stop, axis=axis)

def divergence(cells, speed, axis):
    length = cells.shape[axis]
    widths = [(0, 0)] * cells.ndim
    widths[axis] = (1, 1)
    padded = jnp.pad(cells, widths)
    steps_diff = portion(padded, 1, length + 2, axis) - portion(padded, 0, length + 1, axis)
    slope = minmod(portion(steps_diff, 0, length, axis), portion(steps_diff, 1, length + 1, axis))
    faces = 0.5 * (portion(speed, 0, length - 1, axis) + portion(speed, 1, length, axis))
    left = portion(cells, 0, length - 1, axis) + 0.5 * portion(slope, 0, length - 1, axis)
    right = portion(cells, 1, length, axis) - 0.5 * portion(slope, 1, length, axis)
    flux = jnp.pad(faces * jnp.where(faces > 0, left, right), widths)
    return portion(flux, 1, length + 1, axis) - portion(flux, 0, length, axis)

def divergence_x(extended, faces):
    steps_diff = extended[:, 1:] - extended[:, :-1]
    slope = minmod(steps_diff[:, :-1], steps_diff[:, 1:])
    cells = extended[:, 1:-1]
    left = cells[:, :-1] + 0.5 * slope[:, :-1]
    right = cells[:, 1:] - 0.5 * slope[:, 1:]
    flux = faces * jnp.where(faces > 0, left, right)
    return flux[:, 1:] - flux[:, :-1]

def velocities(padded, coeffs, above, below):
    center, west, east, south, north, upper, lower = neighbors(padded)
    x_low, x_high, y_low, y_high, z_up, z_down, diagonal = coeffs
    vel_x = 0.5 * (x_low * (west - center) + x_high * (center - east))
    vel_y = 0.5 * (y_low * (south - center) + y_high * (center - north))
    vel_z = 0.5 * (z_up * (upper - center + above) + z_down * (center - lower + below))
    return (vel_z, vel_x, vel_y)

def buoyancy_terms(salt_coarse):
    face_salt = 0.5 * (salt_coarse[:-1] + salt_coarse[1:])
    zero_layer = jnp.zeros_like(salt_coarse[:1])
    above = jnp.concatenate([zero_layer, face_salt], axis=0)
    below = jnp.concatenate([face_salt, zero_layer], axis=0)
    return (above, below)

def boundary_penalty(codes):
    return jnp.where(codes == 1, sea_penalty, 0.0) + jnp.where(codes == 2, river_penalty, 0.0)

def source_terms(coeffs, above, below, recharge_frac, codes):
    top_source = recharge_rate * recharge_frac + river_head * jnp.where(
        codes == 2, river_penalty, 0.0
    )
    surface = jnp.concatenate([top_source[None], jnp.zeros_like(above[1:])], axis=0)
    return coeffs[4] * above - coeffs[5] * below + surface

def local_shared(salt, recharge, conductivity, codes):
    layers = salt.shape[0]
    tile = salt.shape[1]
    wet = recharge.astype(jnp.float32)
    blocks = jnp.concatenate([block_mean(salt), block_mean(wet)[None]], axis=0)
    owned = lax.all_to_all(
        jnp.transpose(blocks, (0, 2, 1)), "gx", split_axis=1, concat_axis=2, tiled=True
    )
    salt_coarse = owned[:layers]
    recharge_frac = owned[layers]
    penalty = boundary_penalty(codes)
    cond_padded = padded_2(conductivity, (("gx", 1),), 1)
    coeffs = coefficients(cond_padded, penalty, 1.0)
    above, below = buoyancy_terms(salt_coarse)
    right_side = source_terms(coeffs, above, below, recharge_frac, codes)
    coarse_cond = 0.25 * pair_sum(conductivity)
    coarse_pen = pair_sum(penalty)
    coarse_padded = padded_2(coarse_cond, (("gx", 1),), 1)
    coarse_coeffs = coefficients(coarse_padded, coarse_pen, 4.0)

    def smooth(current):
        padded = padded_2(current, (("gx", 1),), 1)
        return relax(padded, coeffs, right_side)

    head = jnp.zeros_like(conductivity)
    for cycle_no in range(CYCLES):
        for sweep in range(SMOOTH):
            head = smooth(head)
        head_padded = padded_2(head, (("gx", 1),), 1)
        residual = right_side - apply_operator(head_padded, coeffs)
        coarse_resid = pair_sum(residual)
        correction = jnp.zeros_like(coarse_resid)
        for sweep in range(COARSE_SWEEPS):
            corr_padded = padded_2(correction, (("gx", 1),), 1)
            correction = relax(corr_padded, coarse_coeffs, coarse_resid)
        head = head + upsample(correction, 2)
        for sweep in range(SMOOTH):
            head = smooth(head)
    final_padded = padded_2(head, (("gx", 1),), 1)
    vel_z, vel_x, vel_y = velocities(final_padded, coeffs, above, below)
    local_fastest = jnp.max(jnp.abs(vel_x) + jnp.abs(vel_y) + jnp.abs(vel_z))
    fastest = lax.pmax(local_fastest, "gx")
    step = courant / (fastest + 1e-06)
    packed = jnp.stack([vel_z, vel_x, vel_y])
    returned = jnp.transpose(
        lax.all_to_all(packed, "gx", split_axis=3, concat_axis=2, tiled=True), (0, 1, 3, 2)
    )
    fine_x = upsample(returned[1], 4)
    both = padded_2(jnp.stack([salt, fine_x]), (("gx", 2),), 2)
    extended = both[0]
    inner_x = both[1][:, 1:-1]
    faces = 0.5 * (inner_x[:, :-1] + inner_x[:, 1:])
    position = jnp.arange(tile + 1)
    device = lax.axis_index("gx")
    final_device = lax.axis_size("gx") - 1
    edge = (position == 0) & (device == 0) | (position == tile) & (device == final_device)
    faces = jnp.where(edge[None, :, None], 0.0, faces)
    fine_z = upsample(returned[0], 4)
    fine_y = upsample(returned[2], 4)
    change = (
        divergence(salt, fine_z, 0) + divergence_x(extended, faces) + divergence(salt, fine_y, 2)
    )
    dilution = jnp.concatenate(
        [(freshening * wet * salt[0])[None], jnp.zeros_like(salt[1:])], axis=0
    )
    tendency = -step * change - step * dilution
    return (tendency, head)

def split_dot(values, table, terms=3):
    rows = values.shape[0]
    parts = []
    for _ in range(terms):
        parts.append(values.astype(jnp.bfloat16))
        values = values - parts[-1].astype(jnp.float32)
    out = jnp.dot(jnp.concatenate(parts, axis=0), table, preferred_element_type=jnp.float32)
    return sum(out[rows * i : rows * (i + 1)] for i in range(1, terms)) + out[:rows]

def table_of(shape, same):
    row = lax.broadcasted_iota(jnp.int32, shape, 0)
    col = lax.broadcasted_iota(jnp.int32, shape, 1)
    return jnp.where(same(row, col), 1.0, 0.0).astype(jnp.bfloat16)

def iotas(shape):
    return lax.broadcasted_iota(jnp.int32, shape, 0), lax.broadcasted_iota(jnp.int32, shape, 1)

MAIN, SMALL, COLUMNS = 16, 8, 32
ROUNDS = ((9, 3, 5, 1), (3, 9, 5, 1))

def odd_ones(device):
    return ((device ^ (device >> 1) ^ (device >> 2) ^ (device >> 3)) & 1) == 1

def pack_kernel(salt_ref, recharge_ref, cond_ref, codes_ref, block_ref, inner_ref, relay_ref, flat_ref, turn_ref):
    device = lax.axis_index("gx")
    even = (device & 1) == 0
    for j in range(2):
        first = salt_ref[:, j, :]
        last = salt_ref[:, 6 + j, :]
        inward = jnp.where(even, last, first)
        outward = jnp.where(even, first, last)
        for half in range(2):
            place = 8 * (2 * j + half)
            inner_ref[place : place + 8, :] = inward[:, 128 * half : 128 * half + 128]
            place = place + MAIN + SMALL
            block_ref[place : place + 8, :] = outward[:, 128 * half : 128 * half + 128]
    relay = jnp.where(odd_ones(device), jnp.where((device == 2) | (device == 13), 1.0, 0.0), 2.0)
    relay_ref[...] = jnp.broadcast_to(relay, (8, 128))
    turned = device >> 1
    sums = table_of((256, 128), lambda r, c: (r >> 2) == ((c >> 3) << 2) + (((c - turned) & 7) >> 1))
    for i in range(8):
        four = salt_ref[i] + pltpu.roll(salt_ref[i], 7, 0)
        four = four + pltpu.roll(four, 6, 0)
        flat_ref[0, 8 * i : 8 * i + 8, :] = four[:, 0:128]
        flat_ref[1, 8 * i : 8 * i + 8, :] = four[:, 128:256]
    rows = [
        jnp.concatenate([flat_ref[half, pl.ds(start, 8, stride=8), :] for half in range(2)], axis=1) for start in (0, 4)
    ]
    means = split_dot(jnp.concatenate(rows, axis=0), sums) * 0.0625
    sub, lane = iotas((8, 128))
    mine = (sub >> 2) == ((lane - turned) & 1)
    block_ref[0:8, :] = jnp.where(((lane - turned) & 1) == 0, means[0:8], means[8:16])
    wet_y = jnp.dot(
        recharge_ref[...].astype(jnp.float32).astype(jnp.bfloat16), sums, preferred_element_type=jnp.float32
    )
    wet_row = jnp.sum(jnp.where(mine, wet_y, 0.0), axis=0, keepdims=True) * 0.0625
    for layer in range(8):
        turn_ref[4 * layer : 4 * layer + 4, 0:32] = cond_ref[layer]
    spread = table_of((32, 128), lambda r, c: r == ((c & 7) << 2) + (((c >> 3) - device) & 3))
    turn_ref[...] = split_dot(turn_ref[:, 0:32], spread)
    packed = jnp.zeros((8, 128), jnp.float32)
    for j in range(4):
        packed = jnp.where(((((lane >> 3) - device) & 15) >> 2) == j, turn_ref[pl.ds(j, 8, stride=4), :], packed)
    block_ref[8:16, :] = packed
    codes = codes_ref[...]
    penalty = jnp.where(codes == 1, sea_penalty, 0.0) + jnp.where(codes == 2, river_penalty, 0.0)
    penalty_x = jnp.dot(penalty.astype(jnp.bfloat16), spread, preferred_element_type=jnp.float32)
    row4, lane4 = iotas((4, 128))
    penalty_row = jnp.sum(jnp.where(row4 == ((((lane4 >> 3) - device) & 15) >> 2), penalty_x, 0.0), axis=0, keepdims=True)
    slot = (device & 2) + ((device & 8) >> 1)
    block_ref[16:24, :] = jnp.where(sub == slot, wet_row, jnp.where(sub == slot + 1, penalty_row, 0.0))

def harm(first, second):
    return 2.0 * first * second / (first + second)

def slope_of(back, ahead):
    return jnp.maximum(jnp.minimum(back, ahead), 0.0) + jnp.minimum(jnp.maximum(back, ahead), 0.0)

def east_of(cells, k, side):
    return cells[k + 1] if k % side < side - 1 else pltpu.roll(cells[k + 1 - side], 127, 1)

def west_of(cells, k, side):
    return cells[k - 1] if k % side > 0 else pltpu.roll(cells[k - 1 + side], 1, 1)

def north_of(cells, k, side):
    return cells[k + side] if k < side * (side - 1) else pltpu.roll(cells[k % side], 120, 1)

def south_of(cells, k, side):
    return cells[k - side] if k >= side else pltpu.roll(cells[k + side * (side - 1)], 8, 1)

def upper_of(cell):
    return pltpu.roll(cell, 1, 0)

def lower_of(cell):
    return pltpu.roll(cell, 7, 0)

def step_kernel(
    near_ref, far_ref, first_ref, second_ref, salt_ref, recharge_ref, tendency_ref, head_ref, fine_ref, coarse_ref, ring_ref, wide_ref
):
    device = lax.axis_index("gx")
    sub, lane = iotas((8, 128))
    top = sub == 0
    even = (device & 1) == 0
    odd = odd_ones(device)
    orders = [lambda e: ((e >> 3) & 1) + (e & 2) + (e & 4), lambda e: ((e >> 1) & 1) + ((e & 8) >> 2) + (e & 4)]
    here = jnp.where(odd, orders[1](device), orders[0](device))
    there = jnp.where(odd, orders[0](device), orders[1](device))
    flip = (device & 4) != 0
    small = []
    for ref in (near_ref, far_ref):
        halves = [ref[8 * MAIN + SMALL * i : 8 * MAIN + SMALL * (i + 1), :] for i in range(2)]
        small.append([jnp.where(flip, halves[1 - i], halves[i]) for i in range(2)])
    means, conds, smalls = [], [], []
    for e in range(16):
        mine = odd == (bin(e).count("1") % 2 == 1)
        if e % 2 == 0:
            start = pl.multiple_of((here ^ jnp.where(odd, orders[1](e), orders[0](e))) * MAIN, 8)
            near = [near_ref[pl.ds(start, 8), :], near_ref[pl.ds(pl.multiple_of(start + 8, 8), 8), :]]
            start = pl.multiple_of((there ^ jnp.where(odd, orders[0](e), orders[1](e))) * MAIN, 8)
            far = [far_ref[pl.ds(start, 8), :], far_ref[pl.ds(pl.multiple_of(start + 8, 8), 8), :]]
        means.append(jnp.where(mine, near[0], far[0]))
        conds.append(jnp.where(mine, near[1], far[1]))
        smalls.append(jnp.where(mine, small[0][(e >> 2) & 1], small[1][(e >> 2) & 1]))

    slots = [2 * ((e // 2) % 2) + 4 * (e // 8) for e in range(16)]
    wets = [smalls[e][slots[e] : slots[e] + 1] for e in range(16)]
    penalties = [smalls[e][slots[e] + 1 : slots[e] + 2] for e in range(16)]

    def diagonals(fields, index):
        count = len(fields)
        bit = 1
        while bit < count:
            high = (index & bit) != 0
            fields = [jnp.where(high, fields[(m + bit) % count], fields[m]) for m in range(count)]
            bit *= 2
        return fields

    def by_block(fields):
        group = lane[0 : fields[0].shape[0]] >> 3
        picked = diagonals(fields, group)
        return [pltpu.roll(picked[-k % 16], (128 - 8 * k) % 128, 1) for k in range(16)]

    def by_lane(fields):
        within = lane & 7
        out = []
        picked = diagonals(fields, within)
        for s in range(8):
            here = picked[-s % 8]
            if s > 0:
                here = jnp.where(within < 8 - s, pltpu.roll(here, 128 - s, 1), pltpu.roll(here, 8 - s, 1))
            out.append(here)
        return out

    cond = by_block(conds)
    penalties = by_block(penalties)
    salt = [None] * 16
    wet_frac = [None] * 16
    wet_pairs = by_lane([jnp.where(top, wets[2 * b], wets[2 * b + 1]) for b in range(8)])
    for half in range(2):
        columns = by_lane(means[half::2])
        for s in range(8):
            k = 4 * (s // 2) + 2 * half + s % 2
            salt[k] = columns[s]
            wet_frac[k] = wet_pairs[s] if half == 0 else lower_of(wet_pairs[s])

    def coefficients(cells, penalty, side, vertical, weight_ref):
        face_w, face_e, face_s, face_n, face_d = [], [], [], [], []
        for k in range(side * side):
            e = harm(cells[k], east_of(cells, k, side))
            if k % side == side - 1:
                e = jnp.where((lane & 7) < 7, e, 0.0)
            n = harm(cells[k], north_of(cells, k, side))
            if k >= side * (side - 1):
                n = jnp.where(lane < 120, n, 0.0)
            w = face_e[k - 1] if k % side > 0 else None
            if w is None:
                w = jnp.where((lane & 7) > 0, harm(west_of(cells, k, side), cells[k]), 0.0)
            s = face_n[k - side] if k >= side else None
            if s is None:
                s = jnp.where(lane >= 8, harm(south_of(cells, k, side), cells[k]), 0.0)
            face_w.append(w)
            face_e.append(e)
            face_s.append(s)
            face_n.append(n)
            face_d.append(jnp.where(sub < 7, vertical * harm(cells[k], lower_of(cells[k])), 0.0))
        weights = []
        for k in range(side * side):
            six = (face_w[k], face_e[k], face_s[k], face_n[k], upper_of(face_d[k]), face_d[k])
            diag = six[0] + six[1] + six[2] + six[3] + six[4] + six[5] + penalty[k]
            weight = relax_weight / diag
            for number, face in enumerate(six):
                weight_ref[number, k] = weight * face
            weight_ref[6, k] = diag * (1.0 / relax_weight)
            weight_ref[7, k] = weight
            weights.append(weight)
        return (face_w, face_e, face_s, face_n, face_d), weights

    def step(here, west, east, south, north, weights):
        pairs = (west, east, south, north, upper_of(here), lower_of(here))
        terms = [weights(number) * pair for number, pair in enumerate(pairs)]
        base = (1.0 - relax_weight) * here + weights(8)
        return ((terms[0] + terms[1]) + (terms[2] + terms[3])) + ((terms[4] + terms[5]) + base)

    def edges_of(cells):
        return (
            [pltpu.roll(cells[4 * j + 3], 1, 1) for j in range(4)],
            [pltpu.roll(cells[4 * j], 127, 1) for j in range(4)],
            [pltpu.roll(cells[12 + i], 8, 1) for i in range(4)],
            [pltpu.roll(cells[i], 120, 1) for i in range(4)],
        )

    def relaxed(cells, edges):
        out = []
        for k in range(16):
            j, i = k // 4, k % 4
            west = cells[k - 1] if i > 0 else edges[0][j]
            east = cells[k + 1] if i < 3 else edges[1][j]
            south = cells[k - 4] if j > 0 else edges[2][i]
            north = cells[k + 4] if j < 3 else edges[3][i]
            out.append(step(cells[k], west, east, south, north, lambda number, k=k: fine_ref[number, k]))
        return out

    ring = [(j, i) for j in range(-1, 3) for i in range(-1, 3) if (j in (0, 1)) != (i in (0, 1))]

    def beyond(cells, j, i):
        shift = -(8 * (j // 2) + i // 2) % 128
        cell = cells[2 * (j % 2) + i % 2]
        return pltpu.roll(cell, shift, 1) if shift else cell

    def relaxed_around(cells):
        old, new = {}, {}

        def at(j, i):
            if (j, i) not in old:
                old[j, i] = beyond(cells, j, i)
            return old[j, i]

        for j, i in ring + [(0, 0), (0, 1), (1, 0), (1, 1)]:
            if (j, i) in ring:
                weights = lambda number, q=ring.index((j, i)): ring_ref[number, q]
            else:
                weights = lambda number, k=2 * j + i: coarse_ref[number, k]
            new[j, i] = step(at(j, i), at(j, i - 1), at(j, i + 1), at(j - 1, i), at(j + 1, i), weights)
        return new

    def relaxed_within(new):
        return [
            step(new[j, i], new[j, i - 1], new[j, i + 1], new[j - 1, i], new[j + 1, i],
                 lambda number, k=2 * j + i: coarse_ref[number, k])
            for j in range(2) for i in range(2)
        ]

    def pair_sums(cells):
        return [(cells[k] + cells[k + 1]) + (cells[k + 4] + cells[k + 5]) for k in (0, 2, 8, 10)]

    penalty, river = [], []
    for k in range(16):
        penalty.append(jnp.where(top, penalties[k], 0.0))
        river.append(jnp.where(penalties[k] == river_penalty, river_penalty, 0.0))
    faces, weights = coefficients(cond, penalty, 4, vertical_ratio, fine_ref)
    for k in range(16):
        below = jnp.where(sub < 7, 0.5 * (salt[k] + lower_of(salt[k])), 0.0)
        pull = faces[4][k] * below
        source = jnp.where(top, recharge_rate * wet_frac[k] + river_head * river[k], 0.0)
        fine_ref[8, k] = weights[k] * (upper_of(pull) - pull + source)
        fine_ref[9, k] = below
        for number, face in enumerate(faces):
            fine_ref[10 + number, k] = face[k]
    coefficients([0.25 * c for c in pair_sums(cond)], pair_sums(penalty), 2, 4.0 * vertical_ratio, coarse_ref)
    for number in range(6):
        cells = [coarse_ref[number, k] for k in range(4)]
        for q, (j, i) in enumerate(ring):
            ring_ref[number, q] = beyond(cells, j, i)

    head = None
    for cycle_no in range(CYCLES):
        for sweep in range(SMOOTH):
            head = [fine_ref[8, k] for k in range(16)] if head is None else relaxed(head, edges_of(head))
        edges = edges_of(head)
        ahead = relaxed(head, edges)
        resid = pair_sums([(ahead[k] - head[k]) * fine_ref[6, k] for k in range(16)])
        correction = []
        for k in range(4):
            correction.append(coarse_ref[7, k] * resid[k])
            coarse_ref[8, k] = correction[k]
        for q, (j, i) in enumerate(ring):
            ring_ref[8, q] = beyond(correction, j, i)
        sweeps = COARSE_SWEEPS - 1
        while sweeps > 0:
            around = relaxed_around(correction)
            correction = [around[k // 2, k % 2] for k in range(4)]
            sweeps -= 1
            if sweeps > 0:
                correction = relaxed_within(around)
                around = None
                sweeps -= 1
        if around is None:
            around = {place: beyond(correction, *place) for place in ring}
        head = [head[k] + correction[2 * (k // 8) + (k % 4) // 2] for k in range(16)]
        edges = (
            [edges[0][n] + around[n // 2, -1] for n in range(4)],
            [edges[1][n] + around[n // 2, 2] for n in range(4)],
            [edges[2][n] + around[-1, n // 2] for n in range(4)],
            [edges[3][n] + around[2, n // 2] for n in range(4)],
        )
        for sweep in range(SMOOTH):
            head = relaxed(head, edges_of(head) if edges is None else edges)
            edges = None

    largest = None
    for k in range(16):
        here = head[k]
        west, east = west_of(head, k, 4) - here, here - east_of(head, k, 4)
        south, north = south_of(head, k, 4) - here, here - north_of(head, k, 4)
        vel_x = 0.5 * (fine_ref[10, k] * west + fine_ref[11, k] * east)
        vel_y = 0.5 * (fine_ref[12, k] * south + fine_ref[13, k] * north)
        flow_d = fine_ref[14, k] * (here - lower_of(here) + fine_ref[9, k])
        vel_z = 0.5 * (upper_of(flow_d) + flow_d)
        wide_ref[0, k] = vel_x
        wide_ref[1, k] = vel_y
        wide_ref[2, k] = vel_z
        speed = jnp.abs(vel_x) + jnp.abs(vel_y) + jnp.abs(vel_z)
        largest = speed if largest is None else jnp.maximum(largest, speed)
    step = courant / (jnp.max(largest, axis=(0, 1), keepdims=True) + 1e-06)

    def along(field, x, beside=False):
        halves = []
        for half in range(2):
            y = 128 * half + lane
            if beside:
                y = jnp.clip(y + jnp.where((lane & 3) == 3, 1, jnp.where((lane & 3) == 0, -1, 0)), 0, 255)
            y = y >> 2
            source = ((y >> 2) << 3) + (x >> 2)
            part = jnp.take_along_axis(wide_ref[field, x & 3], source, axis=1)
            for j in range(1, 4):
                part = jnp.where((y & 3) == j, jnp.take_along_axis(wide_ref[field, 4 * j + (x & 3)], source, axis=1), part)
            halves.append(part)
        return jnp.concatenate(halves, axis=1)

    xs = [jnp.clip(2 * device - 1 + j, 0, 31) for j in range(4)]
    speed_x = [along(0, x) for x in xs]
    speed_z = [along(2, x) for x in xs[1:3]]
    speed_y = [along(1, x) for x in xs[1:3]]
    beside_y = [along(1, x, True) for x in xs[1:3]]

    layer, column = iotas((8, 256))
    crossed = device ^ jnp.where(even, device - 1, device + 1)
    halo = []
    for i in range(4):
        parts = []
        for half in range(2):
            place = 8 * (2 * i + half)
            here = 8 * (MAIN + 2) + place
            part = far_ref[here : here + 8, :]
            if i < 2:
                start = MAIN + SMALL + place
                straight = first_ref[start : start + 8, :]
                straight = jnp.where(odd, straight, second_ref[MAIN + start : MAIN + start + 8, :])
                part = jnp.where(crossed == 7, part, jnp.where(crossed == 15, near_ref[here : here + 8, :], 0.0))
                part = jnp.where(crossed == 3, straight, part)
            parts.append(part)
        halo.append(jnp.concatenate(parts, axis=1))
    cells = (
        [jnp.where(even, halo[j], halo[2 + j]) for j in range(2)]
        + [salt_ref[:, x, :] for x in range(8)]
        + [jnp.where(even, halo[2 + j], halo[j]) for j in range(2)]
    )
    diffs = [cells[i + 1] - cells[i] for i in range(11)]
    halves = [0.5 * slope_of(diffs[i], diffs[i + 1]) for i in range(10)]
    flux_x = []
    for f in range(9):
        if f % 4 == 0:
            face = 0.5 * (speed_x[f // 4] + speed_x[f // 4 + 1])
            if f == 0:
                face = jnp.where(device == 0, 0.0, face)
            if f == 8:
                face = jnp.where(device == 15, 0.0, face)
        else:
            face = speed_x[1 + f // 4]
        flux_x.append(face * jnp.where(face > 0, cells[f + 1] + halves[f], cells[f + 2] - halves[f + 1]))
    faces_z = [jnp.where(layer < 7, 0.5 * (v + pltpu.roll(v, 7, 0)), 0.0) for v in speed_z]
    between = [0.5 * (v + beside) for v, beside in zip(speed_y, beside_y)]
    faces_n = [jnp.where((column & 3) == 3, b, v) for v, b in zip(speed_y, between)]
    faces_n = [jnp.where(column < 255, face, 0.0) for face in faces_n]
    faces_s = [jnp.where((column & 3) == 0, b, v) for v, b in zip(speed_y, between)]
    faces_s = [jnp.where(column > 0, face, 0.0) for face in faces_s]
    for x in range(8):
        cell = cells[x + 2]
        ahead = jnp.where(layer < 7, pltpu.roll(cell, 7, 0), 0.0) - cell
        half = 0.5 * slope_of(jnp.where(layer > 0, pltpu.roll(ahead, 1, 0), cell), ahead)
        face = faces_z[x // 4]
        flux_z = face * jnp.where(face > 0, cell + half, pltpu.roll(cell - half, 7, 0))
        change = flux_z - pltpu.roll(flux_z, 1, 0)
        change = change + (flux_x[x + 1] - flux_x[x])
        ahead = jnp.where(column < 255, pltpu.roll(cell, 255, 1), 0.0) - cell
        half = 0.5 * slope_of(jnp.where(column > 0, pltpu.roll(ahead, 1, 1), cell), ahead)
        below, above = cell + half, cell - half
        face = faces_n[x // 4]
        flux_n = face * jnp.where(face > 0, below, pltpu.roll(above, 255, 1))
        face = faces_s[x // 4]
        flux_s = face * jnp.where(face > 0, pltpu.roll(below, 1, 1), above)
        change = change + (flux_n - flux_s)
        wet = recharge_ref[x : x + 1, :].astype(jnp.float32)
        dilution = jnp.where(layer == 0, freshening * wet * cell, 0.0)
        tendency_ref[:, x, :] = -step * change - step * dilution

    own = 8 * device + ((lane & 31) >> 2)
    for j in range(4):
        row = jnp.take_along_axis(head[4 * j], own, axis=1)
        for i in range(1, 4):
            row = jnp.where((lane & 3) == i, jnp.take_along_axis(head[4 * j + i], own, axis=1), row)
        head_ref[:, j, :] = row[:, 0:32]

def local_small(salt, recharge, conductivity, codes):
    vmem = pl.BlockSpec(memory_space=pltpu.VMEM)
    block, inner, relay = pl.pallas_call(
        pack_kernel,
        out_shape=(
            pltpu.VMEM((MAIN + SMALL + COLUMNS, 128), jnp.float32),
            pltpu.VMEM((COLUMNS, 128), jnp.float32),
            pltpu.VMEM((8, 128), jnp.float32),
        ),
        in_specs=[vmem] * 4,
        out_specs=(vmem,) * 3,
        scratch_shapes=[pltpu.VMEM((2, 64, 128), jnp.float32), pltpu.VMEM((32, 128), jnp.float32)],
        name="pack",
    )(salt, recharge, conductivity, codes)

    def swapped(array, turn):
        pairs = [(i, i ^ ROUNDS[bin(i).count("1") % 2][turn]) for i in range(lax.axis_size("gx"))]
        return lax.ppermute(array, "gx", pairs)

    def small(array, count):
        return array[count * MAIN : count * MAIN + SMALL]

    def columns(array, count):
        return array[count * MAIN + SMALL :]

    relay = jnp.tile(relay, (COLUMNS // 8, 1))
    first = swapped(block, 0)
    handed = jnp.where(relay > 1.5, columns(block, 1), columns(first, 1))
    block = jnp.concatenate([block[:MAIN], first[:MAIN], small(block, 1) + small(first, 1), handed])
    second = swapped(block, 1)
    handed = jnp.where(relay > 0.5, columns(second, 2), columns(first, 1))
    block = jnp.concatenate(
        [block[: 2 * MAIN], second[: 2 * MAIN], small(block, 2) + small(second, 2), handed]
    )
    other = swapped(block, 2)
    block = jnp.concatenate(
        [block[: 4 * MAIN], other[: 4 * MAIN], small(block, 4), small(other, 4), columns(other, 4), inner]
    )
    other = swapped(block, 3)
    return pl.pallas_call(
        step_kernel,
        out_shape=(
            jax.ShapeDtypeStruct(salt.shape, jnp.float32),
            jax.ShapeDtypeStruct(conductivity.shape, jnp.float32),
        ),
        in_specs=[vmem] * 6,
        out_specs=(vmem,) * 2,
        scratch_shapes=[
            pltpu.VMEM((15, 16, 8, 128), jnp.float32),
            pltpu.VMEM((9, 4, 8, 128), jnp.float32),
            pltpu.VMEM((9, 8, 8, 128), jnp.float32),
            pltpu.VMEM((3, 16, 8, 128), jnp.float32),
        ],
        compiler_params=pltpu.CompilerParams(vmem_limit_bytes=16 * 1024 * 1024),
        name="step",
    )(block, other, first, second, salt, recharge)

def local(salt, recharge, conductivity, codes):
    small = (
        lax.axis_size("gx") == 16
        and salt.shape == (8, 8, 256)
        and recharge.shape == (8, 256)
        and conductivity.shape == (8, 4, 32)
        and codes.shape == (4, 32)
    )
    return (local_small if small else local_shared)(salt, recharge, conductivity, codes)

def solution(mesh):
    return jax.shard_map(
        local,
        mesh=mesh,
        in_specs=(
            P("parts", "gx", None),
            P("gx", "parts"),
            P("parts", "gx", None),
            P("gx", "parts"),
        ),
        out_specs=(P("parts", "gx", None), P("parts", "gx", None)),
        check_vma=False,
    )
```

```python
import jax
import jax.numpy as jnp
from jax import lax
from jax.experimental import pallas as pl
from jax.experimental.pallas import tpu as pltpu
from jax.sharding import PartitionSpec as P

CYCLES = 2
SMOOTH = 2
COARSE_SWEEPS = 6

relax_weight = 0.8
vertical_ratio = 0.5
sea_penalty = 2.0
river_penalty = 0.5
river_head = 1.0
recharge_rate = 1.0
courant = 0.45
freshening = 1.0

def padded_2(array, sides, width):
    for axis, dim in sides:
        count, length = (lax.axis_size(axis), array.shape[dim])
        up = [(i, (i + 1) % count) for i in range(count - 1)]
        down = [(j, i) for i, j in up]
        last = lax.slice_in_dim(array, length - width, length, axis=dim)
        first = lax.slice_in_dim(array, 0, width, axis=dim)
        before = lax.ppermute(last, axis, up)
        after = lax.ppermute(first, axis, down)
        array = jnp.concatenate([before, array, after], axis=dim)
    return array

def harmonic(first, second):
    total = first + second
    return 2.0 * first * second / (total + jnp.where(total > 0, 0.0, 1.0))

def coefficients(padded, penalty, vertical_scale):
    inner = padded[:, 1:-1, :]
    y_low = harmonic(inner, padded[:, :-2, :])
    y_high = harmonic(inner, padded[:, 2:, :])
    x_face = harmonic(inner[:, :, :-1], inner[:, :, 1:])
    zero_col = jnp.zeros_like(inner[:, :, :1])
    x_low = jnp.concatenate([zero_col, x_face], axis=2)
    x_high = jnp.concatenate([x_face, zero_col], axis=2)
    z_face = vertical_scale * vertical_ratio * harmonic(inner[:-1], inner[1:])
    zero_layer = jnp.zeros_like(inner[:1])
    z_up = jnp.concatenate([zero_layer, z_face], axis=0)
    z_down = jnp.concatenate([z_face, zero_layer], axis=0)
    top_term = jnp.concatenate([penalty[None], jnp.zeros_like(inner[1:])], axis=0)
    diagonal = x_low + x_high + y_low + y_high + z_up + z_down + top_term
    return (x_low, x_high, y_low, y_high, z_up, z_down, diagonal)

def neighbors(padded):
    center = padded[:, 1:-1, :]
    zero_col = jnp.zeros_like(center[:, :, :1])
    west = jnp.concatenate([zero_col, center[:, :, :-1]], axis=2)
    east = jnp.concatenate([center[:, :, 1:], zero_col], axis=2)
    zero_layer = jnp.zeros_like(center[:1])
    upper = jnp.concatenate([zero_layer, center[:-1]], axis=0)
    lower = jnp.concatenate([center[1:], zero_layer], axis=0)
    return (center, west, east, padded[:, :-2, :], padded[:, 2:, :], upper, lower)

def apply_operator(padded, coeffs):
    center, west, east, south, north, upper, lower = neighbors(padded)
    x_low, x_high, y_low, y_high, z_up, z_down, diagonal = coeffs
    return (
        diagonal * center
        - x_low * west
        - x_high * east
        - y_low * south
        - y_high * north
        - z_up * upper
        - z_down * lower
    )

def relax(padded, coeffs, right_side):
    return (
        padded[:, 1:-1, :]
        + relax_weight * (right_side - apply_operator(padded, coeffs)) / coeffs[6]
    )

def block_mean(field):
    leading = field.shape[:-2]
    count_a, count_b = field.shape[-2:]
    grouped = field.reshape(leading + (count_a // 4, 4, count_b // 4, 4))
    return jnp.sum(grouped, axis=(-3, -1)) * 0.0625

def pair_sum(field):
    leading = field.shape[:-2]
    count_a, count_b = field.shape[-2:]
    grouped = field.reshape(leading + (count_a // 2, 2, count_b // 2, 2))
    return jnp.sum(grouped, axis=(-3, -1))

def upsample(field, factor):
    return jnp.repeat(jnp.repeat(field, factor, axis=-2), factor, axis=-1)

def minmod(first, second):
    return 0.5 * (jnp.sign(first) + jnp.sign(second)) * jnp.minimum(jnp.abs(first), jnp.abs(second))

def portion(field, start, stop, axis):
    return lax.slice_in_dim(field, start, stop, axis=axis)

def divergence(cells, speed, axis):
    length = cells.shape[axis]
    widths = [(0, 0)] * cells.ndim
    widths[axis] = (1, 1)
    padded = jnp.pad(cells, widths)
    steps_diff = portion(padded, 1, length + 2, axis) - portion(padded, 0, length + 1, axis)
    slope = minmod(portion(steps_diff, 0, length, axis), portion(steps_diff, 1, length + 1, axis))
    faces = 0.5 * (portion(speed, 0, length - 1, axis) + portion(speed, 1, length, axis))
    left = portion(cells, 0, length - 1, axis) + 0.5 * portion(slope, 0, length - 1, axis)
    right = portion(cells, 1, length, axis) - 0.5 * portion(slope, 1, length, axis)
    flux = jnp.pad(faces * jnp.where(faces > 0, left, right), widths)
    return portion(flux, 1, length + 1, axis) - portion(flux, 0, length, axis)

def divergence_x(extended, faces):
    steps_diff = extended[:, 1:] - extended[:, :-1]
    slope = minmod(steps_diff[:, :-1], steps_diff[:, 1:])
    cells = extended[:, 1:-1]
    left = cells[:, :-1] + 0.5 * slope[:, :-1]
    right = cells[:, 1:] - 0.5 * slope[:, 1:]
    flux = faces * jnp.where(faces > 0, left, right)
    return flux[:, 1:] - flux[:, :-1]

def velocities(padded, coeffs, above, below):
    center, west, east, south, north, upper, lower = neighbors(padded)
    x_low, x_high, y_low, y_high, z_up, z_down, diagonal = coeffs
    vel_x = 0.5 * (x_low * (west - center) + x_high * (center - east))
    vel_y = 0.5 * (y_low * (south - center) + y_high * (center - north))
    vel_z = 0.5 * (z_up * (upper - center + above) + z_down * (center - lower + below))
    return (vel_z, vel_x, vel_y)

def buoyancy_terms(salt_coarse):
    face_salt = 0.5 * (salt_coarse[:-1] + salt_coarse[1:])
    zero_layer = jnp.zeros_like(salt_coarse[:1])
    above = jnp.concatenate([zero_layer, face_salt], axis=0)
    below = jnp.concatenate([face_salt, zero_layer], axis=0)
    return (above, below)

def boundary_penalty(codes):
    return jnp.where(codes == 1, sea_penalty, 0.0) + jnp.where(codes == 2, river_penalty, 0.0)

def source_terms(coeffs, above, below, recharge_frac, codes):
    top_source = recharge_rate * recharge_frac + river_head * jnp.where(
        codes == 2, river_penalty, 0.0
    )
    surface = jnp.concatenate([top_source[None], jnp.zeros_like(above[1:])], axis=0)
    return coeffs[4] * above - coeffs[5] * below + surface

def local_shared(salt, recharge, conductivity, codes):
    layers = salt.shape[0]
    tile = salt.shape[1]
    wet = recharge.astype(jnp.float32)
    blocks = jnp.concatenate([block_mean(salt), block_mean(wet)[None]], axis=0)
    owned = lax.all_to_all(
        jnp.transpose(blocks, (0, 2, 1)), "gx", split_axis=1, concat_axis=2, tiled=True
    )
    salt_coarse = owned[:layers]
    recharge_frac = owned[layers]
    penalty = boundary_penalty(codes)
    cond_padded = padded_2(conductivity, (("gx", 1),), 1)
    coeffs = coefficients(cond_padded, penalty, 1.0)
    above, below = buoyancy_terms(salt_coarse)
    right_side = source_terms(coeffs, above, below, recharge_frac, codes)
    coarse_cond = 0.25 * pair_sum(conductivity)
    coarse_pen = pair_sum(penalty)
    coarse_padded = padded_2(coarse_cond, (("gx", 1),), 1)
    coarse_coeffs = coefficients(coarse_padded, coarse_pen, 4.0)

    def smooth(current):
        padded = padded_2(current, (("gx", 1),), 1)
        return relax(padded, coeffs, right_side)

    head = jnp.zeros_like(conductivity)
    for cycle_no in range(CYCLES):
        for sweep in range(SMOOTH):
            head = smooth(head)
        head_padded = padded_2(head, (("gx", 1),), 1)
        residual = right_side - apply_operator(head_padded, coeffs)
        coarse_resid = pair_sum(residual)
        correction = jnp.zeros_like(coarse_resid)
        for sweep in range(COARSE_SWEEPS):
            corr_padded = padded_2(correction, (("gx", 1),), 1)
            correction = relax(corr_padded, coarse_coeffs, coarse_resid)
        head = head + upsample(correction, 2)
        for sweep in range(SMOOTH):
            head = smooth(head)
    final_padded = padded_2(head, (("gx", 1),), 1)
    vel_z, vel_x, vel_y = velocities(final_padded, coeffs, above, below)
    local_fastest = jnp.max(jnp.abs(vel_x) + jnp.abs(vel_y) + jnp.abs(vel_z))
    fastest = lax.pmax(local_fastest, "gx")
    step = courant / (fastest + 1e-06)
    packed = jnp.stack([vel_z, vel_x, vel_y])
    returned = jnp.transpose(
        lax.all_to_all(packed, "gx", split_axis=3, concat_axis=2, tiled=True), (0, 1, 3, 2)
    )
    fine_x = upsample(returned[1], 4)
    both = padded_2(jnp.stack([salt, fine_x]), (("gx", 2),), 2)
    extended = both[0]
    inner_x = both[1][:, 1:-1]
    faces = 0.5 * (inner_x[:, :-1] + inner_x[:, 1:])
    position = jnp.arange(tile + 1)
    device = lax.axis_index("gx")
    final_device = lax.axis_size("gx") - 1
    edge = (position == 0) & (device == 0) | (position == tile) & (device == final_device)
    faces = jnp.where(edge[None, :, None], 0.0, faces)
    fine_z = upsample(returned[0], 4)
    fine_y = upsample(returned[2], 4)
    change = (
        divergence(salt, fine_z, 0) + divergence_x(extended, faces) + divergence(salt, fine_y, 2)
    )
    dilution = jnp.concatenate(
        [(freshening * wet * salt[0])[None], jnp.zeros_like(salt[1:])], axis=0
    )
    tendency = -step * change - step * dilution
    return (tendency, head)

def split_dot(values, table, terms=3):
    rows = values.shape[0]
    parts = []
    for _ in range(terms):
        parts.append(values.astype(jnp.bfloat16))
        values = values - parts[-1].astype(jnp.float32)
    out = jnp.dot(jnp.concatenate(parts, axis=0), table, preferred_element_type=jnp.float32)
    return sum(out[rows * i : rows * (i + 1)] for i in range(1, terms)) + out[:rows]

def table_of(shape, same):
    row = lax.broadcasted_iota(jnp.int32, shape, 0)
    col = lax.broadcasted_iota(jnp.int32, shape, 1)
    return jnp.where(same(row, col), 1.0, 0.0).astype(jnp.bfloat16)

def iotas(shape):
    return lax.broadcasted_iota(jnp.int32, shape, 0), lax.broadcasted_iota(jnp.int32, shape, 1)

MAIN, SMALL, COLUMNS = 16, 8, 32
ROUNDS = ((9, 3, 5, 1), (3, 9, 5, 1))

def odd_ones(device):
    return ((device ^ (device >> 1) ^ (device >> 2) ^ (device >> 3)) & 1) == 1

def pack_kernel(salt_ref, recharge_ref, cond_ref, codes_ref, block_ref, inner_ref, relay_ref, kept_ref, flat_ref, turn_ref):
    kept_ref[...] = salt_ref[...]
    device = lax.axis_index("gx")
    even = (device & 1) == 0
    for j in range(2):
        first = salt_ref[:, j, :]
        last = salt_ref[:, 6 + j, :]
        inward = jnp.where(even, last, first)
        outward = jnp.where(even, first, last)
        for half in range(2):
            place = 8 * (2 * j + half)
            inner_ref[place : place + 8, :] = inward[:, 128 * half : 128 * half + 128]
            place = place + MAIN + SMALL
            block_ref[place : place + 8, :] = outward[:, 128 * half : 128 * half + 128]
    relay = jnp.where(odd_ones(device), jnp.where((device == 2) | (device == 13), 1.0, 0.0), 2.0)
    relay_ref[...] = jnp.broadcast_to(relay, (8, 128))
    turned = device >> 1
    sums = table_of((256, 128), lambda r, c: (r >> 2) == ((c >> 3) << 2) + (((c - turned) & 7) >> 1))
    for i in range(8):
        four = salt_ref[i] + pltpu.roll(salt_ref[i], 7, 0)
        four = four + pltpu.roll(four, 6, 0)
        flat_ref[0, 8 * i : 8 * i + 8, :] = four[:, 0:128]
        flat_ref[1, 8 * i : 8 * i + 8, :] = four[:, 128:256]
    rows = [
        jnp.concatenate([flat_ref[half, pl.ds(start, 8, stride=8), :] for half in range(2)], axis=1) for start in (0, 4)
    ]
    means = split_dot(jnp.concatenate(rows, axis=0), sums) * 0.0625
    sub, lane = iotas((8, 128))
    mine = (sub >> 2) == ((lane - turned) & 1)
    block_ref[0:8, :] = jnp.where(((lane - turned) & 1) == 0, means[0:8], means[8:16])
    wet_y = jnp.dot(
        recharge_ref[...].astype(jnp.float32).astype(jnp.bfloat16), sums, preferred_element_type=jnp.float32
    )
    wet_row = jnp.sum(jnp.where(mine, wet_y, 0.0), axis=0, keepdims=True) * 0.0625
    for layer in range(8):
        turn_ref[4 * layer : 4 * layer + 4, 0:32] = cond_ref[layer]
    spread = table_of((32, 128), lambda r, c: r == ((c & 7) << 2) + (((c >> 3) - device) & 3))
    turn_ref[...] = split_dot(turn_ref[:, 0:32], spread)
    packed = jnp.zeros((8, 128), jnp.float32)
    for j in range(4):
        packed = jnp.where(((((lane >> 3) - device) & 15) >> 2) == j, turn_ref[pl.ds(j, 8, stride=4), :], packed)
    block_ref[8:16, :] = packed
    codes = codes_ref[...]
    penalty = jnp.where(codes == 1, sea_penalty, 0.0) + jnp.where(codes == 2, river_penalty, 0.0)
    penalty_x = jnp.dot(penalty.astype(jnp.bfloat16), spread, preferred_element_type=jnp.float32)
    row4, lane4 = iotas((4, 128))
    penalty_row = jnp.sum(jnp.where(row4 == ((((lane4 >> 3) - device) & 15) >> 2), penalty_x, 0.0), axis=0, keepdims=True)
    slot = (device & 2) + ((device & 8) >> 1)
    block_ref[16:24, :] = jnp.where(sub == slot, wet_row, jnp.where(sub == slot + 1, penalty_row, 0.0))

def harm(first, second):
    return 2.0 * first * second / (first + second)

def slope_of(back, ahead):
    return jnp.maximum(jnp.minimum(back, ahead), 0.0) + jnp.minimum(jnp.maximum(back, ahead), 0.0)

def east_of(cells, k, side):
    return cells[k + 1] if k % side < side - 1 else pltpu.roll(cells[k + 1 - side], 127, 1)

def west_of(cells, k, side):
    return cells[k - 1] if k % side > 0 else pltpu.roll(cells[k - 1 + side], 1, 1)

def north_of(cells, k, side):
    return cells[k + side] if k < side * (side - 1) else pltpu.roll(cells[k % side], 120, 1)

def south_of(cells, k, side):
    return cells[k - side] if k >= side else pltpu.roll(cells[k + side * (side - 1)], 8, 1)

def upper_of(cell):
    return pltpu.roll(cell, 1, 0)

def lower_of(cell):
    return pltpu.roll(cell, 7, 0)

def sides_kernel(salt_ref, side_ref):
    layer, column = iotas((8, 256))
    cells = [salt_ref[:, x, :] for x in range(8)]
    for x in range(8):
        cell = cells[x]
        ahead = jnp.where(layer < 7, lower_of(cell), 0.0) - cell
        half = 0.5 * slope_of(jnp.where(layer > 0, upper_of(ahead), cell), ahead)
        side_ref[0, x] = cell + half
        side_ref[1, x] = lower_of(cell - half)
        ahead = jnp.where(column < 255, pltpu.roll(cell, 255, 1), 0.0) - cell
        half = 0.5 * slope_of(jnp.where(column > 0, pltpu.roll(ahead, 1, 1), cell), ahead)
        side_ref[2, x] = cell + half
        side_ref[3, x] = pltpu.roll(cell - half, 255, 1)
        side_ref[4, x] = pltpu.roll(cell + half, 1, 1)
        side_ref[5, x] = cell - half
        if 0 < x < 7:
            half = 0.5 * slope_of(cell - cells[x - 1], cells[x + 1] - cell)
            side_ref[6, x] = cell + half
            side_ref[7, x] = cell - half

def step_kernel(
    near_ref, far_ref, first_ref, second_ref, side_ref, salt_ref, recharge_ref, tendency_ref, head_ref, fine_ref, coarse_ref, ring_ref, wide_ref
):
    device = lax.axis_index("gx")
    sub, lane = iotas((8, 128))
    top = sub == 0
    even = (device & 1) == 0
    odd = odd_ones(device)
    orders = [lambda e: ((e >> 3) & 1) + (e & 2) + (e & 4), lambda e: ((e >> 1) & 1) + ((e & 8) >> 2) + (e & 4)]
    here = jnp.where(odd, orders[1](device), orders[0](device))
    there = jnp.where(odd, orders[0](device), orders[1](device))
    flip = (device & 4) != 0
    small = []
    for ref in (near_ref, far_ref):
        halves = [ref[8 * MAIN + SMALL * i : 8 * MAIN + SMALL * (i + 1), :] for i in range(2)]
        small.append([jnp.where(flip, halves[1 - i], halves[i]) for i in range(2)])
    means, conds, smalls = [], [], []
    for e in range(16):
        mine = odd == (bin(e).count("1") % 2 == 1)
        if e % 2 == 0:
            start = pl.multiple_of((here ^ jnp.where(odd, orders[1](e), orders[0](e))) * MAIN, 8)
            near = [near_ref[pl.ds(start, 8), :], near_ref[pl.ds(pl.multiple_of(start + 8, 8), 8), :]]
            start = pl.multiple_of((there ^ jnp.where(odd, orders[0](e), orders[1](e))) * MAIN, 8)
            far = [far_ref[pl.ds(start, 8), :], far_ref[pl.ds(pl.multiple_of(start + 8, 8), 8), :]]
        means.append(jnp.where(mine, near[0], far[0]))
        conds.append(jnp.where(mine, near[1], far[1]))
        smalls.append(jnp.where(mine, small[0][(e >> 2) & 1], small[1][(e >> 2) & 1]))

    slots = [2 * ((e // 2) % 2) + 4 * (e // 8) for e in range(16)]
    wets = [smalls[e][slots[e] : slots[e] + 1] for e in range(16)]
    penalties = [smalls[e][slots[e] + 1 : slots[e] + 2] for e in range(16)]

    def diagonals(fields, index):
        count = len(fields)
        bit = 1
        while bit < count:
            high = (index & bit) != 0
            fields = [jnp.where(high, fields[(m + bit) % count], fields[m]) for m in range(count)]
            bit *= 2
        return fields

    def by_block(fields):
        group = lane[0 : fields[0].shape[0]] >> 3
        picked = diagonals(fields, group)
        return [pltpu.roll(picked[-k % 16], (128 - 8 * k) % 128, 1) for k in range(16)]

    def by_lane(fields):
        within = lane & 7
        out = []
        picked = diagonals(fields, within)
        for s in range(8):
            here = picked[-s % 8]
            if s > 0:
                here = jnp.where(within < 8 - s, pltpu.roll(here, 128 - s, 1), pltpu.roll(here, 8 - s, 1))
            out.append(here)
        return out

    cond = by_block(conds)
    penalties = by_block(penalties)
    salt = [None] * 16
    wet_frac = [None] * 16
    wet_pairs = by_lane([jnp.where(top, wets[2 * b], wets[2 * b + 1]) for b in range(8)])
    for half in range(2):
        columns = by_lane(means[half::2])
        for s in range(8):
            k = 4 * (s // 2) + 2 * half + s % 2
            salt[k] = columns[s]
            wet_frac[k] = wet_pairs[s] if half == 0 else lower_of(wet_pairs[s])

    def coefficients(cells, penalty, side, vertical, weight_ref):
        face_w, face_e, face_s, face_n, face_d = [], [], [], [], []
        for k in range(side * side):
            e = harm(cells[k], east_of(cells, k, side))
            if k % side == side - 1:
                e = jnp.where((lane & 7) < 7, e, 0.0)
            n = harm(cells[k], north_of(cells, k, side))
            if k >= side * (side - 1):
                n = jnp.where(lane < 120, n, 0.0)
            w = face_e[k - 1] if k % side > 0 else None
            if w is None:
                w = jnp.where((lane & 7) > 0, harm(west_of(cells, k, side), cells[k]), 0.0)
            s = face_n[k - side] if k >= side else None
            if s is None:
                s = jnp.where(lane >= 8, harm(south_of(cells, k, side), cells[k]), 0.0)
            face_w.append(w)
            face_e.append(e)
            face_s.append(s)
            face_n.append(n)
            face_d.append(jnp.where(sub < 7, vertical * harm(cells[k], lower_of(cells[k])), 0.0))
        weights = []
        for k in range(side * side):
            six = (face_w[k], face_e[k], face_s[k], face_n[k], upper_of(face_d[k]), face_d[k])
            diag = six[0] + six[1] + six[2] + six[3] + six[4] + six[5] + penalty[k]
            weight = relax_weight / diag
            for number, face in enumerate(six):
                weight_ref[number, k] = weight * face
            weight_ref[6, k] = diag * (1.0 / relax_weight)
            weight_ref[7, k] = weight
            weights.append(weight)
        return (face_w, face_e, face_s, face_n, face_d), weights

    def step(here, west, east, south, north, weights):
        pairs = (west, east, south, north, upper_of(here), lower_of(here))
        terms = [weights(number) * pair for number, pair in enumerate(pairs)]
        base = (1.0 - relax_weight) * here + weights(8)
        return ((terms[0] + terms[1]) + (terms[2] + terms[3])) + ((terms[4] + terms[5]) + base)

    def edges_of(cells):
        return (
            [pltpu.roll(cells[4 * j + 3], 1, 1) for j in range(4)],
            [pltpu.roll(cells[4 * j], 127, 1) for j in range(4)],
            [pltpu.roll(cells[12 + i], 8, 1) for i in range(4)],
            [pltpu.roll(cells[i], 120, 1) for i in range(4)],
        )

    def relaxed(cells, edges):
        out = []
        for k in range(16):
            j, i = k // 4, k % 4
            west = cells[k - 1] if i > 0 else edges[0][j]
            east = cells[k + 1] if i < 3 else edges[1][j]
            south = cells[k - 4] if j > 0 else edges[2][i]
            north = cells[k + 4] if j < 3 else edges[3][i]
            out.append(step(cells[k], west, east, south, north, lambda number, k=k: fine_ref[number, k]))
        return out

    ring = [(j, i) for j in range(-1, 3) for i in range(-1, 3) if (j in (0, 1)) != (i in (0, 1))]

    def beyond(cells, j, i):
        shift = -(8 * (j // 2) + i // 2) % 128
        cell = cells[2 * (j % 2) + i % 2]
        return pltpu.roll(cell, shift, 1) if shift else cell

    def relaxed_around(cells):
        old, new = {}, {}

        def at(j, i):
            if (j, i) not in old:
                old[j, i] = beyond(cells, j, i)
            return old[j, i]

        for j, i in ring + [(0, 0), (0, 1), (1, 0), (1, 1)]:
            if (j, i) in ring:
                weights = lambda number, q=ring.index((j, i)): ring_ref[number, q]
            else:
                weights = lambda number, k=2 * j + i: coarse_ref[number, k]
            new[j, i] = step(at(j, i), at(j, i - 1), at(j, i + 1), at(j - 1, i), at(j + 1, i), weights)
        return new

    def relaxed_within(new):
        return [
            step(new[j, i], new[j, i - 1], new[j, i + 1], new[j - 1, i], new[j + 1, i],
                 lambda number, k=2 * j + i: coarse_ref[number, k])
            for j in range(2) for i in range(2)
        ]

    def pair_sums(cells):
        return [(cells[k] + cells[k + 1]) + (cells[k + 4] + cells[k + 5]) for k in (0, 2, 8, 10)]

    penalty, river = [], []
    for k in range(16):
        penalty.append(jnp.where(top, penalties[k], 0.0))
        river.append(jnp.where(penalties[k] == river_penalty, river_penalty, 0.0))
    faces, weights = coefficients(cond, penalty, 4, vertical_ratio, fine_ref)
    for k in range(16):
        below = jnp.where(sub < 7, 0.5 * (salt[k] + lower_of(salt[k])), 0.0)
        pull = faces[4][k] * below
        source = jnp.where(top, recharge_rate * wet_frac[k] + river_head * river[k], 0.0)
        fine_ref[8, k] = weights[k] * (upper_of(pull) - pull + source)
        fine_ref[9, k] = below
        for number, face in enumerate(faces):
            fine_ref[10 + number, k] = face[k]
    coefficients([0.25 * c for c in pair_sums(cond)], pair_sums(penalty), 2, 4.0 * vertical_ratio, coarse_ref)
    for number in range(6):
        cells = [coarse_ref[number, k] for k in range(4)]
        for q, (j, i) in enumerate(ring):
            ring_ref[number, q] = beyond(cells, j, i)

    head = None
    for cycle_no in range(CYCLES):
        for sweep in range(SMOOTH):
            head = [fine_ref[8, k] for k in range(16)] if head is None else relaxed(head, edges_of(head))
        edges = edges_of(head)
        ahead = relaxed(head, edges)
        resid = pair_sums([(ahead[k] - head[k]) * fine_ref[6, k] for k in range(16)])
        correction = []
        for k in range(4):
            correction.append(coarse_ref[7, k] * resid[k])
            coarse_ref[8, k] = correction[k]
        for q, (j, i) in enumerate(ring):
            ring_ref[8, q] = beyond(correction, j, i)
        sweeps = COARSE_SWEEPS - 1
        while sweeps > 0:
            around = relaxed_around(correction)
            correction = [around[k // 2, k % 2] for k in range(4)]
            sweeps -= 1
            if sweeps > 0:
                correction = relaxed_within(around)
                around = None
                sweeps -= 1
        if around is None:
            around = {place: beyond(correction, *place) for place in ring}
        head = [head[k] + correction[2 * (k // 8) + (k % 4) // 2] for k in range(16)]
        edges = (
            [edges[0][n] + around[n // 2, -1] for n in range(4)],
            [edges[1][n] + around[n // 2, 2] for n in range(4)],
            [edges[2][n] + around[-1, n // 2] for n in range(4)],
            [edges[3][n] + around[2, n // 2] for n in range(4)],
        )
        for sweep in range(SMOOTH):
            head = relaxed(head, edges_of(head) if edges is None else edges)
            edges = None

    largest = None
    for k in range(16):
        here = head[k]
        west, east = west_of(head, k, 4) - here, here - east_of(head, k, 4)
        south, north = south_of(head, k, 4) - here, here - north_of(head, k, 4)
        vel_x = 0.5 * (fine_ref[10, k] * west + fine_ref[11, k] * east)
        vel_y = 0.5 * (fine_ref[12, k] * south + fine_ref[13, k] * north)
        flow_d = fine_ref[14, k] * (here - lower_of(here) + fine_ref[9, k])
        vel_z = 0.5 * (upper_of(flow_d) + flow_d)
        wide_ref[0, k] = vel_x
        wide_ref[1, k] = vel_y
        wide_ref[2, k] = vel_z
        speed = jnp.abs(vel_x) + jnp.abs(vel_y) + jnp.abs(vel_z)
        largest = speed if largest is None else jnp.maximum(largest, speed)
    step = courant / (jnp.max(largest, axis=(0, 1), keepdims=True) + 1e-06)

    def along(field, x, beside=False):
        halves = []
        for half in range(2):
            y = 128 * half + lane
            if beside:
                y = jnp.clip(y + jnp.where((lane & 3) == 3, 1, jnp.where((lane & 3) == 0, -1, 0)), 0, 255)
            y = y >> 2
            source = ((y >> 2) << 3) + (x >> 2)
            part = jnp.take_along_axis(wide_ref[field, x & 3], source, axis=1)
            for j in range(1, 4):
                part = jnp.where((y & 3) == j, jnp.take_along_axis(wide_ref[field, 4 * j + (x & 3)], source, axis=1), part)
            halves.append(part)
        return jnp.concatenate(halves, axis=1)

    xs = [jnp.clip(2 * device - 1 + j, 0, 31) for j in range(4)]
    speed_x = [along(0, x) for x in xs]
    speed_z = [along(2, x) for x in xs[1:3]]
    speed_y = [along(1, x) for x in xs[1:3]]
    beside_y = [along(1, x, True) for x in xs[1:3]]

    layer, column = iotas((8, 256))
    crossed = device ^ jnp.where(even, device - 1, device + 1)
    halo = []
    for i in range(4):
        parts = []
        for half in range(2):
            place = 8 * (2 * i + half)
            here = 8 * (MAIN + 2) + place
            part = far_ref[here : here + 8, :]
            if i < 2:
                start = MAIN + SMALL + place
                straight = first_ref[start : start + 8, :]
                straight = jnp.where(odd, straight, second_ref[MAIN + start : MAIN + start + 8, :])
                part = jnp.where(crossed == 7, part, jnp.where(crossed == 15, near_ref[here : here + 8, :], 0.0))
                part = jnp.where(crossed == 3, straight, part)
            parts.append(part)
        halo.append(jnp.concatenate(parts, axis=1))
    cells = (
        [jnp.where(even, halo[j], halo[2 + j]) for j in range(2)]
        + [salt_ref[:, x, :] for x in range(8)]
        + [jnp.where(even, halo[2 + j], halo[j]) for j in range(2)]
    )
    lower, upper = {}, {}
    for x in (-1, 0, 7, 8):
        cell = cells[x + 2]
        half = 0.5 * slope_of(cell - cells[x + 1], cells[x + 3] - cell)
        lower[x], upper[x] = cell + half, cell - half
    for x in range(1, 7):
        lower[x], upper[x] = side_ref[6, x], side_ref[7, x]
    flux_x = []
    for f in range(9):
        if f % 4 == 0:
            face = 0.5 * (speed_x[f // 4] + speed_x[f // 4 + 1])
            if f == 0:
                face = jnp.where(device == 0, 0.0, face)
            if f == 8:
                face = jnp.where(device == 15, 0.0, face)
        else:
            face = speed_x[1 + f // 4]
        flux_x.append(face * jnp.where(face > 0, lower[f - 1], upper[f]))
    faces_z = [jnp.where(layer < 7, 0.5 * (v + pltpu.roll(v, 7, 0)), 0.0) for v in speed_z]
    between = [0.5 * (v + beside) for v, beside in zip(speed_y, beside_y)]
    faces_n = [jnp.where((column & 3) == 3, b, v) for v, b in zip(speed_y, between)]
    faces_n = [jnp.where(column < 255, face, 0.0) for face in faces_n]
    faces_s = [jnp.where((column & 3) == 0, b, v) for v, b in zip(speed_y, between)]
    faces_s = [jnp.where(column > 0, face, 0.0) for face in faces_s]
    for x in range(8):
        face = faces_z[x // 4]
        flux_z = face * jnp.where(face > 0, side_ref[0, x], side_ref[1, x])
        change = flux_z - upper_of(flux_z)
        change = change + (flux_x[x + 1] - flux_x[x])
        face = faces_n[x // 4]
        flux_n = face * jnp.where(face > 0, side_ref[2, x], side_ref[3, x])
        face = faces_s[x // 4]
        flux_s = face * jnp.where(face > 0, side_ref[4, x], side_ref[5, x])
        change = change + (flux_n - flux_s)
        wet = recharge_ref[x : x + 1, :].astype(jnp.float32)
        dilution = jnp.where(layer == 0, freshening * wet * cells[x + 2], 0.0)
        tendency_ref[:, x, :] = -step * change - step * dilution

    own = 8 * device + ((lane & 31) >> 2)
    for j in range(4):
        row = jnp.take_along_axis(head[4 * j], own, axis=1)
        for i in range(1, 4):
            row = jnp.where((lane & 3) == i, jnp.take_along_axis(head[4 * j + i], own, axis=1), row)
        head_ref[:, j, :] = row[:, 0:32]

def local_small(salt, recharge, conductivity, codes):
    vmem = pl.BlockSpec(memory_space=pltpu.VMEM)
    block, inner, relay, kept = pl.pallas_call(
        pack_kernel,
        out_shape=(
            pltpu.VMEM((MAIN + SMALL + COLUMNS, 128), jnp.float32),
            pltpu.VMEM((COLUMNS, 128), jnp.float32),
            pltpu.VMEM((8, 128), jnp.float32),
            pltpu.VMEM(salt.shape, jnp.float32),
        ),
        in_specs=[vmem] * 4,
        out_specs=(vmem,) * 4,
        scratch_shapes=[pltpu.VMEM((2, 64, 128), jnp.float32), pltpu.VMEM((32, 128), jnp.float32)],
        name="pack",
    )(salt, recharge, conductivity, codes)

    def swapped(array, turn):
        pairs = [(i, i ^ ROUNDS[bin(i).count("1") % 2][turn]) for i in range(lax.axis_size("gx"))]
        return lax.ppermute(array, "gx", pairs)

    def small(array, count):
        return array[count * MAIN : count * MAIN + SMALL]

    def columns(array, count):
        return array[count * MAIN + SMALL :]

    relay = jnp.tile(relay, (COLUMNS // 8, 1))
    first = swapped(block, 0)
    handed = jnp.where(relay > 1.5, columns(block, 1), columns(first, 1))
    block = jnp.concatenate([block[:MAIN], first[:MAIN], small(block, 1) + small(first, 1), handed])
    second = swapped(block, 1)
    handed = jnp.where(relay > 0.5, columns(second, 2), columns(first, 1))
    block = jnp.concatenate(
        [block[: 2 * MAIN], second[: 2 * MAIN], small(block, 2) + small(second, 2), handed]
    )
    other = swapped(block, 2)
    block = jnp.concatenate(
        [block[: 4 * MAIN], other[: 4 * MAIN], small(block, 4), small(other, 4), columns(other, 4), inner]
    )
    other = swapped(block, 3)
    sides = pl.pallas_call(
        sides_kernel,
        out_shape=pltpu.VMEM((8, 8, 8, 256), jnp.float32),
        in_specs=[vmem],
        out_specs=vmem,
        cost_estimate=pl.CostEstimate(flops=1 << 20, bytes_accessed=1 << 20, transcendentals=0),
        name="sides",
    )(pltpu.with_memory_space_constraint(kept, pltpu.VMEM))
    return pl.pallas_call(
        step_kernel,
        out_shape=(
            jax.ShapeDtypeStruct(salt.shape, jnp.float32),
            jax.ShapeDtypeStruct(conductivity.shape, jnp.float32),
        ),
        in_specs=[vmem] * 7,
        out_specs=(vmem,) * 2,
        scratch_shapes=[
            pltpu.VMEM((15, 16, 8, 128), jnp.float32),
            pltpu.VMEM((9, 4, 8, 128), jnp.float32),
            pltpu.VMEM((9, 8, 8, 128), jnp.float32),
            pltpu.VMEM((3, 16, 8, 128), jnp.float32),
        ],
        compiler_params=pltpu.CompilerParams(vmem_limit_bytes=16 * 1024 * 1024),
        name="step",
    )(block, other, first, second, sides, kept, recharge)

def local(salt, recharge, conductivity, codes):
    small = (
        lax.axis_size("gx") == 16
        and salt.shape == (8, 8, 256)
        and recharge.shape == (8, 256)
        and conductivity.shape == (8, 4, 32)
        and codes.shape == (4, 32)
    )
    return (local_small if small else local_shared)(salt, recharge, conductivity, codes)

def solution(mesh):
    return jax.shard_map(
        local,
        mesh=mesh,
        in_specs=(
            P("parts", "gx", None),
            P("gx", "parts"),
            P("parts", "gx", None),
            P("gx", "parts"),
        ),
        out_specs=(P("parts", "gx", None), P("parts", "gx", None)),
        check_vma=False,
    )
```

```python
import jax
import jax.numpy as jnp
from jax import lax
from jax.experimental import pallas as pl
from jax.experimental.pallas import tpu as pltpu
from jax.sharding import PartitionSpec as P

CYCLES = 2
SMOOTH = 2
COARSE_SWEEPS = 6

relax_weight = 0.8
vertical_ratio = 0.5
sea_penalty = 2.0
river_penalty = 0.5
river_head = 1.0
recharge_rate = 1.0
courant = 0.45
freshening = 1.0

def padded_2(array, sides, width):
    for axis, dim in sides:
        count, length = (lax.axis_size(axis), array.shape[dim])
        up = [(i, (i + 1) % count) for i in range(count - 1)]
        down = [(j, i) for i, j in up]
        last = lax.slice_in_dim(array, length - width, length, axis=dim)
        first = lax.slice_in_dim(array, 0, width, axis=dim)
        before = lax.ppermute(last, axis, up)
        after = lax.ppermute(first, axis, down)
        array = jnp.concatenate([before, array, after], axis=dim)
    return array

def harmonic(first, second):
    total = first + second
    return 2.0 * first * second / (total + jnp.where(total > 0, 0.0, 1.0))

def coefficients(padded, penalty, vertical_scale):
    inner = padded[:, 1:-1, :]
    y_low = harmonic(inner, padded[:, :-2, :])
    y_high = harmonic(inner, padded[:, 2:, :])
    x_face = harmonic(inner[:, :, :-1], inner[:, :, 1:])
    zero_col = jnp.zeros_like(inner[:, :, :1])
    x_low = jnp.concatenate([zero_col, x_face], axis=2)
    x_high = jnp.concatenate([x_face, zero_col], axis=2)
    z_face = vertical_scale * vertical_ratio * harmonic(inner[:-1], inner[1:])
    zero_layer = jnp.zeros_like(inner[:1])
    z_up = jnp.concatenate([zero_layer, z_face], axis=0)
    z_down = jnp.concatenate([z_face, zero_layer], axis=0)
    top_term = jnp.concatenate([penalty[None], jnp.zeros_like(inner[1:])], axis=0)
    diagonal = x_low + x_high + y_low + y_high + z_up + z_down + top_term
    return (x_low, x_high, y_low, y_high, z_up, z_down, diagonal)

def neighbors(padded):
    center = padded[:, 1:-1, :]
    zero_col = jnp.zeros_like(center[:, :, :1])
    west = jnp.concatenate([zero_col, center[:, :, :-1]], axis=2)
    east = jnp.concatenate([center[:, :, 1:], zero_col], axis=2)
    zero_layer = jnp.zeros_like(center[:1])
    upper = jnp.concatenate([zero_layer, center[:-1]], axis=0)
    lower = jnp.concatenate([center[1:], zero_layer], axis=0)
    return (center, west, east, padded[:, :-2, :], padded[:, 2:, :], upper, lower)

def apply_operator(padded, coeffs):
    center, west, east, south, north, upper, lower = neighbors(padded)
    x_low, x_high, y_low, y_high, z_up, z_down, diagonal = coeffs
    return (
        diagonal * center
        - x_low * west
        - x_high * east
        - y_low * south
        - y_high * north
        - z_up * upper
        - z_down * lower
    )

def relax(padded, coeffs, right_side):
    return (
        padded[:, 1:-1, :]
        + relax_weight * (right_side - apply_operator(padded, coeffs)) / coeffs[6]
    )

def block_mean(field):
    leading = field.shape[:-2]
    count_a, count_b = field.shape[-2:]
    grouped = field.reshape(leading + (count_a // 4, 4, count_b // 4, 4))
    return jnp.sum(grouped, axis=(-3, -1)) * 0.0625

def pair_sum(field):
    leading = field.shape[:-2]
    count_a, count_b = field.shape[-2:]
    grouped = field.reshape(leading + (count_a // 2, 2, count_b // 2, 2))
    return jnp.sum(grouped, axis=(-3, -1))

def upsample(field, factor):
    return jnp.repeat(jnp.repeat(field, factor, axis=-2), factor, axis=-1)

def minmod(first, second):
    return 0.5 * (jnp.sign(first) + jnp.sign(second)) * jnp.minimum(jnp.abs(first), jnp.abs(second))

def portion(field, start, stop, axis):
    return lax.slice_in_dim(field, start, stop, axis=axis)

def divergence(cells, speed, axis):
    length = cells.shape[axis]
    widths = [(0, 0)] * cells.ndim
    widths[axis] = (1, 1)
    padded = jnp.pad(cells, widths)
    steps_diff = portion(padded, 1, length + 2, axis) - portion(padded, 0, length + 1, axis)
    slope = minmod(portion(steps_diff, 0, length, axis), portion(steps_diff, 1, length + 1, axis))
    faces = 0.5 * (portion(speed, 0, length - 1, axis) + portion(speed, 1, length, axis))
    left = portion(cells, 0, length - 1, axis) + 0.5 * portion(slope, 0, length - 1, axis)
    right = portion(cells, 1, length, axis) - 0.5 * portion(slope, 1, length, axis)
    flux = jnp.pad(faces * jnp.where(faces > 0, left, right), widths)
    return portion(flux, 1, length + 1, axis) - portion(flux, 0, length, axis)

def divergence_x(extended, faces):
    steps_diff = extended[:, 1:] - extended[:, :-1]
    slope = minmod(steps_diff[:, :-1], steps_diff[:, 1:])
    cells = extended[:, 1:-1]
    left = cells[:, :-1] + 0.5 * slope[:, :-1]
    right = cells[:, 1:] - 0.5 * slope[:, 1:]
    flux = faces * jnp.where(faces > 0, left, right)
    return flux[:, 1:] - flux[:, :-1]

def velocities(padded, coeffs, above, below):
    center, west, east, south, north, upper, lower = neighbors(padded)
    x_low, x_high, y_low, y_high, z_up, z_down, diagonal = coeffs
    vel_x = 0.5 * (x_low * (west - center) + x_high * (center - east))
    vel_y = 0.5 * (y_low * (south - center) + y_high * (center - north))
    vel_z = 0.5 * (z_up * (upper - center + above) + z_down * (center - lower + below))
    return (vel_z, vel_x, vel_y)

def buoyancy_terms(salt_coarse):
    face_salt = 0.5 * (salt_coarse[:-1] + salt_coarse[1:])
    zero_layer = jnp.zeros_like(salt_coarse[:1])
    above = jnp.concatenate([zero_layer, face_salt], axis=0)
    below = jnp.concatenate([face_salt, zero_layer], axis=0)
    return (above, below)

def boundary_penalty(codes):
    return jnp.where(codes == 1, sea_penalty, 0.0) + jnp.where(codes == 2, river_penalty, 0.0)

def source_terms(coeffs, above, below, recharge_frac, codes):
    top_source = recharge_rate * recharge_frac + river_head * jnp.where(
        codes == 2, river_penalty, 0.0
    )
    surface = jnp.concatenate([top_source[None], jnp.zeros_like(above[1:])], axis=0)
    return coeffs[4] * above - coeffs[5] * below + surface

def local_shared(salt, recharge, conductivity, codes):
    layers = salt.shape[0]
    tile = salt.shape[1]
    wet = recharge.astype(jnp.float32)
    blocks = jnp.concatenate([block_mean(salt), block_mean(wet)[None]], axis=0)
    owned = lax.all_to_all(
        jnp.transpose(blocks, (0, 2, 1)), "gx", split_axis=1, concat_axis=2, tiled=True
    )
    salt_coarse = owned[:layers]
    recharge_frac = owned[layers]
    penalty = boundary_penalty(codes)
    cond_padded = padded_2(conductivity, (("gx", 1),), 1)
    coeffs = coefficients(cond_padded, penalty, 1.0)
    above, below = buoyancy_terms(salt_coarse)
    right_side = source_terms(coeffs, above, below, recharge_frac, codes)
    coarse_cond = 0.25 * pair_sum(conductivity)
    coarse_pen = pair_sum(penalty)
    coarse_padded = padded_2(coarse_cond, (("gx", 1),), 1)
    coarse_coeffs = coefficients(coarse_padded, coarse_pen, 4.0)

    def smooth(current):
        padded = padded_2(current, (("gx", 1),), 1)
        return relax(padded, coeffs, right_side)

    head = jnp.zeros_like(conductivity)
    for cycle_no in range(CYCLES):
        for sweep in range(SMOOTH):
            head = smooth(head)
        head_padded = padded_2(head, (("gx", 1),), 1)
        residual = right_side - apply_operator(head_padded, coeffs)
        coarse_resid = pair_sum(residual)
        correction = jnp.zeros_like(coarse_resid)
        for sweep in range(COARSE_SWEEPS):
            corr_padded = padded_2(correction, (("gx", 1),), 1)
            correction = relax(corr_padded, coarse_coeffs, coarse_resid)
        head = head + upsample(correction, 2)
        for sweep in range(SMOOTH):
            head = smooth(head)
    final_padded = padded_2(head, (("gx", 1),), 1)
    vel_z, vel_x, vel_y = velocities(final_padded, coeffs, above, below)
    local_fastest = jnp.max(jnp.abs(vel_x) + jnp.abs(vel_y) + jnp.abs(vel_z))
    fastest = lax.pmax(local_fastest, "gx")
    step = courant / (fastest + 1e-06)
    packed = jnp.stack([vel_z, vel_x, vel_y])
    returned = jnp.transpose(
        lax.all_to_all(packed, "gx", split_axis=3, concat_axis=2, tiled=True), (0, 1, 3, 2)
    )
    fine_x = upsample(returned[1], 4)
    both = padded_2(jnp.stack([salt, fine_x]), (("gx", 2),), 2)
    extended = both[0]
    inner_x = both[1][:, 1:-1]
    faces = 0.5 * (inner_x[:, :-1] + inner_x[:, 1:])
    position = jnp.arange(tile + 1)
    device = lax.axis_index("gx")
    final_device = lax.axis_size("gx") - 1
    edge = (position == 0) & (device == 0) | (position == tile) & (device == final_device)
    faces = jnp.where(edge[None, :, None], 0.0, faces)
    fine_z = upsample(returned[0], 4)
    fine_y = upsample(returned[2], 4)
    change = (
        divergence(salt, fine_z, 0) + divergence_x(extended, faces) + divergence(salt, fine_y, 2)
    )
    dilution = jnp.concatenate(
        [(freshening * wet * salt[0])[None], jnp.zeros_like(salt[1:])], axis=0
    )
    tendency = -step * change - step * dilution
    return (tendency, head)

def split_dot(values, table, terms=3):
    rows = values.shape[0]
    parts = []
    for _ in range(terms):
        parts.append(values.astype(jnp.bfloat16))
        values = values - parts[-1].astype(jnp.float32)
    out = jnp.dot(jnp.concatenate(parts, axis=0), table, preferred_element_type=jnp.float32)
    return sum(out[rows * i : rows * (i + 1)] for i in range(1, terms)) + out[:rows]

def table_of(shape, same):
    row = lax.broadcasted_iota(jnp.int32, shape, 0)
    col = lax.broadcasted_iota(jnp.int32, shape, 1)
    return jnp.where(same(row, col), 1.0, 0.0).astype(jnp.bfloat16)

def iotas(shape):
    return lax.broadcasted_iota(jnp.int32, shape, 0), lax.broadcasted_iota(jnp.int32, shape, 1)

MAIN, SMALL, COLUMNS = 16, 8, 32
ROUNDS = ((9, 3, 5, 1), (3, 9, 5, 1))

def odd_ones(device):
    return ((device ^ (device >> 1) ^ (device >> 2) ^ (device >> 3)) & 1) == 1

def pack_kernel(salt_ref, recharge_ref, cond_ref, codes_ref, block_ref, inner_ref, relay_ref, kept_ref, wet_ref, flat_ref, turn_ref):
    kept_ref[...] = salt_ref[...]
    wet_ref[...] = recharge_ref[...]
    device = lax.axis_index("gx")
    even = (device & 1) == 0
    for j in range(2):
        first = salt_ref[:, j, :]
        last = salt_ref[:, 6 + j, :]
        inward = jnp.where(even, last, first)
        outward = jnp.where(even, first, last)
        for half in range(2):
            place = 8 * (2 * j + half)
            inner_ref[place : place + 8, :] = inward[:, 128 * half : 128 * half + 128]
            place = place + MAIN + SMALL
            block_ref[place : place + 8, :] = outward[:, 128 * half : 128 * half + 128]
    relay = jnp.where(odd_ones(device), jnp.where((device == 2) | (device == 13), 1.0, 0.0), 2.0)
    relay_ref[...] = jnp.broadcast_to(relay, (8, 128))
    turned = device >> 1
    sums = table_of((256, 128), lambda r, c: (r >> 2) == ((c >> 3) << 2) + (((c - turned) & 7) >> 1))
    for i in range(8):
        four = salt_ref[i] + pltpu.roll(salt_ref[i], 7, 0)
        four = four + pltpu.roll(four, 6, 0)
        flat_ref[0, 8 * i : 8 * i + 8, :] = four[:, 0:128]
        flat_ref[1, 8 * i : 8 * i + 8, :] = four[:, 128:256]
    rows = [
        jnp.concatenate([flat_ref[half, pl.ds(start, 8, stride=8), :] for half in range(2)], axis=1) for start in (0, 4)
    ]
    means = split_dot(jnp.concatenate(rows, axis=0), sums) * 0.0625
    sub, lane = iotas((8, 128))
    mine = (sub >> 2) == ((lane - turned) & 1)
    block_ref[0:8, :] = jnp.where(((lane - turned) & 1) == 0, means[0:8], means[8:16])
    wet_y = jnp.dot(
        recharge_ref[...].astype(jnp.float32).astype(jnp.bfloat16), sums, preferred_element_type=jnp.float32
    )
    wet_row = jnp.sum(jnp.where(mine, wet_y, 0.0), axis=0, keepdims=True) * 0.0625
    for layer in range(8):
        turn_ref[4 * layer : 4 * layer + 4, 0:32] = cond_ref[layer]
    spread = table_of((32, 128), lambda r, c: r == ((c & 7) << 2) + (((c >> 3) - device) & 3))
    turn_ref[...] = split_dot(turn_ref[:, 0:32], spread)
    packed = jnp.zeros((8, 128), jnp.float32)
    for j in range(4):
        packed = jnp.where(((((lane >> 3) - device) & 15) >> 2) == j, turn_ref[pl.ds(j, 8, stride=4), :], packed)
    block_ref[8:16, :] = packed
    codes = codes_ref[...]
    penalty = jnp.where(codes == 1, sea_penalty, 0.0) + jnp.where(codes == 2, river_penalty, 0.0)
    penalty_x = jnp.dot(penalty.astype(jnp.bfloat16), spread, preferred_element_type=jnp.float32)
    row4, lane4 = iotas((4, 128))
    penalty_row = jnp.sum(jnp.where(row4 == ((((lane4 >> 3) - device) & 15) >> 2), penalty_x, 0.0), axis=0, keepdims=True)
    slot = (device & 2) + ((device & 8) >> 1)
    block_ref[16:24, :] = jnp.where(sub == slot, wet_row, jnp.where(sub == slot + 1, penalty_row, 0.0))

def harm(first, second):
    return 2.0 * first * second / (first + second)

def slope_of(back, ahead):
    return jnp.maximum(jnp.minimum(back, ahead), 0.0) + jnp.minimum(jnp.maximum(back, ahead), 0.0)

def east_of(cells, k, side):
    return cells[k + 1] if k % side < side - 1 else pltpu.roll(cells[k + 1 - side], 127, 1)

def west_of(cells, k, side):
    return cells[k - 1] if k % side > 0 else pltpu.roll(cells[k - 1 + side], 1, 1)

def north_of(cells, k, side):
    return cells[k + side] if k < side * (side - 1) else pltpu.roll(cells[k % side], 120, 1)

def south_of(cells, k, side):
    return cells[k - side] if k >= side else pltpu.roll(cells[k + side * (side - 1)], 8, 1)

def upper_of(cell):
    return pltpu.roll(cell, 1, 0)

def lower_of(cell):
    return pltpu.roll(cell, 7, 0)

def sides_kernel(salt_ref, recharge_ref, side_ref, dilution_ref):
    layer, column = iotas((8, 256))
    cells = [salt_ref[:, x, :] for x in range(8)]
    for x in range(8):
        cell = cells[x]
        wet = recharge_ref[x : x + 1, :].astype(jnp.float32)
        dilution_ref[x] = jnp.where(layer == 0, freshening * wet * cell, 0.0)
        ahead = jnp.where(layer < 7, lower_of(cell), 0.0) - cell
        half = 0.5 * slope_of(jnp.where(layer > 0, upper_of(ahead), cell), ahead)
        side_ref[0, x] = cell + half
        side_ref[1, x] = lower_of(cell - half)
        ahead = jnp.where(column < 255, pltpu.roll(cell, 255, 1), 0.0) - cell
        half = 0.5 * slope_of(jnp.where(column > 0, pltpu.roll(ahead, 1, 1), cell), ahead)
        side_ref[2, x] = cell + half
        side_ref[3, x] = pltpu.roll(cell - half, 255, 1)
        side_ref[4, x] = pltpu.roll(cell + half, 1, 1)
        side_ref[5, x] = cell - half
        if 0 < x < 7:
            half = 0.5 * slope_of(cell - cells[x - 1], cells[x + 1] - cell)
            side_ref[6, x] = cell + half
            side_ref[7, x] = cell - half

def step_kernel(
    near_ref, far_ref, first_ref, second_ref, side_ref, dilution_ref, salt_ref, tendency_ref, head_ref, fine_ref, coarse_ref, ring_ref, wide_ref
):
    device = lax.axis_index("gx")
    sub, lane = iotas((8, 128))
    top = sub == 0
    even = (device & 1) == 0
    odd = odd_ones(device)
    orders = [lambda e: ((e >> 3) & 1) + (e & 2) + (e & 4), lambda e: ((e >> 1) & 1) + ((e & 8) >> 2) + (e & 4)]
    here = jnp.where(odd, orders[1](device), orders[0](device))
    there = jnp.where(odd, orders[0](device), orders[1](device))
    flip = (device & 4) != 0
    small = []
    for ref in (near_ref, far_ref):
        halves = [ref[8 * MAIN + SMALL * i : 8 * MAIN + SMALL * (i + 1), :] for i in range(2)]
        small.append([jnp.where(flip, halves[1 - i], halves[i]) for i in range(2)])
    means, conds, smalls = [], [], []
    for e in range(16):
        mine = odd == (bin(e).count("1") % 2 == 1)
        if e % 2 == 0:
            start = pl.multiple_of((here ^ jnp.where(odd, orders[1](e), orders[0](e))) * MAIN, 8)
            near = [near_ref[pl.ds(start, 8), :], near_ref[pl.ds(pl.multiple_of(start + 8, 8), 8), :]]
            start = pl.multiple_of((there ^ jnp.where(odd, orders[0](e), orders[1](e))) * MAIN, 8)
            far = [far_ref[pl.ds(start, 8), :], far_ref[pl.ds(pl.multiple_of(start + 8, 8), 8), :]]
        means.append(jnp.where(mine, near[0], far[0]))
        conds.append(jnp.where(mine, near[1], far[1]))
        smalls.append(jnp.where(mine, small[0][(e >> 2) & 1], small[1][(e >> 2) & 1]))

    slots = [2 * ((e // 2) % 2) + 4 * (e // 8) for e in range(16)]
    wets = [smalls[e][slots[e] : slots[e] + 1] for e in range(16)]
    penalties = [smalls[e][slots[e] + 1 : slots[e] + 2] for e in range(16)]

    def diagonals(fields, index):
        count = len(fields)
        bit = 1
        while bit < count:
            high = (index & bit) != 0
            fields = [jnp.where(high, fields[(m + bit) % count], fields[m]) for m in range(count)]
            bit *= 2
        return fields

    def by_block(fields):
        group = lane[0 : fields[0].shape[0]] >> 3
        picked = diagonals(fields, group)
        return [pltpu.roll(picked[-k % 16], (128 - 8 * k) % 128, 1) for k in range(16)]

    def by_lane(fields):
        within = lane & 7
        out = []
        picked = diagonals(fields, within)
        for s in range(8):
            here = picked[-s % 8]
            if s > 0:
                here = jnp.where(within < 8 - s, pltpu.roll(here, 128 - s, 1), pltpu.roll(here, 8 - s, 1))
            out.append(here)
        return out

    cond = by_block(conds)
    penalties = by_block(penalties)
    salt = [None] * 16
    wet_frac = [None] * 16
    wet_pairs = by_lane([jnp.where(top, wets[2 * b], wets[2 * b + 1]) for b in range(8)])
    for half in range(2):
        columns = by_lane(means[half::2])
        for s in range(8):
            k = 4 * (s // 2) + 2 * half + s % 2
            salt[k] = columns[s]
            wet_frac[k] = wet_pairs[s] if half == 0 else lower_of(wet_pairs[s])

    def coefficients(cells, penalty, side, vertical, weight_ref):
        face_w, face_e, face_s, face_n, face_d = [], [], [], [], []
        for k in range(side * side):
            e = harm(cells[k], east_of(cells, k, side))
            if k % side == side - 1:
                e = jnp.where((lane & 7) < 7, e, 0.0)
            n = harm(cells[k], north_of(cells, k, side))
            if k >= side * (side - 1):
                n = jnp.where(lane < 120, n, 0.0)
            w = face_e[k - 1] if k % side > 0 else None
            if w is None:
                w = jnp.where((lane & 7) > 0, harm(west_of(cells, k, side), cells[k]), 0.0)
            s = face_n[k - side] if k >= side else None
            if s is None:
                s = jnp.where(lane >= 8, harm(south_of(cells, k, side), cells[k]), 0.0)
            face_w.append(w)
            face_e.append(e)
            face_s.append(s)
            face_n.append(n)
            face_d.append(jnp.where(sub < 7, vertical * harm(cells[k], lower_of(cells[k])), 0.0))
        weights = []
        for k in range(side * side):
            six = (face_w[k], face_e[k], face_s[k], face_n[k], upper_of(face_d[k]), face_d[k])
            diag = six[0] + six[1] + six[2] + six[3] + six[4] + six[5] + penalty[k]
            weight = relax_weight / diag
            for number, face in enumerate(six):
                weight_ref[number, k] = weight * face
            weight_ref[6, k] = diag * (1.0 / relax_weight)
            weight_ref[7, k] = weight
            weights.append(weight)
        return (face_w, face_e, face_s, face_n, face_d), weights

    def step(here, west, east, south, north, weights):
        pairs = (west, east, south, north, upper_of(here), lower_of(here))
        terms = [weights(number) * pair for number, pair in enumerate(pairs)]
        base = (1.0 - relax_weight) * here + weights(8)
        return ((terms[0] + terms[1]) + (terms[2] + terms[3])) + ((terms[4] + terms[5]) + base)

    def edges_of(cells):
        return (
            [pltpu.roll(cells[4 * j + 3], 1, 1) for j in range(4)],
            [pltpu.roll(cells[4 * j], 127, 1) for j in range(4)],
            [pltpu.roll(cells[12 + i], 8, 1) for i in range(4)],
            [pltpu.roll(cells[i], 120, 1) for i in range(4)],
        )

    def relaxed(cells, edges):
        out = []
        for k in range(16):
            j, i = k // 4, k % 4
            west = cells[k - 1] if i > 0 else edges[0][j]
            east = cells[k + 1] if i < 3 else edges[1][j]
            south = cells[k - 4] if j > 0 else edges[2][i]
            north = cells[k + 4] if j < 3 else edges[3][i]
            out.append(step(cells[k], west, east, south, north, lambda number, k=k: fine_ref[number, k]))
        return out

    ring = [(j, i) for j in range(-1, 3) for i in range(-1, 3) if (j in (0, 1)) != (i in (0, 1))]

    def beyond(cells, j, i):
        shift = -(8 * (j // 2) + i // 2) % 128
        cell = cells[2 * (j % 2) + i % 2]
        return pltpu.roll(cell, shift, 1) if shift else cell

    def relaxed_around(cells):
        old, new = {}, {}

        def at(j, i):
            if (j, i) not in old:
                old[j, i] = beyond(cells, j, i)
            return old[j, i]

        for j, i in ring + [(0, 0), (0, 1), (1, 0), (1, 1)]:
            if (j, i) in ring:
                weights = lambda number, q=ring.index((j, i)): ring_ref[number, q]
            else:
                weights = lambda number, k=2 * j + i: coarse_ref[number, k]
            new[j, i] = step(at(j, i), at(j, i - 1), at(j, i + 1), at(j - 1, i), at(j + 1, i), weights)
        return new

    def relaxed_within(new):
        return [
            step(new[j, i], new[j, i - 1], new[j, i + 1], new[j - 1, i], new[j + 1, i],
                 lambda number, k=2 * j + i: coarse_ref[number, k])
            for j in range(2) for i in range(2)
        ]

    def pair_sums(cells):
        return [(cells[k] + cells[k + 1]) + (cells[k + 4] + cells[k + 5]) for k in (0, 2, 8, 10)]

    penalty, river = [], []
    for k in range(16):
        penalty.append(jnp.where(top, penalties[k], 0.0))
        river.append(jnp.where(penalties[k] == river_penalty, river_penalty, 0.0))
    faces, weights = coefficients(cond, penalty, 4, vertical_ratio, fine_ref)
    for k in range(16):
        below = jnp.where(sub < 7, 0.5 * (salt[k] + lower_of(salt[k])), 0.0)
        pull = faces[4][k] * below
        source = jnp.where(top, recharge_rate * wet_frac[k] + river_head * river[k], 0.0)
        fine_ref[8, k] = weights[k] * (upper_of(pull) - pull + source)
        fine_ref[9, k] = below
        for number, face in enumerate(faces):
            fine_ref[10 + number, k] = face[k]
    coefficients([0.25 * c for c in pair_sums(cond)], pair_sums(penalty), 2, 4.0 * vertical_ratio, coarse_ref)
    for number in range(6):
        cells = [coarse_ref[number, k] for k in range(4)]
        for q, (j, i) in enumerate(ring):
            ring_ref[number, q] = beyond(cells, j, i)

    head = None
    for cycle_no in range(CYCLES):
        for sweep in range(SMOOTH):
            head = [fine_ref[8, k] for k in range(16)] if head is None else relaxed(head, edges_of(head))
        edges = edges_of(head)
        ahead = relaxed(head, edges)
        resid = pair_sums([(ahead[k] - head[k]) * fine_ref[6, k] for k in range(16)])
        correction = []
        for k in range(4):
            correction.append(coarse_ref[7, k] * resid[k])
            coarse_ref[8, k] = correction[k]
        for q, (j, i) in enumerate(ring):
            ring_ref[8, q] = beyond(correction, j, i)
        sweeps = COARSE_SWEEPS - 1
        while sweeps > 0:
            around = relaxed_around(correction)
            correction = [around[k // 2, k % 2] for k in range(4)]
            sweeps -= 1
            if sweeps > 0:
                correction = relaxed_within(around)
                around = None
                sweeps -= 1
        if around is None:
            around = {place: beyond(correction, *place) for place in ring}
        head = [head[k] + correction[2 * (k // 8) + (k % 4) // 2] for k in range(16)]
        edges = (
            [edges[0][n] + around[n // 2, -1] for n in range(4)],
            [edges[1][n] + around[n // 2, 2] for n in range(4)],
            [edges[2][n] + around[-1, n // 2] for n in range(4)],
            [edges[3][n] + around[2, n // 2] for n in range(4)],
        )
        for sweep in range(SMOOTH):
            head = relaxed(head, edges_of(head) if edges is None else edges)
            edges = None

    largest = None
    for k in range(16):
        here = head[k]
        west, east = west_of(head, k, 4) - here, here - east_of(head, k, 4)
        south, north = south_of(head, k, 4) - here, here - north_of(head, k, 4)
        vel_x = 0.5 * (fine_ref[10, k] * west + fine_ref[11, k] * east)
        vel_y = 0.5 * (fine_ref[12, k] * south + fine_ref[13, k] * north)
        flow_d = fine_ref[14, k] * (here - lower_of(here) + fine_ref[9, k])
        vel_z = 0.5 * (upper_of(flow_d) + flow_d)
        wide_ref[0, k] = vel_x
        wide_ref[1, k] = vel_y
        wide_ref[2, k] = vel_z
        speed = jnp.abs(vel_x) + jnp.abs(vel_y) + jnp.abs(vel_z)
        largest = speed if largest is None else jnp.maximum(largest, speed)
    step = courant / (jnp.max(largest, axis=(0, 1), keepdims=True) + 1e-06)

    def along(field, x, beside=False):
        halves = []
        for half in range(2):
            y = 128 * half + lane
            if beside:
                y = jnp.clip(y + jnp.where((lane & 3) == 3, 1, jnp.where((lane & 3) == 0, -1, 0)), 0, 255)
            y = y >> 2
            source = ((y >> 2) << 3) + (x >> 2)
            part = jnp.take_along_axis(wide_ref[field, x & 3], source, axis=1)
            for j in range(1, 4):
                part = jnp.where((y & 3) == j, jnp.take_along_axis(wide_ref[field, 4 * j + (x & 3)], source, axis=1), part)
            halves.append(part)
        return jnp.concatenate(halves, axis=1)

    xs = [jnp.clip(2 * device - 1 + j, 0, 31) for j in range(4)]
    speed_x = [along(0, x) for x in xs]
    speed_z = [along(2, x) for x in xs[1:3]]
    speed_y = [along(1, x) for x in xs[1:3]]
    beside_y = [along(1, x, True) for x in xs[1:3]]

    layer, column = iotas((8, 256))
    crossed = device ^ jnp.where(even, device - 1, device + 1)
    halo = []
    for i in range(4):
        parts = []
        for half in range(2):
            place = 8 * (2 * i + half)
            here = 8 * (MAIN + 2) + place
            part = far_ref[here : here + 8, :]
            if i < 2:
                start = MAIN + SMALL + place
                straight = first_ref[start : start + 8, :]
                straight = jnp.where(odd, straight, second_ref[MAIN + start : MAIN + start + 8, :])
                part = jnp.where(crossed == 7, part, jnp.where(crossed == 15, near_ref[here : here + 8, :], 0.0))
                part = jnp.where(crossed == 3, straight, part)
            parts.append(part)
        halo.append(jnp.concatenate(parts, axis=1))
    cells = (
        [jnp.where(even, halo[j], halo[2 + j]) for j in range(2)]
        + [salt_ref[:, x, :] for x in range(8)]
        + [jnp.where(even, halo[2 + j], halo[j]) for j in range(2)]
    )
    lower, upper = {}, {}
    for x in (-1, 0, 7, 8):
        cell = cells[x + 2]
        half = 0.5 * slope_of(cell - cells[x + 1], cells[x + 3] - cell)
        lower[x], upper[x] = cell + half, cell - half
    for x in range(1, 7):
        lower[x], upper[x] = side_ref[6, x], side_ref[7, x]
    flux_x = []
    for f in range(9):
        if f % 4 == 0:
            face = 0.5 * (speed_x[f // 4] + speed_x[f // 4 + 1])
            if f == 0:
                face = jnp.where(device == 0, 0.0, face)
            if f == 8:
                face = jnp.where(device == 15, 0.0, face)
        else:
            face = speed_x[1 + f // 4]
        flux_x.append(face * jnp.where(face > 0, lower[f - 1], upper[f]))
    faces_z = [jnp.where(layer < 7, 0.5 * (v + pltpu.roll(v, 7, 0)), 0.0) for v in speed_z]
    between = [0.5 * (v + beside) for v, beside in zip(speed_y, beside_y)]
    faces_n = [jnp.where((column & 3) == 3, b, v) for v, b in zip(speed_y, between)]
    faces_n = [jnp.where(column < 255, face, 0.0) for face in faces_n]
    faces_s = [jnp.where((column & 3) == 0, b, v) for v, b in zip(speed_y, between)]
    faces_s = [jnp.where(column > 0, face, 0.0) for face in faces_s]
    for x in range(8):
        face = faces_z[x // 4]
        flux_z = face * jnp.where(face > 0, side_ref[0, x], side_ref[1, x])
        change = flux_z - upper_of(flux_z)
        change = change + (flux_x[x + 1] - flux_x[x])
        face = faces_n[x // 4]
        flux_n = face * jnp.where(face > 0, side_ref[2, x], side_ref[3, x])
        face = faces_s[x // 4]
        flux_s = face * jnp.where(face > 0, side_ref[4, x], side_ref[5, x])
        change = change + (flux_n - flux_s)
        tendency_ref[:, x, :] = -step * (change + dilution_ref[x])

    own = 8 * device + ((lane & 31) >> 2)
    for j in range(4):
        row = jnp.take_along_axis(head[4 * j], own, axis=1)
        for i in range(1, 4):
            row = jnp.where((lane & 3) == i, jnp.take_along_axis(head[4 * j + i], own, axis=1), row)
        head_ref[:, j, :] = row[:, 0:32]

def local_small(salt, recharge, conductivity, codes):
    vmem = pl.BlockSpec(memory_space=pltpu.VMEM)
    block, inner, relay, kept, wet = pl.pallas_call(
        pack_kernel,
        out_shape=(
            pltpu.VMEM((MAIN + SMALL + COLUMNS, 128), jnp.float32),
            pltpu.VMEM((COLUMNS, 128), jnp.float32),
            pltpu.VMEM((8, 128), jnp.float32),
            pltpu.VMEM(salt.shape, jnp.float32),
            pltpu.VMEM(recharge.shape, jnp.int32),
        ),
        in_specs=[vmem] * 4,
        out_specs=(vmem,) * 5,
        scratch_shapes=[pltpu.VMEM((2, 64, 128), jnp.float32), pltpu.VMEM((32, 128), jnp.float32)],
        name="pack",
    )(salt, recharge, conductivity, codes)

    def swapped(array, turn):
        pairs = [(i, i ^ ROUNDS[bin(i).count("1") % 2][turn]) for i in range(lax.axis_size("gx"))]
        return lax.ppermute(array, "gx", pairs)

    def small(array, count):
        return array[count * MAIN : count * MAIN + SMALL]

    def columns(array, count):
        return array[count * MAIN + SMALL :]

    relay = jnp.tile(relay, (COLUMNS // 8, 1))
    first = swapped(block, 0)
    handed = jnp.where(relay > 1.5, columns(block, 1), columns(first, 1))
    block = jnp.concatenate([block[:MAIN], first[:MAIN], small(block, 1) + small(first, 1), handed])
    second = swapped(block, 1)
    handed = jnp.where(relay > 0.5, columns(second, 2), columns(first, 1))
    block = jnp.concatenate(
        [block[: 2 * MAIN], second[: 2 * MAIN], small(block, 2) + small(second, 2), handed]
    )
    other = swapped(block, 2)
    block = jnp.concatenate(
        [block[: 4 * MAIN], other[: 4 * MAIN], small(block, 4), small(other, 4), columns(other, 4), inner]
    )
    other = swapped(block, 3)
    sides, dilution = pl.pallas_call(
        sides_kernel,
        out_shape=(pltpu.VMEM((8, 8, 8, 256), jnp.float32), pltpu.VMEM((8, 8, 256), jnp.float32)),
        in_specs=[vmem] * 2,
        out_specs=(vmem,) * 2,
        cost_estimate=pl.CostEstimate(flops=1 << 20, bytes_accessed=1 << 20, transcendentals=0),
        name="sides",
    )(*(pltpu.with_memory_space_constraint(array, pltpu.VMEM) for array in (kept, wet)))
    return pl.pallas_call(
        step_kernel,
        out_shape=(
            jax.ShapeDtypeStruct(salt.shape, jnp.float32),
            jax.ShapeDtypeStruct(conductivity.shape, jnp.float32),
        ),
        in_specs=[vmem] * 7,
        out_specs=(vmem,) * 2,
        scratch_shapes=[
            pltpu.VMEM((15, 16, 8, 128), jnp.float32),
            pltpu.VMEM((9, 4, 8, 128), jnp.float32),
            pltpu.VMEM((9, 8, 8, 128), jnp.float32),
            pltpu.VMEM((3, 16, 8, 128), jnp.float32),
        ],
        compiler_params=pltpu.CompilerParams(vmem_limit_bytes=16 * 1024 * 1024),
        name="step",
    )(block, other, first, second, sides, dilution, kept)

def local(salt, recharge, conductivity, codes):
    small = (
        lax.axis_size("gx") == 16
        and salt.shape == (8, 8, 256)
        and recharge.shape == (8, 256)
        and conductivity.shape == (8, 4, 32)
        and codes.shape == (4, 32)
    )
    return (local_small if small else local_shared)(salt, recharge, conductivity, codes)

def solution(mesh):
    return jax.shard_map(
        local,
        mesh=mesh,
        in_specs=(
            P("parts", "gx", None),
            P("gx", "parts"),
            P("parts", "gx", None),
            P("gx", "parts"),
        ),
        out_specs=(P("parts", "gx", None), P("parts", "gx", None)),
        check_vma=False,
    )
```

```python
import jax
import jax.numpy as jnp
from jax import lax
from jax.experimental import pallas as pl
from jax.experimental.pallas import tpu as pltpu
from jax.sharding import PartitionSpec as P

CYCLES = 2
SMOOTH = 2
COARSE_SWEEPS = 6

relax_weight = 0.8
vertical_ratio = 0.5
sea_penalty = 2.0
river_penalty = 0.5
river_head = 1.0
recharge_rate = 1.0
courant = 0.45
freshening = 1.0

def padded_2(array, sides, width):
    for axis, dim in sides:
        count, length = (lax.axis_size(axis), array.shape[dim])
        up = [(i, (i + 1) % count) for i in range(count - 1)]
        down = [(j, i) for i, j in up]
        last = lax.slice_in_dim(array, length - width, length, axis=dim)
        first = lax.slice_in_dim(array, 0, width, axis=dim)
        before = lax.ppermute(last, axis, up)
        after = lax.ppermute(first, axis, down)
        array = jnp.concatenate([before, array, after], axis=dim)
    return array

def harmonic(first, second):
    total = first + second
    return 2.0 * first * second / (total + jnp.where(total > 0, 0.0, 1.0))

def coefficients(padded, penalty, vertical_scale):
    inner = padded[:, 1:-1, :]
    y_low = harmonic(inner, padded[:, :-2, :])
    y_high = harmonic(inner, padded[:, 2:, :])
    x_face = harmonic(inner[:, :, :-1], inner[:, :, 1:])
    zero_col = jnp.zeros_like(inner[:, :, :1])
    x_low = jnp.concatenate([zero_col, x_face], axis=2)
    x_high = jnp.concatenate([x_face, zero_col], axis=2)
    z_face = vertical_scale * vertical_ratio * harmonic(inner[:-1], inner[1:])
    zero_layer = jnp.zeros_like(inner[:1])
    z_up = jnp.concatenate([zero_layer, z_face], axis=0)
    z_down = jnp.concatenate([z_face, zero_layer], axis=0)
    top_term = jnp.concatenate([penalty[None], jnp.zeros_like(inner[1:])], axis=0)
    diagonal = x_low + x_high + y_low + y_high + z_up + z_down + top_term
    return (x_low, x_high, y_low, y_high, z_up, z_down, diagonal)

def neighbors(padded):
    center = padded[:, 1:-1, :]
    zero_col = jnp.zeros_like(center[:, :, :1])
    west = jnp.concatenate([zero_col, center[:, :, :-1]], axis=2)
    east = jnp.concatenate([center[:, :, 1:], zero_col], axis=2)
    zero_layer = jnp.zeros_like(center[:1])
    upper = jnp.concatenate([zero_layer, center[:-1]], axis=0)
    lower = jnp.concatenate([center[1:], zero_layer], axis=0)
    return (center, west, east, padded[:, :-2, :], padded[:, 2:, :], upper, lower)

def apply_operator(padded, coeffs):
    center, west, east, south, north, upper, lower = neighbors(padded)
    x_low, x_high, y_low, y_high, z_up, z_down, diagonal = coeffs
    return (
        diagonal * center
        - x_low * west
        - x_high * east
        - y_low * south
        - y_high * north
        - z_up * upper
        - z_down * lower
    )

def relax(padded, coeffs, right_side):
    return (
        padded[:, 1:-1, :]
        + relax_weight * (right_side - apply_operator(padded, coeffs)) / coeffs[6]
    )

def block_mean(field):
    leading = field.shape[:-2]
    count_a, count_b = field.shape[-2:]
    grouped = field.reshape(leading + (count_a // 4, 4, count_b // 4, 4))
    return jnp.sum(grouped, axis=(-3, -1)) * 0.0625

def pair_sum(field):
    leading = field.shape[:-2]
    count_a, count_b = field.shape[-2:]
    grouped = field.reshape(leading + (count_a // 2, 2, count_b // 2, 2))
    return jnp.sum(grouped, axis=(-3, -1))

def upsample(field, factor):
    return jnp.repeat(jnp.repeat(field, factor, axis=-2), factor, axis=-1)

def minmod(first, second):
    return 0.5 * (jnp.sign(first) + jnp.sign(second)) * jnp.minimum(jnp.abs(first), jnp.abs(second))

def portion(field, start, stop, axis):
    return lax.slice_in_dim(field, start, stop, axis=axis)

def divergence(cells, speed, axis):
    length = cells.shape[axis]
    widths = [(0, 0)] * cells.ndim
    widths[axis] = (1, 1)
    padded = jnp.pad(cells, widths)
    steps_diff = portion(padded, 1, length + 2, axis) - portion(padded, 0, length + 1, axis)
    slope = minmod(portion(steps_diff, 0, length, axis), portion(steps_diff, 1, length + 1, axis))
    faces = 0.5 * (portion(speed, 0, length - 1, axis) + portion(speed, 1, length, axis))
    left = portion(cells, 0, length - 1, axis) + 0.5 * portion(slope, 0, length - 1, axis)
    right = portion(cells, 1, length, axis) - 0.5 * portion(slope, 1, length, axis)
    flux = jnp.pad(faces * jnp.where(faces > 0, left, right), widths)
    return portion(flux, 1, length + 1, axis) - portion(flux, 0, length, axis)

def divergence_x(extended, faces):
    steps_diff = extended[:, 1:] - extended[:, :-1]
    slope = minmod(steps_diff[:, :-1], steps_diff[:, 1:])
    cells = extended[:, 1:-1]
    left = cells[:, :-1] + 0.5 * slope[:, :-1]
    right = cells[:, 1:] - 0.5 * slope[:, 1:]
    flux = faces * jnp.where(faces > 0, left, right)
    return flux[:, 1:] - flux[:, :-1]

def velocities(padded, coeffs, above, below):
    center, west, east, south, north, upper, lower = neighbors(padded)
    x_low, x_high, y_low, y_high, z_up, z_down, diagonal = coeffs
    vel_x = 0.5 * (x_low * (west - center) + x_high * (center - east))
    vel_y = 0.5 * (y_low * (south - center) + y_high * (center - north))
    vel_z = 0.5 * (z_up * (upper - center + above) + z_down * (center - lower + below))
    return (vel_z, vel_x, vel_y)

def buoyancy_terms(salt_coarse):
    face_salt = 0.5 * (salt_coarse[:-1] + salt_coarse[1:])
    zero_layer = jnp.zeros_like(salt_coarse[:1])
    above = jnp.concatenate([zero_layer, face_salt], axis=0)
    below = jnp.concatenate([face_salt, zero_layer], axis=0)
    return (above, below)

def boundary_penalty(codes):
    return jnp.where(codes == 1, sea_penalty, 0.0) + jnp.where(codes == 2, river_penalty, 0.0)

def source_terms(coeffs, above, below, recharge_frac, codes):
    top_source = recharge_rate * recharge_frac + river_head * jnp.where(
        codes == 2, river_penalty, 0.0
    )
    surface = jnp.concatenate([top_source[None], jnp.zeros_like(above[1:])], axis=0)
    return coeffs[4] * above - coeffs[5] * below + surface

def local_shared(salt, recharge, conductivity, codes):
    layers = salt.shape[0]
    tile = salt.shape[1]
    wet = recharge.astype(jnp.float32)
    blocks = jnp.concatenate([block_mean(salt), block_mean(wet)[None]], axis=0)
    owned = lax.all_to_all(
        jnp.transpose(blocks, (0, 2, 1)), "gx", split_axis=1, concat_axis=2, tiled=True
    )
    salt_coarse = owned[:layers]
    recharge_frac = owned[layers]
    penalty = boundary_penalty(codes)
    cond_padded = padded_2(conductivity, (("gx", 1),), 1)
    coeffs = coefficients(cond_padded, penalty, 1.0)
    above, below = buoyancy_terms(salt_coarse)
    right_side = source_terms(coeffs, above, below, recharge_frac, codes)
    coarse_cond = 0.25 * pair_sum(conductivity)
    coarse_pen = pair_sum(penalty)
    coarse_padded = padded_2(coarse_cond, (("gx", 1),), 1)
    coarse_coeffs = coefficients(coarse_padded, coarse_pen, 4.0)

    def smooth(current):
        padded = padded_2(current, (("gx", 1),), 1)
        return relax(padded, coeffs, right_side)

    head = jnp.zeros_like(conductivity)
    for cycle_no in range(CYCLES):
        for sweep in range(SMOOTH):
            head = smooth(head)
        head_padded = padded_2(head, (("gx", 1),), 1)
        residual = right_side - apply_operator(head_padded, coeffs)
        coarse_resid = pair_sum(residual)
        correction = jnp.zeros_like(coarse_resid)
        for sweep in range(COARSE_SWEEPS):
            corr_padded = padded_2(correction, (("gx", 1),), 1)
            correction = relax(corr_padded, coarse_coeffs, coarse_resid)
        head = head + upsample(correction, 2)
        for sweep in range(SMOOTH):
            head = smooth(head)
    final_padded = padded_2(head, (("gx", 1),), 1)
    vel_z, vel_x, vel_y = velocities(final_padded, coeffs, above, below)
    local_fastest = jnp.max(jnp.abs(vel_x) + jnp.abs(vel_y) + jnp.abs(vel_z))
    fastest = lax.pmax(local_fastest, "gx")
    step = courant / (fastest + 1e-06)
    packed = jnp.stack([vel_z, vel_x, vel_y])
    returned = jnp.transpose(
        lax.all_to_all(packed, "gx", split_axis=3, concat_axis=2, tiled=True), (0, 1, 3, 2)
    )
    fine_x = upsample(returned[1], 4)
    both = padded_2(jnp.stack([salt, fine_x]), (("gx", 2),), 2)
    extended = both[0]
    inner_x = both[1][:, 1:-1]
    faces = 0.5 * (inner_x[:, :-1] + inner_x[:, 1:])
    position = jnp.arange(tile + 1)
    device = lax.axis_index("gx")
    final_device = lax.axis_size("gx") - 1
    edge = (position == 0) & (device == 0) | (position == tile) & (device == final_device)
    faces = jnp.where(edge[None, :, None], 0.0, faces)
    fine_z = upsample(returned[0], 4)
    fine_y = upsample(returned[2], 4)
    change = (
        divergence(salt, fine_z, 0) + divergence_x(extended, faces) + divergence(salt, fine_y, 2)
    )
    dilution = jnp.concatenate(
        [(freshening * wet * salt[0])[None], jnp.zeros_like(salt[1:])], axis=0
    )
    tendency = -step * change - step * dilution
    return (tendency, head)

def split_dot(values, table, terms=3):
    rows = values.shape[0]
    parts = []
    for _ in range(terms):
        parts.append(values.astype(jnp.bfloat16))
        values = values - parts[-1].astype(jnp.float32)
    out = jnp.dot(jnp.concatenate(parts, axis=0), table, preferred_element_type=jnp.float32)
    return sum(out[rows * i : rows * (i + 1)] for i in range(1, terms)) + out[:rows]

def table_of(shape, same):
    row = lax.broadcasted_iota(jnp.int32, shape, 0)
    col = lax.broadcasted_iota(jnp.int32, shape, 1)
    return jnp.where(same(row, col), 1.0, 0.0).astype(jnp.bfloat16)

def iotas(shape):
    return lax.broadcasted_iota(jnp.int32, shape, 0), lax.broadcasted_iota(jnp.int32, shape, 1)

MAIN, SMALL, COLUMNS = 16, 8, 32
ROUNDS = ((9, 3, 5, 1), (3, 9, 5, 1))

def odd_ones(device):
    return ((device ^ (device >> 1) ^ (device >> 2) ^ (device >> 3)) & 1) == 1

def pack_kernel(salt_ref, recharge_ref, cond_ref, codes_ref, block_ref, inner_ref, relay_ref, kept_ref, wet_ref, flat_ref, turn_ref):
    kept_ref[...] = salt_ref[...]
    wet_ref[...] = recharge_ref[...]
    device = lax.axis_index("gx")
    even = (device & 1) == 0
    for j in range(2):
        first = salt_ref[:, j, :]
        last = salt_ref[:, 6 + j, :]
        inward = jnp.where(even, last, first)
        outward = jnp.where(even, first, last)
        for half in range(2):
            place = 8 * (2 * j + half)
            inner_ref[place : place + 8, :] = inward[:, 128 * half : 128 * half + 128]
            place = place + MAIN + SMALL
            block_ref[place : place + 8, :] = outward[:, 128 * half : 128 * half + 128]
    relay = jnp.where(odd_ones(device), jnp.where((device == 2) | (device == 13), 1.0, 0.0), 2.0)
    relay_ref[...] = jnp.broadcast_to(relay, (8, 128))
    turned = device >> 1
    sums = table_of((256, 128), lambda r, c: (r >> 2) == ((c >> 3) << 2) + (((c - turned) & 7) >> 1))
    for i in range(8):
        four = salt_ref[i] + pltpu.roll(salt_ref[i], 7, 0)
        four = four + pltpu.roll(four, 6, 0)
        flat_ref[0, 8 * i : 8 * i + 8, :] = four[:, 0:128]
        flat_ref[1, 8 * i : 8 * i + 8, :] = four[:, 128:256]
    rows = [
        jnp.concatenate([flat_ref[half, pl.ds(start, 8, stride=8), :] for half in range(2)], axis=1) for start in (0, 4)
    ]
    means = split_dot(jnp.concatenate(rows, axis=0), sums) * 0.0625
    sub, lane = iotas((8, 128))
    mine = (sub >> 2) == ((lane - turned) & 1)
    block_ref[0:8, :] = jnp.where(((lane - turned) & 1) == 0, means[0:8], means[8:16])
    wet_y = jnp.dot(
        recharge_ref[...].astype(jnp.float32).astype(jnp.bfloat16), sums, preferred_element_type=jnp.float32
    )
    wet_row = jnp.sum(jnp.where(mine, wet_y, 0.0), axis=0, keepdims=True) * 0.0625
    for layer in range(8):
        turn_ref[4 * layer : 4 * layer + 4, 0:32] = cond_ref[layer]
    spread = table_of((32, 128), lambda r, c: r == ((c & 7) << 2) + (((c >> 3) - device) & 3))
    turn_ref[...] = split_dot(turn_ref[:, 0:32], spread)
    packed = jnp.zeros((8, 128), jnp.float32)
    for j in range(4):
        packed = jnp.where(((((lane >> 3) - device) & 15) >> 2) == j, turn_ref[pl.ds(j, 8, stride=4), :], packed)
    block_ref[8:16, :] = packed
    codes = codes_ref[...]
    penalty = jnp.where(codes == 1, sea_penalty, 0.0) + jnp.where(codes == 2, river_penalty, 0.0)
    penalty_x = jnp.dot(penalty.astype(jnp.bfloat16), spread, preferred_element_type=jnp.float32)
    row4, lane4 = iotas((4, 128))
    penalty_row = jnp.sum(jnp.where(row4 == ((((lane4 >> 3) - device) & 15) >> 2), penalty_x, 0.0), axis=0, keepdims=True)
    slot = (device & 2) + ((device & 8) >> 1)
    block_ref[16:24, :] = jnp.where(sub == slot, wet_row, jnp.where(sub == slot + 1, penalty_row, 0.0))

def harm(first, second):
    return 2.0 * first * second / (first + second)

def slope_of(back, ahead):
    return jnp.maximum(jnp.minimum(back, ahead), 0.0) + jnp.minimum(jnp.maximum(back, ahead), 0.0)

def east_of(cells, k, side):
    return cells[k + 1] if k % side < side - 1 else pltpu.roll(cells[k + 1 - side], 127, 1)

def west_of(cells, k, side):
    return cells[k - 1] if k % side > 0 else pltpu.roll(cells[k - 1 + side], 1, 1)

def north_of(cells, k, side):
    return cells[k + side] if k < side * (side - 1) else pltpu.roll(cells[k % side], 120, 1)

def south_of(cells, k, side):
    return cells[k - side] if k >= side else pltpu.roll(cells[k + side * (side - 1)], 8, 1)

def upper_of(cell):
    return pltpu.roll(cell, 1, 0)

def lower_of(cell):
    return pltpu.roll(cell, 7, 0)

def sides_kernel(salt_ref, recharge_ref, side_ref, dilution_ref):
    layer, column = iotas((8, 256))
    cells = [salt_ref[:, x, :] for x in range(8)]
    for x in range(8):
        cell = cells[x]
        wet = recharge_ref[x : x + 1, :].astype(jnp.float32)
        dilution_ref[x] = jnp.where(layer == 0, freshening * wet * cell, 0.0)
        ahead = jnp.where(layer < 7, lower_of(cell), 0.0) - cell
        half = 0.5 * slope_of(jnp.where(layer > 0, upper_of(ahead), cell), ahead)
        side_ref[0, x] = cell + half
        side_ref[1, x] = lower_of(cell - half)
        ahead = jnp.where(column < 255, pltpu.roll(cell, 255, 1), 0.0) - cell
        half = 0.5 * slope_of(jnp.where(column > 0, pltpu.roll(ahead, 1, 1), cell), ahead)
        side_ref[2, x] = cell + half
        side_ref[3, x] = pltpu.roll(cell - half, 255, 1)
        side_ref[4, x] = pltpu.roll(cell + half, 1, 1)
        side_ref[5, x] = cell - half
        if 0 < x < 7:
            half = 0.5 * slope_of(cell - cells[x - 1], cells[x + 1] - cell)
            side_ref[6, x] = cell + half
            side_ref[7, x] = cell - half

def step_kernel(
    near_ref, far_ref, first_ref, second_ref, side_ref, dilution_ref, salt_ref, tendency_ref, head_ref, fine_ref, coarse_ref, ring_ref, wide_ref
):
    device = lax.axis_index("gx")
    sub, lane = iotas((8, 128))
    top = sub == 0
    even = (device & 1) == 0
    odd = odd_ones(device)
    orders = [lambda e: ((e >> 3) & 1) + (e & 2) + (e & 4), lambda e: ((e >> 1) & 1) + ((e & 8) >> 2) + (e & 4)]
    here = jnp.where(odd, orders[1](device), orders[0](device))
    there = jnp.where(odd, orders[0](device), orders[1](device))
    flip = (device & 4) != 0
    small = []
    for ref in (near_ref, far_ref):
        halves = [ref[8 * MAIN + SMALL * i : 8 * MAIN + SMALL * (i + 1), :] for i in range(2)]
        small.append([jnp.where(flip, halves[1 - i], halves[i]) for i in range(2)])
    means, conds, smalls = [], [], []
    for e in range(16):
        mine = odd == (bin(e).count("1") % 2 == 1)
        if e % 2 == 0:
            start = pl.multiple_of((here ^ jnp.where(odd, orders[1](e), orders[0](e))) * MAIN, 8)
            near = [near_ref[pl.ds(start, 8), :], near_ref[pl.ds(pl.multiple_of(start + 8, 8), 8), :]]
            start = pl.multiple_of((there ^ jnp.where(odd, orders[0](e), orders[1](e))) * MAIN, 8)
            far = [far_ref[pl.ds(start, 8), :], far_ref[pl.ds(pl.multiple_of(start + 8, 8), 8), :]]
        means.append(jnp.where(mine, near[0], far[0]))
        conds.append(jnp.where(mine, near[1], far[1]))
        smalls.append(jnp.where(mine, small[0][(e >> 2) & 1], small[1][(e >> 2) & 1]))

    slots = [2 * ((e // 2) % 2) + 4 * (e // 8) for e in range(16)]
    wets = [smalls[e][slots[e] : slots[e] + 1] for e in range(16)]
    penalties = [smalls[e][slots[e] + 1 : slots[e] + 2] for e in range(16)]

    def diagonals(fields, index):
        count = len(fields)
        bit = 1
        while bit < count:
            high = (index & bit) != 0
            fields = [jnp.where(high, fields[(m + bit) % count], fields[m]) for m in range(count)]
            bit *= 2
        return fields

    def by_block(fields):
        group = lane[0 : fields[0].shape[0]] >> 3
        picked = diagonals(fields, group)
        return [pltpu.roll(picked[-k % 16], (128 - 8 * k) % 128, 1) for k in range(16)]

    def by_lane(fields):
        within = lane & 7
        out = []
        picked = diagonals(fields, within)
        for s in range(8):
            here = picked[-s % 8]
            if s > 0:
                here = jnp.where(within < 8 - s, pltpu.roll(here, 128 - s, 1), pltpu.roll(here, 8 - s, 1))
            out.append(here)
        return out

    cond = by_block(conds)
    penalties = by_block(penalties)
    salt = [None] * 16
    wet_frac = [None] * 16
    wet_pairs = by_lane([jnp.where(top, wets[2 * b], wets[2 * b + 1]) for b in range(8)])
    for half in range(2):
        columns = by_lane(means[half::2])
        for s in range(8):
            k = 4 * (s // 2) + 2 * half + s % 2
            salt[k] = columns[s]
            wet_frac[k] = wet_pairs[s] if half == 0 else lower_of(wet_pairs[s])

    def coefficients(cells, penalty, side, vertical, weight_ref):
        face_w, face_e, face_s, face_n, face_d = [], [], [], [], []
        for k in range(side * side):
            e = harm(cells[k], east_of(cells, k, side))
            if k % side == side - 1:
                e = jnp.where((lane & 7) < 7, e, 0.0)
            n = harm(cells[k], north_of(cells, k, side))
            if k >= side * (side - 1):
                n = jnp.where(lane < 120, n, 0.0)
            w = face_e[k - 1] if k % side > 0 else None
            if w is None:
                w = jnp.where((lane & 7) > 0, harm(west_of(cells, k, side), cells[k]), 0.0)
            s = face_n[k - side] if k >= side else None
            if s is None:
                s = jnp.where(lane >= 8, harm(south_of(cells, k, side), cells[k]), 0.0)
            face_w.append(w)
            face_e.append(e)
            face_s.append(s)
            face_n.append(n)
            face_d.append(jnp.where(sub < 7, vertical * harm(cells[k], lower_of(cells[k])), 0.0))
        weights = []
        for k in range(side * side):
            six = (face_w[k], face_e[k], face_s[k], face_n[k], upper_of(face_d[k]), face_d[k])
            diag = six[0] + six[1] + six[2] + six[3] + six[4] + six[5] + penalty[k]
            weight = relax_weight / diag
            for number, face in enumerate(six):
                weight_ref[number, k] = weight * face
            weight_ref[6, k] = diag * (1.0 / relax_weight)
            if side == 2:
                weight_ref[7, k] = weight
            weights.append(weight)
        return (face_w, face_e, face_s, face_n, face_d), weights

    def step(here, west, east, south, north, weights):
        pairs = (west, east, south, north, upper_of(here), lower_of(here))
        terms = [weights(number) * pair for number, pair in enumerate(pairs)]
        base = (1.0 - relax_weight) * here + weights(8)
        return ((terms[0] + terms[1]) + (terms[2] + terms[3])) + ((terms[4] + terms[5]) + base)

    def edges_of(cells):
        return (
            [pltpu.roll(cells[4 * j + 3], 1, 1) for j in range(4)],
            [pltpu.roll(cells[4 * j], 127, 1) for j in range(4)],
            [pltpu.roll(cells[12 + i], 8, 1) for i in range(4)],
            [pltpu.roll(cells[i], 120, 1) for i in range(4)],
        )

    def relaxed(cells, edges):
        out = []
        for k in range(16):
            j, i = k // 4, k % 4
            west = cells[k - 1] if i > 0 else edges[0][j]
            east = cells[k + 1] if i < 3 else edges[1][j]
            south = cells[k - 4] if j > 0 else edges[2][i]
            north = cells[k + 4] if j < 3 else edges[3][i]
            out.append(step(cells[k], west, east, south, north, lambda number, k=k: fine_ref[number, k]))
        return out

    ring = [(j, i) for j in range(-1, 3) for i in range(-1, 3) if (j in (0, 1)) != (i in (0, 1))]

    def beyond(cells, j, i):
        shift = -(8 * (j // 2) + i // 2) % 128
        cell = cells[2 * (j % 2) + i % 2]
        return pltpu.roll(cell, shift, 1) if shift else cell

    def relaxed_around(cells):
        old, new = {}, {}

        def at(j, i):
            if (j, i) not in old:
                old[j, i] = beyond(cells, j, i)
            return old[j, i]

        for j, i in ring + [(0, 0), (0, 1), (1, 0), (1, 1)]:
            if (j, i) in ring:
                weights = lambda number, q=ring.index((j, i)): ring_ref[number, q]
            else:
                weights = lambda number, k=2 * j + i: coarse_ref[number, k]
            new[j, i] = step(at(j, i), at(j, i - 1), at(j, i + 1), at(j - 1, i), at(j + 1, i), weights)
        return new

    def relaxed_within(new):
        return [
            step(new[j, i], new[j, i - 1], new[j, i + 1], new[j - 1, i], new[j + 1, i],
                 lambda number, k=2 * j + i: coarse_ref[number, k])
            for j in range(2) for i in range(2)
        ]

    def pair_sums(cells):
        return [(cells[k] + cells[k + 1]) + (cells[k + 4] + cells[k + 5]) for k in (0, 2, 8, 10)]

    penalty, river = [], []
    for k in range(16):
        penalty.append(jnp.where(top, penalties[k], 0.0))
        river.append(jnp.where(penalties[k] == river_penalty, river_penalty, 0.0))
    faces, weights = coefficients(cond, penalty, 4, vertical_ratio, fine_ref)
    for k in range(16):
        below = jnp.where(sub < 7, 0.5 * (salt[k] + lower_of(salt[k])), 0.0)
        pull = faces[4][k] * below
        source = jnp.where(top, recharge_rate * wet_frac[k] + river_head * river[k], 0.0)
        fine_ref[8, k] = weights[k] * (upper_of(pull) - pull + source)
        fine_ref[7, k] = below
    coefficients([0.25 * c for c in pair_sums(cond)], pair_sums(penalty), 2, 4.0 * vertical_ratio, coarse_ref)
    for number in range(6):
        cells = [coarse_ref[number, k] for k in range(4)]
        for q, (j, i) in enumerate(ring):
            ring_ref[number, q] = beyond(cells, j, i)

    head = None
    for cycle_no in range(CYCLES):
        for sweep in range(SMOOTH):
            head = [fine_ref[8, k] for k in range(16)] if head is None else relaxed(head, edges_of(head))
        edges = edges_of(head)
        ahead = relaxed(head, edges)
        resid = pair_sums([(ahead[k] - head[k]) * fine_ref[6, k] for k in range(16)])
        correction = []
        for k in range(4):
            correction.append(coarse_ref[7, k] * resid[k])
            coarse_ref[8, k] = correction[k]
        for q, (j, i) in enumerate(ring):
            ring_ref[8, q] = beyond(correction, j, i)
        sweeps = COARSE_SWEEPS - 1
        while sweeps > 0:
            around = relaxed_around(correction)
            correction = [around[k // 2, k % 2] for k in range(4)]
            sweeps -= 1
            if sweeps > 0:
                correction = relaxed_within(around)
                around = None
                sweeps -= 1
        if around is None:
            around = {place: beyond(correction, *place) for place in ring}
        head = [head[k] + correction[2 * (k // 8) + (k % 4) // 2] for k in range(16)]
        edges = (
            [edges[0][n] + around[n // 2, -1] for n in range(4)],
            [edges[1][n] + around[n // 2, 2] for n in range(4)],
            [edges[2][n] + around[-1, n // 2] for n in range(4)],
            [edges[3][n] + around[2, n // 2] for n in range(4)],
        )
        for sweep in range(SMOOTH):
            head = relaxed(head, edges_of(head) if edges is None else edges)
            edges = None

    largest = None
    for k in range(16):
        here = head[k]
        west, east = west_of(head, k, 4) - here, here - east_of(head, k, 4)
        south, north = south_of(head, k, 4) - here, here - north_of(head, k, 4)
        scale = 0.5 * fine_ref[6, k]
        vel_x = scale * (fine_ref[0, k] * west + fine_ref[1, k] * east)
        vel_y = scale * (fine_ref[2, k] * south + fine_ref[3, k] * north)
        flow_d = scale * fine_ref[5, k] * (here - lower_of(here) + fine_ref[7, k])
        vel_z = upper_of(flow_d) + flow_d
        wide_ref[0, k] = vel_x
        wide_ref[1, k] = vel_y
        wide_ref[2, k] = vel_z
        speed = jnp.abs(vel_x) + jnp.abs(vel_y) + jnp.abs(vel_z)
        largest = speed if largest is None else jnp.maximum(largest, speed)
    step = courant / (jnp.max(largest, axis=(0, 1), keepdims=True) + 1e-06)

    def along(field, x, beside=False):
        halves = []
        for half in range(2):
            y = 128 * half + lane
            if beside:
                y = jnp.clip(y + jnp.where((lane & 3) == 3, 1, jnp.where((lane & 3) == 0, -1, 0)), 0, 255)
            y = y >> 2
            source = ((y >> 2) << 3) + (x >> 2)
            part = jnp.take_along_axis(wide_ref[field, x & 3], source, axis=1)
            for j in range(1, 4):
                part = jnp.where((y & 3) == j, jnp.take_along_axis(wide_ref[field, 4 * j + (x & 3)], source, axis=1), part)
            halves.append(part)
        return jnp.concatenate(halves, axis=1)

    xs = [jnp.clip(2 * device - 1 + j, 0, 31) for j in range(4)]
    speed_x = [along(0, x) for x in xs]
    speed_z = [along(2, x) for x in xs[1:3]]
    speed_y = [along(1, x) for x in xs[1:3]]
    beside_y = [along(1, x, True) for x in xs[1:3]]

    layer, column = iotas((8, 256))
    crossed = device ^ jnp.where(even, device - 1, device + 1)
    halo = []
    for i in range(4):
        parts = []
        for half in range(2):
            place = 8 * (2 * i + half)
            here = 8 * (MAIN + 2) + place
            part = far_ref[here : here + 8, :]
            if i < 2:
                start = MAIN + SMALL + place
                straight = first_ref[start : start + 8, :]
                straight = jnp.where(odd, straight, second_ref[MAIN + start : MAIN + start + 8, :])
                part = jnp.where(crossed == 7, part, jnp.where(crossed == 15, near_ref[here : here + 8, :], 0.0))
                part = jnp.where(crossed == 3, straight, part)
            parts.append(part)
        halo.append(jnp.concatenate(parts, axis=1))
    cells = (
        [jnp.where(even, halo[j], halo[2 + j]) for j in range(2)]
        + [salt_ref[:, x, :] for x in range(8)]
        + [jnp.where(even, halo[2 + j], halo[j]) for j in range(2)]
    )
    lower, upper = {}, {}
    for x in (-1, 0, 7, 8):
        cell = cells[x + 2]
        half = 0.5 * slope_of(cell - cells[x + 1], cells[x + 3] - cell)
        lower[x], upper[x] = cell + half, cell - half
    for x in range(1, 7):
        lower[x], upper[x] = side_ref[6, x], side_ref[7, x]
    flux_x = []
    for f in range(9):
        if f % 4 == 0:
            face = 0.5 * (speed_x[f // 4] + speed_x[f // 4 + 1])
            if f == 0:
                face = jnp.where(device == 0, 0.0, face)
            if f == 8:
                face = jnp.where(device == 15, 0.0, face)
        else:
            face = speed_x[1 + f // 4]
        flux_x.append(face * jnp.where(face > 0, lower[f - 1], upper[f]))
    faces_z = [jnp.where(layer < 7, 0.5 * (v + pltpu.roll(v, 7, 0)), 0.0) for v in speed_z]
    between = [0.5 * (v + beside) for v, beside in zip(speed_y, beside_y)]
    faces_n = [jnp.where((column & 3) == 3, b, v) for v, b in zip(speed_y, between)]
    faces_n = [jnp.where(column < 255, face, 0.0) for face in faces_n]
    faces_s = [jnp.where((column & 3) == 0, b, v) for v, b in zip(speed_y, between)]
    faces_s = [jnp.where(column > 0, face, 0.0) for face in faces_s]
    for x in range(8):
        face = faces_z[x // 4]
        flux_z = face * jnp.where(face > 0, side_ref[0, x], side_ref[1, x])
        change = flux_z - upper_of(flux_z)
        change = change + (flux_x[x + 1] - flux_x[x])
        face = faces_n[x // 4]
        flux_n = face * jnp.where(face > 0, side_ref[2, x], side_ref[3, x])
        face = faces_s[x // 4]
        flux_s = face * jnp.where(face > 0, side_ref[4, x], side_ref[5, x])
        change = change + (flux_n - flux_s)
        tendency_ref[:, x, :] = -step * (change + dilution_ref[x])

    own = 8 * device + ((lane & 31) >> 2)
    for j in range(4):
        row = jnp.take_along_axis(head[4 * j], own, axis=1)
        for i in range(1, 4):
            row = jnp.where((lane & 3) == i, jnp.take_along_axis(head[4 * j + i], own, axis=1), row)
        head_ref[:, j, :] = row[:, 0:32]

def local_small(salt, recharge, conductivity, codes):
    vmem = pl.BlockSpec(memory_space=pltpu.VMEM)
    block, inner, relay, kept, wet = pl.pallas_call(
        pack_kernel,
        out_shape=(
            pltpu.VMEM((MAIN + SMALL + COLUMNS, 128), jnp.float32),
            pltpu.VMEM((COLUMNS, 128), jnp.float32),
            pltpu.VMEM((8, 128), jnp.float32),
            pltpu.VMEM(salt.shape, jnp.float32),
            pltpu.VMEM(recharge.shape, jnp.int32),
        ),
        in_specs=[vmem] * 4,
        out_specs=(vmem,) * 5,
        scratch_shapes=[pltpu.VMEM((2, 64, 128), jnp.float32), pltpu.VMEM((32, 128), jnp.float32)],
        name="pack",
    )(salt, recharge, conductivity, codes)

    def swapped(array, turn):
        pairs = [(i, i ^ ROUNDS[bin(i).count("1") % 2][turn]) for i in range(lax.axis_size("gx"))]
        return lax.ppermute(array, "gx", pairs)

    def small(array, count):
        return array[count * MAIN : count * MAIN + SMALL]

    def columns(array, count):
        return array[count * MAIN + SMALL :]

    relay = jnp.tile(relay, (COLUMNS // 8, 1))
    first = swapped(block, 0)
    handed = jnp.where(relay > 1.5, columns(block, 1), columns(first, 1))
    block = jnp.concatenate([block[:MAIN], first[:MAIN], small(block, 1) + small(first, 1), handed])
    second = swapped(block, 1)
    handed = jnp.where(relay > 0.5, columns(second, 2), columns(first, 1))
    block = jnp.concatenate(
        [block[: 2 * MAIN], second[: 2 * MAIN], small(block, 2) + small(second, 2), handed]
    )
    other = swapped(block, 2)
    block = jnp.concatenate(
        [block[: 4 * MAIN], other[: 4 * MAIN], small(block, 4), small(other, 4), columns(other, 4), inner]
    )
    other = swapped(block, 3)
    sides, dilution = pl.pallas_call(
        sides_kernel,
        out_shape=(pltpu.VMEM((8, 8, 8, 256), jnp.float32), pltpu.VMEM((8, 8, 256), jnp.float32)),
        in_specs=[vmem] * 2,
        out_specs=(vmem,) * 2,
        cost_estimate=pl.CostEstimate(flops=1 << 20, bytes_accessed=1 << 20, transcendentals=0),
        name="sides",
    )(*(pltpu.with_memory_space_constraint(array, pltpu.VMEM) for array in (kept, wet)))
    return pl.pallas_call(
        step_kernel,
        out_shape=(
            jax.ShapeDtypeStruct(salt.shape, jnp.float32),
            jax.ShapeDtypeStruct(conductivity.shape, jnp.float32),
        ),
        in_specs=[vmem] * 7,
        out_specs=(vmem,) * 2,
        scratch_shapes=[
            pltpu.VMEM((9, 16, 8, 128), jnp.float32),
            pltpu.VMEM((9, 4, 8, 128), jnp.float32),
            pltpu.VMEM((9, 8, 8, 128), jnp.float32),
            pltpu.VMEM((3, 16, 8, 128), jnp.float32),
        ],
        compiler_params=pltpu.CompilerParams(vmem_limit_bytes=16 * 1024 * 1024),
        name="step",
    )(block, other, first, second, sides, dilution, kept)

def local(salt, recharge, conductivity, codes):
    small = (
        lax.axis_size("gx") == 16
        and salt.shape == (8, 8, 256)
        and recharge.shape == (8, 256)
        and conductivity.shape == (8, 4, 32)
        and codes.shape == (4, 32)
    )
    return (local_small if small else local_shared)(salt, recharge, conductivity, codes)

def solution(mesh):
    return jax.shard_map(
        local,
        mesh=mesh,
        in_specs=(
            P("parts", "gx", None),
            P("gx", "parts"),
            P("parts", "gx", None),
            P("gx", "parts"),
        ),
        out_specs=(P("parts", "gx", None), P("parts", "gx", None)),
        check_vma=False,
    )
```

```python
import jax
import jax.numpy as jnp
from jax import lax
from jax.experimental import pallas as pl
from jax.experimental.pallas import tpu as pltpu
from jax.sharding import PartitionSpec as P

CYCLES = 2
SMOOTH = 2
COARSE_SWEEPS = 6

relax_weight = 0.8
vertical_ratio = 0.5
sea_penalty = 2.0
river_penalty = 0.5
river_head = 1.0
recharge_rate = 1.0
courant = 0.45
freshening = 1.0

def padded_2(array, sides, width):
    for axis, dim in sides:
        count, length = (lax.axis_size(axis), array.shape[dim])
        up = [(i, (i + 1) % count) for i in range(count - 1)]
        down = [(j, i) for i, j in up]
        last = lax.slice_in_dim(array, length - width, length, axis=dim)
        first = lax.slice_in_dim(array, 0, width, axis=dim)
        before = lax.ppermute(last, axis, up)
        after = lax.ppermute(first, axis, down)
        array = jnp.concatenate([before, array, after], axis=dim)
    return array

def harmonic(first, second):
    total = first + second
    return 2.0 * first * second / (total + jnp.where(total > 0, 0.0, 1.0))

def coefficients(padded, penalty, vertical_scale):
    inner = padded[:, 1:-1, :]
    y_low = harmonic(inner, padded[:, :-2, :])
    y_high = harmonic(inner, padded[:, 2:, :])
    x_face = harmonic(inner[:, :, :-1], inner[:, :, 1:])
    zero_col = jnp.zeros_like(inner[:, :, :1])
    x_low = jnp.concatenate([zero_col, x_face], axis=2)
    x_high = jnp.concatenate([x_face, zero_col], axis=2)
    z_face = vertical_scale * vertical_ratio * harmonic(inner[:-1], inner[1:])
    zero_layer = jnp.zeros_like(inner[:1])
    z_up = jnp.concatenate([zero_layer, z_face], axis=0)
    z_down = jnp.concatenate([z_face, zero_layer], axis=0)
    top_term = jnp.concatenate([penalty[None], jnp.zeros_like(inner[1:])], axis=0)
    diagonal = x_low + x_high + y_low + y_high + z_up + z_down + top_term
    return (x_low, x_high, y_low, y_high, z_up, z_down, diagonal)

def neighbors(padded):
    center = padded[:, 1:-1, :]
    zero_col = jnp.zeros_like(center[:, :, :1])
    west = jnp.concatenate([zero_col, center[:, :, :-1]], axis=2)
    east = jnp.concatenate([center[:, :, 1:], zero_col], axis=2)
    zero_layer = jnp.zeros_like(center[:1])
    upper = jnp.concatenate([zero_layer, center[:-1]], axis=0)
    lower = jnp.concatenate([center[1:], zero_layer], axis=0)
    return (center, west, east, padded[:, :-2, :], padded[:, 2:, :], upper, lower)

def apply_operator(padded, coeffs):
    center, west, east, south, north, upper, lower = neighbors(padded)
    x_low, x_high, y_low, y_high, z_up, z_down, diagonal = coeffs
    return (
        diagonal * center
        - x_low * west
        - x_high * east
        - y_low * south
        - y_high * north
        - z_up * upper
        - z_down * lower
    )

def relax(padded, coeffs, right_side):
    return (
        padded[:, 1:-1, :]
        + relax_weight * (right_side - apply_operator(padded, coeffs)) / coeffs[6]
    )

def block_mean(field):
    leading = field.shape[:-2]
    count_a, count_b = field.shape[-2:]
    grouped = field.reshape(leading + (count_a // 4, 4, count_b // 4, 4))
    return jnp.sum(grouped, axis=(-3, -1)) * 0.0625

def pair_sum(field):
    leading = field.shape[:-2]
    count_a, count_b = field.shape[-2:]
    grouped = field.reshape(leading + (count_a // 2, 2, count_b // 2, 2))
    return jnp.sum(grouped, axis=(-3, -1))

def upsample(field, factor):
    return jnp.repeat(jnp.repeat(field, factor, axis=-2), factor, axis=-1)

def minmod(first, second):
    return 0.5 * (jnp.sign(first) + jnp.sign(second)) * jnp.minimum(jnp.abs(first), jnp.abs(second))

def portion(field, start, stop, axis):
    return lax.slice_in_dim(field, start, stop, axis=axis)

def divergence(cells, speed, axis):
    length = cells.shape[axis]
    widths = [(0, 0)] * cells.ndim
    widths[axis] = (1, 1)
    padded = jnp.pad(cells, widths)
    steps_diff = portion(padded, 1, length + 2, axis) - portion(padded, 0, length + 1, axis)
    slope = minmod(portion(steps_diff, 0, length, axis), portion(steps_diff, 1, length + 1, axis))
    faces = 0.5 * (portion(speed, 0, length - 1, axis) + portion(speed, 1, length, axis))
    left = portion(cells, 0, length - 1, axis) + 0.5 * portion(slope, 0, length - 1, axis)
    right = portion(cells, 1, length, axis) - 0.5 * portion(slope, 1, length, axis)
    flux = jnp.pad(faces * jnp.where(faces > 0, left, right), widths)
    return portion(flux, 1, length + 1, axis) - portion(flux, 0, length, axis)

def divergence_x(extended, faces):
    steps_diff = extended[:, 1:] - extended[:, :-1]
    slope = minmod(steps_diff[:, :-1], steps_diff[:, 1:])
    cells = extended[:, 1:-1]
    left = cells[:, :-1] + 0.5 * slope[:, :-1]
    right = cells[:, 1:] - 0.5 * slope[:, 1:]
    flux = faces * jnp.where(faces > 0, left, right)
    return flux[:, 1:] - flux[:, :-1]

def velocities(padded, coeffs, above, below):
    center, west, east, south, north, upper, lower = neighbors(padded)
    x_low, x_high, y_low, y_high, z_up, z_down, diagonal = coeffs
    vel_x = 0.5 * (x_low * (west - center) + x_high * (center - east))
    vel_y = 0.5 * (y_low * (south - center) + y_high * (center - north))
    vel_z = 0.5 * (z_up * (upper - center + above) + z_down * (center - lower + below))
    return (vel_z, vel_x, vel_y)

def buoyancy_terms(salt_coarse):
    face_salt = 0.5 * (salt_coarse[:-1] + salt_coarse[1:])
    zero_layer = jnp.zeros_like(salt_coarse[:1])
    above = jnp.concatenate([zero_layer, face_salt], axis=0)
    below = jnp.concatenate([face_salt, zero_layer], axis=0)
    return (above, below)

def boundary_penalty(codes):
    return jnp.where(codes == 1, sea_penalty, 0.0) + jnp.where(codes == 2, river_penalty, 0.0)

def source_terms(coeffs, above, below, recharge_frac, codes):
    top_source = recharge_rate * recharge_frac + river_head * jnp.where(
        codes == 2, river_penalty, 0.0
    )
    surface = jnp.concatenate([top_source[None], jnp.zeros_like(above[1:])], axis=0)
    return coeffs[4] * above - coeffs[5] * below + surface

def local_shared(salt, recharge, conductivity, codes):
    layers = salt.shape[0]
    tile = salt.shape[1]
    wet = recharge.astype(jnp.float32)
    blocks = jnp.concatenate([block_mean(salt), block_mean(wet)[None]], axis=0)
    owned = lax.all_to_all(
        jnp.transpose(blocks, (0, 2, 1)), "gx", split_axis=1, concat_axis=2, tiled=True
    )
    salt_coarse = owned[:layers]
    recharge_frac = owned[layers]
    penalty = boundary_penalty(codes)
    cond_padded = padded_2(conductivity, (("gx", 1),), 1)
    coeffs = coefficients(cond_padded, penalty, 1.0)
    above, below = buoyancy_terms(salt_coarse)
    right_side = source_terms(coeffs, above, below, recharge_frac, codes)
    coarse_cond = 0.25 * pair_sum(conductivity)
    coarse_pen = pair_sum(penalty)
    coarse_padded = padded_2(coarse_cond, (("gx", 1),), 1)
    coarse_coeffs = coefficients(coarse_padded, coarse_pen, 4.0)

    def smooth(current):
        padded = padded_2(current, (("gx", 1),), 1)
        return relax(padded, coeffs, right_side)

    head = jnp.zeros_like(conductivity)
    for cycle_no in range(CYCLES):
        for sweep in range(SMOOTH):
            head = smooth(head)
        head_padded = padded_2(head, (("gx", 1),), 1)
        residual = right_side - apply_operator(head_padded, coeffs)
        coarse_resid = pair_sum(residual)
        correction = jnp.zeros_like(coarse_resid)
        for sweep in range(COARSE_SWEEPS):
            corr_padded = padded_2(correction, (("gx", 1),), 1)
            correction = relax(corr_padded, coarse_coeffs, coarse_resid)
        head = head + upsample(correction, 2)
        for sweep in range(SMOOTH):
            head = smooth(head)
    final_padded = padded_2(head, (("gx", 1),), 1)
    vel_z, vel_x, vel_y = velocities(final_padded, coeffs, above, below)
    local_fastest = jnp.max(jnp.abs(vel_x) + jnp.abs(vel_y) + jnp.abs(vel_z))
    fastest = lax.pmax(local_fastest, "gx")
    step = courant / (fastest + 1e-06)
    packed = jnp.stack([vel_z, vel_x, vel_y])
    returned = jnp.transpose(
        lax.all_to_all(packed, "gx", split_axis=3, concat_axis=2, tiled=True), (0, 1, 3, 2)
    )
    fine_x = upsample(returned[1], 4)
    both = padded_2(jnp.stack([salt, fine_x]), (("gx", 2),), 2)
    extended = both[0]
    inner_x = both[1][:, 1:-1]
    faces = 0.5 * (inner_x[:, :-1] + inner_x[:, 1:])
    position = jnp.arange(tile + 1)
    device = lax.axis_index("gx")
    final_device = lax.axis_size("gx") - 1
    edge = (position == 0) & (device == 0) | (position == tile) & (device == final_device)
    faces = jnp.where(edge[None, :, None], 0.0, faces)
    fine_z = upsample(returned[0], 4)
    fine_y = upsample(returned[2], 4)
    change = (
        divergence(salt, fine_z, 0) + divergence_x(extended, faces) + divergence(salt, fine_y, 2)
    )
    dilution = jnp.concatenate(
        [(freshening * wet * salt[0])[None], jnp.zeros_like(salt[1:])], axis=0
    )
    tendency = -step * change - step * dilution
    return (tendency, head)

def split_dot(values, table, terms=3):
    rows = values.shape[0]
    parts = []
    for _ in range(terms):
        parts.append(values.astype(jnp.bfloat16))
        values = values - parts[-1].astype(jnp.float32)
    out = jnp.dot(jnp.concatenate(parts, axis=0), table, preferred_element_type=jnp.float32)
    return sum(out[rows * i : rows * (i + 1)] for i in range(1, terms)) + out[:rows]

def table_of(shape, same):
    row = lax.broadcasted_iota(jnp.int32, shape, 0)
    col = lax.broadcasted_iota(jnp.int32, shape, 1)
    return jnp.where(same(row, col), 1.0, 0.0).astype(jnp.bfloat16)

def iotas(shape):
    return lax.broadcasted_iota(jnp.int32, shape, 0), lax.broadcasted_iota(jnp.int32, shape, 1)

MAIN, SMALL, COLUMNS = 16, 8, 32
ROUNDS = ((9, 3, 5, 1), (3, 9, 5, 1))

def odd_ones(device):
    return ((device ^ (device >> 1) ^ (device >> 2) ^ (device >> 3)) & 1) == 1

def pack_kernel(salt_ref, recharge_ref, cond_ref, codes_ref, block_ref, inner_ref, relay_ref, kept_ref, wet_ref, flat_ref, turn_ref):
    kept_ref[...] = salt_ref[...]
    wet_ref[...] = recharge_ref[...]
    device = lax.axis_index("gx")
    even = (device & 1) == 0
    for j in range(2):
        first = salt_ref[:, j, :]
        last = salt_ref[:, 6 + j, :]
        inward = jnp.where(even, last, first)
        outward = jnp.where(even, first, last)
        for half in range(2):
            place = 8 * (2 * j + half)
            inner_ref[place : place + 8, :] = inward[:, 128 * half : 128 * half + 128]
            place = place + MAIN + SMALL
            block_ref[place : place + 8, :] = outward[:, 128 * half : 128 * half + 128]
    relay = jnp.where(odd_ones(device), jnp.where((device == 2) | (device == 13), 1.0, 0.0), 2.0)
    relay_ref[...] = jnp.broadcast_to(relay, (8, 128))
    turned = device >> 1
    sums = table_of((256, 128), lambda r, c: (r >> 2) == ((c >> 3) << 2) + (((c - turned) & 7) >> 1))
    for i in range(8):
        four = salt_ref[i] + pltpu.roll(salt_ref[i], 7, 0)
        four = four + pltpu.roll(four, 6, 0)
        flat_ref[0, 8 * i : 8 * i + 8, :] = four[:, 0:128]
        flat_ref[1, 8 * i : 8 * i + 8, :] = four[:, 128:256]
    rows = [
        jnp.concatenate([flat_ref[half, pl.ds(start, 8, stride=8), :] for half in range(2)], axis=1) for start in (0, 4)
    ]
    means = split_dot(jnp.concatenate(rows, axis=0), sums) * 0.0625
    sub, lane = iotas((8, 128))
    mine = (sub >> 2) == ((lane - turned) & 1)
    block_ref[0:8, :] = jnp.where(((lane - turned) & 1) == 0, means[0:8], means[8:16])
    wet_y = jnp.dot(
        recharge_ref[...].astype(jnp.float32).astype(jnp.bfloat16), sums, preferred_element_type=jnp.float32
    )
    wet_row = jnp.sum(jnp.where(mine, wet_y, 0.0), axis=0, keepdims=True) * 0.0625
    for layer in range(8):
        turn_ref[4 * layer : 4 * layer + 4, 0:32] = cond_ref[layer]
    spread = table_of((32, 128), lambda r, c: r == ((c & 7) << 2) + (((c >> 3) - device) & 3))
    turn_ref[...] = split_dot(turn_ref[:, 0:32], spread)
    packed = jnp.zeros((8, 128), jnp.float32)
    for j in range(4):
        packed = jnp.where(((((lane >> 3) - device) & 15) >> 2) == j, turn_ref[pl.ds(j, 8, stride=4), :], packed)
    block_ref[8:16, :] = packed
    codes = codes_ref[...]
    penalty = jnp.where(codes == 1, sea_penalty, 0.0) + jnp.where(codes == 2, river_penalty, 0.0)
    penalty_x = jnp.dot(penalty.astype(jnp.bfloat16), spread, preferred_element_type=jnp.float32)
    row4, lane4 = iotas((4, 128))
    penalty_row = jnp.sum(jnp.where(row4 == ((((lane4 >> 3) - device) & 15) >> 2), penalty_x, 0.0), axis=0, keepdims=True)
    slot = (device & 2) + ((device & 8) >> 1)
    block_ref[16:24, :] = jnp.where(sub == slot, wet_row, jnp.where(sub == slot + 1, penalty_row, 0.0))

def harm(first, second):
    return 2.0 * first * second / (first + second)

def slope_of(back, ahead):
    return jnp.maximum(jnp.minimum(back, ahead), 0.0) + jnp.minimum(jnp.maximum(back, ahead), 0.0)

def east_of(cells, k, side):
    return cells[k + 1] if k % side < side - 1 else pltpu.roll(cells[k + 1 - side], 127, 1)

def west_of(cells, k, side):
    return cells[k - 1] if k % side > 0 else pltpu.roll(cells[k - 1 + side], 1, 1)

def north_of(cells, k, side):
    return cells[k + side] if k < side * (side - 1) else pltpu.roll(cells[k % side], 120, 1)

def south_of(cells, k, side):
    return cells[k - side] if k >= side else pltpu.roll(cells[k + side * (side - 1)], 8, 1)

def upper_of(cell):
    return pltpu.roll(cell, 1, 0)

def lower_of(cell):
    return pltpu.roll(cell, 7, 0)

def sides_kernel(salt_ref, recharge_ref, side_ref, dilution_ref):
    layer, column = iotas((8, 256))
    cells = [salt_ref[:, x, :] for x in range(8)]
    for x in range(8):
        cell = cells[x]
        wet = recharge_ref[x : x + 1, :].astype(jnp.float32)
        dilution_ref[x] = jnp.where(layer == 0, freshening * wet * cell, 0.0)
        ahead = jnp.where(layer < 7, lower_of(cell), 0.0) - cell
        half = 0.5 * slope_of(jnp.where(layer > 0, upper_of(ahead), cell), ahead)
        side_ref[0, x] = cell + half
        side_ref[1, x] = lower_of(cell - half)
        ahead = jnp.where(column < 255, pltpu.roll(cell, 255, 1), 0.0) - cell
        half = 0.5 * slope_of(jnp.where(column > 0, pltpu.roll(ahead, 1, 1), cell), ahead)
        side_ref[2, x] = cell + half
        side_ref[3, x] = pltpu.roll(cell - half, 255, 1)
        side_ref[4, x] = pltpu.roll(cell + half, 1, 1)
        side_ref[5, x] = cell - half
        if 0 < x < 7:
            half = 0.5 * slope_of(cell - cells[x - 1], cells[x + 1] - cell)
            side_ref[6, x] = cell + half
            side_ref[7, x] = cell - half

def step_kernel(
    near_ref, far_ref, first_ref, second_ref, side_ref, dilution_ref, salt_ref, tendency_ref, head_ref, fine_ref, coarse_ref, ring_ref, wide_ref
):
    device = lax.axis_index("gx")
    sub, lane = iotas((8, 128))
    top = sub == 0
    even = (device & 1) == 0
    odd = odd_ones(device)
    orders = [lambda e: ((e >> 3) & 1) + (e & 2) + (e & 4), lambda e: ((e >> 1) & 1) + ((e & 8) >> 2) + (e & 4)]
    here = jnp.where(odd, orders[1](device), orders[0](device))
    there = jnp.where(odd, orders[0](device), orders[1](device))
    flip = (device & 4) != 0
    small = []
    for ref in (near_ref, far_ref):
        halves = [ref[8 * MAIN + SMALL * i : 8 * MAIN + SMALL * (i + 1), :] for i in range(2)]
        small.append([jnp.where(flip, halves[1 - i], halves[i]) for i in range(2)])
    means, conds, smalls = [], [], []
    for e in range(16):
        mine = odd == (bin(e).count("1") % 2 == 1)
        if e % 2 == 0:
            start = pl.multiple_of((here ^ jnp.where(odd, orders[1](e), orders[0](e))) * MAIN, 8)
            near = [near_ref[pl.ds(start, 8), :], near_ref[pl.ds(pl.multiple_of(start + 8, 8), 8), :]]
            start = pl.multiple_of((there ^ jnp.where(odd, orders[0](e), orders[1](e))) * MAIN, 8)
            far = [far_ref[pl.ds(start, 8), :], far_ref[pl.ds(pl.multiple_of(start + 8, 8), 8), :]]
        means.append(jnp.where(mine, near[0], far[0]))
        conds.append(jnp.where(mine, near[1], far[1]))
        smalls.append(jnp.where(mine, small[0][(e >> 2) & 1], small[1][(e >> 2) & 1]))

    slots = [2 * ((e // 2) % 2) + 4 * (e // 8) for e in range(16)]
    wets = [smalls[e][slots[e] : slots[e] + 1] for e in range(16)]
    penalties = [smalls[e][slots[e] + 1 : slots[e] + 2] for e in range(16)]

    def diagonals(fields, index):
        count = len(fields)
        bit = 1
        while bit < count:
            high = (index & bit) != 0
            fields = [jnp.where(high, fields[(m + bit) % count], fields[m]) for m in range(count)]
            bit *= 2
        return fields

    def by_block(fields):
        group = lane[0 : fields[0].shape[0]] >> 3
        picked = diagonals(fields, group)
        return [pltpu.roll(picked[-k % 16], (128 - 8 * k) % 128, 1) for k in range(16)]

    def by_lane(fields):
        within = lane & 7
        out = []
        picked = diagonals(fields, within)
        for s in range(8):
            here = picked[-s % 8]
            if s > 0:
                here = jnp.where(within < 8 - s, pltpu.roll(here, 128 - s, 1), pltpu.roll(here, 8 - s, 1))
            out.append(here)
        return out

    cond = by_block(conds)
    penalties = by_block(penalties)
    salt = [None] * 16
    wet_frac = [None] * 16
    wet_pairs = by_lane([jnp.where(top, wets[2 * b], wets[2 * b + 1]) for b in range(8)])
    for half in range(2):
        columns = by_lane(means[half::2])
        for s in range(8):
            k = 4 * (s // 2) + 2 * half + s % 2
            salt[k] = columns[s]
            wet_frac[k] = wet_pairs[s] if half == 0 else lower_of(wet_pairs[s])

    def coefficients(cells, penalty, side, vertical, weight_ref):
        face_w, face_e, face_s, face_n, face_d = [], [], [], [], []
        for k in range(side * side):
            e = harm(cells[k], east_of(cells, k, side))
            if k % side == side - 1:
                e = jnp.where((lane & 7) < 7, e, 0.0)
            n = harm(cells[k], north_of(cells, k, side))
            if k >= side * (side - 1):
                n = jnp.where(lane < 120, n, 0.0)
            w = face_e[k - 1] if k % side > 0 else None
            if w is None:
                w = jnp.where((lane & 7) > 0, harm(west_of(cells, k, side), cells[k]), 0.0)
            s = face_n[k - side] if k >= side else None
            if s is None:
                s = jnp.where(lane >= 8, harm(south_of(cells, k, side), cells[k]), 0.0)
            face_w.append(w)
            face_e.append(e)
            face_s.append(s)
            face_n.append(n)
            face_d.append(jnp.where(sub < 7, vertical * harm(cells[k], lower_of(cells[k])), 0.0))
        weights = []
        for k in range(side * side):
            six = (face_w[k], face_e[k], face_s[k], face_n[k], upper_of(face_d[k]), face_d[k])
            diag = six[0] + six[1] + six[2] + six[3] + six[4] + six[5] + penalty[k]
            weight = relax_weight / diag
            for number, face in enumerate(six):
                weight_ref[number, k] = weight * face
            weight_ref[6, k] = diag * (1.0 / relax_weight)
            if side == 2:
                weight_ref[7, k] = weight
            weights.append(weight)
        return (face_w, face_e, face_s, face_n, face_d), weights

    def step(here, west, east, south, north, weights, kept=1.0 - relax_weight):
        pairs = (west, east, south, north, upper_of(here), lower_of(here))
        terms = [weights(number) * pair for number, pair in enumerate(pairs)]
        base = kept * here + weights(8)
        return ((terms[0] + terms[1]) + (terms[2] + terms[3])) + ((terms[4] + terms[5]) + base)

    def edges_of(cells):
        return (
            [pltpu.roll(cells[4 * j + 3], 1, 1) for j in range(4)],
            [pltpu.roll(cells[4 * j], 127, 1) for j in range(4)],
            [pltpu.roll(cells[12 + i], 8, 1) for i in range(4)],
            [pltpu.roll(cells[i], 120, 1) for i in range(4)],
        )

    def relaxed(cells, edges, kept=1.0 - relax_weight):
        out = []
        for k in range(16):
            j, i = k // 4, k % 4
            west = cells[k - 1] if i > 0 else edges[0][j]
            east = cells[k + 1] if i < 3 else edges[1][j]
            south = cells[k - 4] if j > 0 else edges[2][i]
            north = cells[k + 4] if j < 3 else edges[3][i]
            out.append(step(cells[k], west, east, south, north, lambda number, k=k: fine_ref[number, k], kept))
        return out

    ring = [(j, i) for j in range(-1, 3) for i in range(-1, 3) if (j in (0, 1)) != (i in (0, 1))]

    def beyond(cells, j, i):
        shift = -(8 * (j // 2) + i // 2) % 128
        cell = cells[2 * (j % 2) + i % 2]
        return pltpu.roll(cell, shift, 1) if shift else cell

    def relaxed_around(cells):
        old, new = {}, {}

        def at(j, i):
            if (j, i) not in old:
                old[j, i] = beyond(cells, j, i)
            return old[j, i]

        for j, i in ring + [(0, 0), (0, 1), (1, 0), (1, 1)]:
            if (j, i) in ring:
                weights = lambda number, q=ring.index((j, i)): ring_ref[number, q]
            else:
                weights = lambda number, k=2 * j + i: coarse_ref[number, k]
            new[j, i] = step(at(j, i), at(j, i - 1), at(j, i + 1), at(j - 1, i), at(j + 1, i), weights)
        return new

    def relaxed_within(new):
        return [
            step(new[j, i], new[j, i - 1], new[j, i + 1], new[j - 1, i], new[j + 1, i],
                 lambda number, k=2 * j + i: coarse_ref[number, k])
            for j in range(2) for i in range(2)
        ]

    def pair_sums(cells):
        return [(cells[k] + cells[k + 1]) + (cells[k + 4] + cells[k + 5]) for k in (0, 2, 8, 10)]

    penalty, river = [], []
    for k in range(16):
        penalty.append(jnp.where(top, penalties[k], 0.0))
        river.append(jnp.where(penalties[k] == river_penalty, river_penalty, 0.0))
    faces, weights = coefficients(cond, penalty, 4, vertical_ratio, fine_ref)
    for k in range(16):
        below = jnp.where(sub < 7, 0.5 * (salt[k] + lower_of(salt[k])), 0.0)
        pull = faces[4][k] * below
        source = jnp.where(top, recharge_rate * wet_frac[k] + river_head * river[k], 0.0)
        fine_ref[8, k] = weights[k] * (upper_of(pull) - pull + source)
        fine_ref[7, k] = below
    coefficients([0.25 * c for c in pair_sums(cond)], pair_sums(penalty), 2, 4.0 * vertical_ratio, coarse_ref)
    for number in range(6):
        cells = [coarse_ref[number, k] for k in range(4)]
        for q, (j, i) in enumerate(ring):
            ring_ref[number, q] = beyond(cells, j, i)

    head = None
    for cycle_no in range(CYCLES):
        for sweep in range(SMOOTH):
            head = [fine_ref[8, k] for k in range(16)] if head is None else relaxed(head, edges_of(head))
        edges = edges_of(head)
        change = relaxed(head, edges, -relax_weight)
        resid = pair_sums([change[k] * fine_ref[6, k] for k in range(16)])
        correction = []
        for k in range(4):
            correction.append(coarse_ref[7, k] * resid[k])
            coarse_ref[8, k] = correction[k]
        for q, (j, i) in enumerate(ring):
            ring_ref[8, q] = beyond(correction, j, i)
        sweeps = COARSE_SWEEPS - 1
        while sweeps > 0:
            around = relaxed_around(correction)
            correction = [around[k // 2, k % 2] for k in range(4)]
            sweeps -= 1
            if sweeps > 0:
                correction = relaxed_within(around)
                around = None
                sweeps -= 1
        if around is None:
            around = {place: beyond(correction, *place) for place in ring}
        head = [head[k] + correction[2 * (k // 8) + (k % 4) // 2] for k in range(16)]
        edges = (
            [edges[0][n] + around[n // 2, -1] for n in range(4)],
            [edges[1][n] + around[n // 2, 2] for n in range(4)],
            [edges[2][n] + around[-1, n // 2] for n in range(4)],
            [edges[3][n] + around[2, n // 2] for n in range(4)],
        )
        for sweep in range(SMOOTH):
            head = relaxed(head, edges_of(head) if edges is None else edges)
            edges = None

    largest = None
    for k in range(16):
        here = head[k]
        west, east = west_of(head, k, 4) - here, here - east_of(head, k, 4)
        south, north = south_of(head, k, 4) - here, here - north_of(head, k, 4)
        scale = 0.5 * fine_ref[6, k]
        vel_x = scale * (fine_ref[0, k] * west + fine_ref[1, k] * east)
        vel_y = scale * (fine_ref[2, k] * south + fine_ref[3, k] * north)
        flow_d = scale * fine_ref[5, k] * (here - lower_of(here) + fine_ref[7, k])
        vel_z = upper_of(flow_d) + flow_d
        wide_ref[0, k] = vel_x
        wide_ref[1, k] = vel_y
        wide_ref[2, k] = vel_z
        speed = jnp.abs(vel_x) + jnp.abs(vel_y) + jnp.abs(vel_z)
        largest = speed if largest is None else jnp.maximum(largest, speed)
    step = courant / (jnp.max(largest, axis=(0, 1), keepdims=True) + 1e-06)

    def along(field, x, beside=False):
        halves = []
        for half in range(2):
            y = 128 * half + lane
            if beside:
                y = jnp.clip(y + jnp.where((lane & 3) == 3, 1, jnp.where((lane & 3) == 0, -1, 0)), 0, 255)
            y = y >> 2
            source = ((y >> 2) << 3) + (x >> 2)
            part = jnp.take_along_axis(wide_ref[field, x & 3], source, axis=1)
            for j in range(1, 4):
                part = jnp.where((y & 3) == j, jnp.take_along_axis(wide_ref[field, 4 * j + (x & 3)], source, axis=1), part)
            halves.append(part)
        return jnp.concatenate(halves, axis=1)

    xs = [jnp.clip(2 * device - 1 + j, 0, 31) for j in range(4)]
    speed_x = [along(0, x) for x in xs]
    speed_z = [along(2, x) for x in xs[1:3]]
    speed_y = [along(1, x) for x in xs[1:3]]
    beside_y = [along(1, x, True) for x in xs[1:3]]

    layer, column = iotas((8, 256))
    crossed = device ^ jnp.where(even, device - 1, device + 1)
    halo = []
    for i in range(4):
        parts = []
        for half in range(2):
            place = 8 * (2 * i + half)
            here = 8 * (MAIN + 2) + place
            part = far_ref[here : here + 8, :]
            if i < 2:
                start = MAIN + SMALL + place
                straight = first_ref[start : start + 8, :]
                straight = jnp.where(odd, straight, second_ref[MAIN + start : MAIN + start + 8, :])
                part = jnp.where(crossed == 7, part, jnp.where(crossed == 15, near_ref[here : here + 8, :], 0.0))
                part = jnp.where(crossed == 3, straight, part)
            parts.append(part)
        halo.append(jnp.concatenate(parts, axis=1))
    cells = (
        [jnp.where(even, halo[j], halo[2 + j]) for j in range(2)]
        + [salt_ref[:, x, :] for x in range(8)]
        + [jnp.where(even, halo[2 + j], halo[j]) for j in range(2)]
    )
    lower, upper = {}, {}
    for x in (-1, 0, 7, 8):
        cell = cells[x + 2]
        half = 0.5 * slope_of(cell - cells[x + 1], cells[x + 3] - cell)
        lower[x], upper[x] = cell + half, cell - half
    for x in range(1, 7):
        lower[x], upper[x] = side_ref[6, x], side_ref[7, x]
    flux_x = []
    for f in range(9):
        if f % 4 == 0:
            face = 0.5 * (speed_x[f // 4] + speed_x[f // 4 + 1])
            if f == 0:
                face = jnp.where(device == 0, 0.0, face)
            if f == 8:
                face = jnp.where(device == 15, 0.0, face)
        else:
            face = speed_x[1 + f // 4]
        flux_x.append(face * jnp.where(face > 0, lower[f - 1], upper[f]))
    faces_z = [jnp.where(layer < 7, 0.5 * (v + pltpu.roll(v, 7, 0)), 0.0) for v in speed_z]
    between = [0.5 * (v + beside) for v, beside in zip(speed_y, beside_y)]
    faces_n = [jnp.where((column & 3) == 3, b, v) for v, b in zip(speed_y, between)]
    faces_n = [jnp.where(column < 255, face, 0.0) for face in faces_n]
    faces_s = [jnp.where((column & 3) == 0, b, v) for v, b in zip(speed_y, between)]
    faces_s = [jnp.where(column > 0, face, 0.0) for face in faces_s]
    for x in range(8):
        face = faces_z[x // 4]
        flux_z = face * jnp.where(face > 0, side_ref[0, x], side_ref[1, x])
        change = flux_z - upper_of(flux_z)
        change = change + (flux_x[x + 1] - flux_x[x])
        face = faces_n[x // 4]
        flux_n = face * jnp.where(face > 0, side_ref[2, x], side_ref[3, x])
        face = faces_s[x // 4]
        flux_s = face * jnp.where(face > 0, side_ref[4, x], side_ref[5, x])
        change = change + (flux_n - flux_s)
        tendency_ref[:, x, :] = -step * (change + dilution_ref[x])

    own = 8 * device + ((lane & 31) >> 2)
    for j in range(4):
        row = jnp.take_along_axis(head[4 * j], own, axis=1)
        for i in range(1, 4):
            row = jnp.where((lane & 3) == i, jnp.take_along_axis(head[4 * j + i], own, axis=1), row)
        head_ref[:, j, :] = row[:, 0:32]

def local_small(salt, recharge, conductivity, codes):
    vmem = pl.BlockSpec(memory_space=pltpu.VMEM)
    block, inner, relay, kept, wet = pl.pallas_call(
        pack_kernel,
        out_shape=(
            pltpu.VMEM((MAIN + SMALL + COLUMNS, 128), jnp.float32),
            pltpu.VMEM((COLUMNS, 128), jnp.float32),
            pltpu.VMEM((8, 128), jnp.float32),
            pltpu.VMEM(salt.shape, jnp.float32),
            pltpu.VMEM(recharge.shape, jnp.int32),
        ),
        in_specs=[vmem] * 4,
        out_specs=(vmem,) * 5,
        scratch_shapes=[pltpu.VMEM((2, 64, 128), jnp.float32), pltpu.VMEM((32, 128), jnp.float32)],
        name="pack",
    )(salt, recharge, conductivity, codes)

    def swapped(array, turn):
        pairs = [(i, i ^ ROUNDS[bin(i).count("1") % 2][turn]) for i in range(lax.axis_size("gx"))]
        return lax.ppermute(array, "gx", pairs)

    def small(array, count):
        return array[count * MAIN : count * MAIN + SMALL]

    def columns(array, count):
        return array[count * MAIN + SMALL :]

    relay = jnp.tile(relay, (COLUMNS // 8, 1))
    first = swapped(block, 0)
    handed = jnp.where(relay > 1.5, columns(block, 1), columns(first, 1))
    block = jnp.concatenate([block[:MAIN], first[:MAIN], small(block, 1) + small(first, 1), handed])
    second = swapped(block, 1)
    handed = jnp.where(relay > 0.5, columns(second, 2), columns(first, 1))
    block = jnp.concatenate(
        [block[: 2 * MAIN], second[: 2 * MAIN], small(block, 2) + small(second, 2), handed]
    )
    other = swapped(block, 2)
    block = jnp.concatenate(
        [block[: 4 * MAIN], other[: 4 * MAIN], small(block, 4), small(other, 4), columns(other, 4), inner]
    )
    other = swapped(block, 3)
    sides, dilution = pl.pallas_call(
        sides_kernel,
        out_shape=(pltpu.VMEM((8, 8, 8, 256), jnp.float32), pltpu.VMEM((8, 8, 256), jnp.float32)),
        in_specs=[vmem] * 2,
        out_specs=(vmem,) * 2,
        cost_estimate=pl.CostEstimate(flops=1 << 20, bytes_accessed=1 << 20, transcendentals=0),
        name="sides",
    )(*(pltpu.with_memory_space_constraint(array, pltpu.VMEM) for array in (kept, wet)))
    return pl.pallas_call(
        step_kernel,
        out_shape=(
            jax.ShapeDtypeStruct(salt.shape, jnp.float32),
            jax.ShapeDtypeStruct(conductivity.shape, jnp.float32),
        ),
        in_specs=[vmem] * 7,
        out_specs=(vmem,) * 2,
        scratch_shapes=[
            pltpu.VMEM((9, 16, 8, 128), jnp.float32),
            pltpu.VMEM((9, 4, 8, 128), jnp.float32),
            pltpu.VMEM((9, 8, 8, 128), jnp.float32),
            pltpu.VMEM((3, 16, 8, 128), jnp.float32),
        ],
        compiler_params=pltpu.CompilerParams(vmem_limit_bytes=16 * 1024 * 1024),
        name="step",
    )(block, other, first, second, sides, dilution, kept)

def local(salt, recharge, conductivity, codes):
    small = (
        lax.axis_size("gx") == 16
        and salt.shape == (8, 8, 256)
        and recharge.shape == (8, 256)
        and conductivity.shape == (8, 4, 32)
        and codes.shape == (4, 32)
    )
    return (local_small if small else local_shared)(salt, recharge, conductivity, codes)

def solution(mesh):
    return jax.shard_map(
        local,
        mesh=mesh,
        in_specs=(
            P("parts", "gx", None),
            P("gx", "parts"),
            P("parts", "gx", None),
            P("gx", "parts"),
        ),
        out_specs=(P("parts", "gx", None), P("parts", "gx", None)),
        check_vma=False,
    )
```
